32 devices in a mesh: ctx: 8 (over y, x, core), fsdp: 4 (over z).
Axes of the slice: x: 2, y: 2, z: 4, core: 2. Of those that a mesh axis runs over, the one named last changes fastest.
Arguments:
- tokens: bfloat16 [6144, 2560], P(('ctx', 'fsdp')), may hold values from -6 to 6
- lengths: int32 [6], replicated, may hold values from 1 to 5952, 6144 in all
- block_place: int32 [16], replicated, may hold values from 0 to 15, as said below
- gain_attn: bfloat16 [2560], P(('ctx', 'fsdp')), may hold values from 0.099609375 to 1.8984375
- w_query: bfloat16 [2560, 2560], P(('ctx', 'fsdp')), may hold values from -0.125 to 0.125
- w_key: bfloat16 [2560, 256], P(('ctx', 'fsdp')), may hold values from -0.125 to 0.125
- w_value: bfloat16 [2560, 256], P(('ctx', 'fsdp')), may hold values from -0.125 to 0.125
- w_out: bfloat16 [2560, 2560], P(None, ('ctx', 'fsdp')), may hold values from -0.5 to 0.5
- gain_ffn: bfloat16 [2560], P(('ctx', 'fsdp')), may hold values from 0.099609375 to 1.8984375
- w_gate: bfloat16 [2560, 7680], P('ctx', 'fsdp'), may hold values from -0.125 to 0.125
- w_up: bfloat16 [2560, 7680], P('ctx', 'fsdp'), may hold values from -0.125 to 0.125
- w_down: bfloat16 [7680, 2560], P('fsdp', 'ctx'), may hold values from -0.0625 to 0.0625
- cotangent: bfloat16 [6144, 2560], P(('ctx', 'fsdp')), may hold values from -6 to 6
Outputs:
- activations: bfloat16 [6144, 2560], P(('ctx', 'fsdp'))
- grad_tokens: float32 [6144, 2560], P(('ctx', 'fsdp'))
- grad_gain_attn: float32 [2560], P(('ctx', 'fsdp'))
- grad_w_query: float32 [2560, 2560], P(('ctx', 'fsdp'))
- grad_w_key: float32 [2560, 256], P(('ctx', 'fsdp'))
- grad_w_value: float32 [2560, 256], P(('ctx', 'fsdp'))
- grad_w_out: float32 [2560, 2560], P(None, ('ctx', 'fsdp'))
- grad_gain_ffn: float32 [2560], P(('ctx', 'fsdp'))
- grad_w_gate: float32 [2560, 7680], P('ctx', 'fsdp')
- grad_w_up: float32 [2560, 7680], P('ctx', 'fsdp')
- grad_w_down: float32 [7680, 2560], P('fsdp', 'ctx')
The draws below stay inside these ranges and needn't reach their ends.
Inputs may be any that keep to these rules, and one draw needn't show every extreme that they name: `block_place`: A permutation: entries 2c and 2c + 1 are q and 15 - q with q = (c + r) mod (8), r drawn afresh. `lengths`: they sum to 6144; the longest is exactly 5952.
All inputs are finite; a program needn't handle non-finite values.
Results may differ from the reference program's by a relative error of at most 0.018.
Values may be sent and summed in bfloat16 or wider, within the bound.
A program may use at most 320 MiB of HBM per device.

```python
import math
import jax
import jax.numpy as jnp
import numpy as np
from jax import lax

D = 2560
H = 10
HD = 256
FF = 7680
WIN = 2048
TOK_DEV = 192
NSEQ = 6
TOKENS = 6144
BLOCKS = 16
LONG = 5952


def draw_block_place(key, part):
    key = jax.random.fold_in(key, 11)
    device_total = BLOCKS // 2
    offset = jax.random.randint(key, (), 0, device_total)
    holders = (jnp.arange(device_total, dtype=jnp.int32) + offset) % device_total
    return jnp.stack([holders, BLOCKS - 1 - holders], 1).reshape(BLOCKS).astype(jnp.int32)


def level_of(rng, extent, pieces, least, top_value):
    factor_of = 1.0
    for dim, parts in pieces:
        steps = jax.random.uniform(jax.random.fold_in(jax.random.fold_in(rng, 6), dim), (parts,), jnp.float32, least / len(pieces), top_value / len(pieces))
        factor_of = factor_of * jnp.repeat(jnp.exp(steps), extent[dim] // parts).reshape((-1,) + (1,) * (len(extent) - 1 - dim))
    return factor_of


def profile(count, total, reach, slope):
    loads = [(1 << 20) // math.isqrt(grade ** slope) + 1 for grade in range(2, count + 1)]
    rest, counts = total - reach - (count - 1), [1] * (count - 1)
    while rest > 0:
        candidates = [i for i in range(count - 1) if counts[i] < reach]
        pool, left = sum([loads[i] for i in candidates]), rest
        for i in candidates:
            more = min(reach - counts[i], max(1, left * loads[i] // pool), rest)
            counts[i] = counts[i] + more
            rest = rest - more
    return np.array([reach] + counts)


def uneven_parts(own_key, amount, total, limit, skew):
    if amount == 2:
        one = jax.random.randint(own_key, (), max(1, total - limit), min(limit, total - 1) + 1)
        return jnp.stack([one, total - one])
    sizes = jnp.asarray(profile(amount, total, limit, skew), jnp.int32)
    pairs = (amount - 1) // 2
    donor, taker = sizes[1:1 + 2 * pairs:2], sizes[2:2 + 2 * pairs:2]
    room = jnp.minimum(donor - 1, limit - taker)
    moved = jax.random.randint(jax.random.fold_in(own_key, 1), (pairs,), 0, 1 << 20) % (room + 1)
    sizes = sizes.at[1:1 + 2 * pairs:2].set(donor - moved).at[2:2 + 2 * pairs:2].set(taker + moved)
    return sizes[jax.random.permutation(jax.random.fold_in(own_key, 2), amount)]


def centred(rng, dims, deviation, reach, cuts=(), kind=jnp.bfloat16):
    drawn = jax.random.normal(rng, dims, jnp.float32) * deviation
    if len(cuts) > 0:
        drawn = level_of(rng, dims, cuts, -0.22, 0.18) * drawn
    return jnp.clip(drawn, min=-reach, max=reach).astype(kind)


def setup_inputs(seed: int = 0) -> dict:
    key_of = jax.random.split(jax.random.key(seed), 14)
    tokens = centred(key_of[0], (TOKENS, D), 1.0, 6.0, ((0, 32),))
    lengths = uneven_parts(key_of[1], NSEQ, TOKENS, LONG, 2).astype(jnp.int32)
    block_place = draw_block_place(jax.random.fold_in(key_of[13], 71), 0)
    gain_attn = jnp.clip(1.0 + 0.18 * jax.random.normal(key_of[3], (D,), jnp.float32), 0.099609375, 1.8984375).astype(jnp.bfloat16)
    w_query = centred(key_of[4], (D, H * HD), D ** -0.5, 0.125, ((0, 32),))
    w_key = centred(key_of[5], (D, HD), D ** -0.5, 0.125, ((0, 32),))
    w_value = centred(key_of[6], (D, HD), D ** -0.5, 0.125, ((0, 32),))
    w_out = centred(key_of[7], (H * HD, D), (H * HD // 16) ** -0.5, 0.5, ((1, 32),))
    gain_ffn = jnp.clip(1.0 + 0.18 * jax.random.normal(key_of[8], (D,), jnp.float32), 0.099609375, 1.8984375).astype(jnp.bfloat16)
    w_gate = centred(key_of[9], (D, FF), D ** -0.5, 0.125, ((0, 8), (1, 4)))
    w_up = centred(key_of[10], (D, FF), D ** -0.5, 0.125, ((0, 8), (1, 4)))
    w_down = centred(key_of[11], (FF, D), FF ** -0.5, 0.0625, ((0, 4), (1, 8)))
    cotangent = centred(key_of[12], (TOKENS, D), 1.0, 6.0, ((0, 32),))
    return {"tokens": tokens, "lengths": lengths, "block_place": block_place, "gain_attn": gain_attn, "w_query": w_query, "w_key": w_key, "w_value": w_value, "w_out": w_out, "gain_ffn": gain_ffn, "w_gate": w_gate, "w_up": w_up, "w_down": w_down, "cotangent": cotangent}


@jax.custom_vjp
def low(v):
    return lax.optimization_barrier(v.astype(jnp.bfloat16)).astype(jnp.float32)

@jax.custom_vjp
def low_back(v):
    return v

def low_keep(v):
    return (low(v), None)

def low_pass(kept, grad):
    return (grad,)

def back_keep(v):
    return (v, None)

def back_low(kept, grad):
    return (low(grad),)
low.defvjp(low_keep, low_pass)
low_back.defvjp(back_keep, back_low)
epsilon = 1e-06
highest = lax.Precision.HIGHEST

def matmul(first_op, second_op):
    return jnp.dot(first_op, second_op, precision=highest, preferred_element_type=jnp.float32)

def norm_rows(values, scales):
    return values * lax.rsqrt(lax.optimization_barrier(jnp.mean(values * values, -1, keepdims=True)) + epsilon) * scales

def rotate(values, places):
    half_dim = values.shape[-1] // 2
    frequency = jnp.exp(jnp.arange(half_dim, dtype=jnp.float32) * (-jnp.log(10000.0) / half_dim))
    angles = places.astype(jnp.float32)[:, None, None] * frequency
    cosine = jnp.cos(angles)
    sine_part = jnp.sin(angles)
    front_half = values[..., :half_dim]
    back_half = values[..., half_dim:]
    return jnp.concatenate([front_half * cosine - back_half * sine_part, back_half * cosine + front_half * sine_part], -1)

def doc_info(places, lengths):
    doc_ends = jnp.cumsum(lengths)
    passed = places[:, None] >= doc_ends[None, :]
    doc_ids = lax.optimization_barrier(jnp.sum(passed.astype(jnp.int32), 1))
    offsets = lax.optimization_barrier(jnp.sum(jnp.where(passed, lengths[None, :], 0), 1))
    return (doc_ids, places - offsets)

def inverse_order(block_place):
    block_total = block_place.shape[0]
    numbers = jnp.arange(block_total, dtype=jnp.int32)
    return lax.optimization_barrier(jnp.sum(jnp.where(block_place[None, :] == numbers[:, None], numbers[None, :], 0), 1))

def reference(tokens, lengths, block_place, gain_attn, w_query, w_key, w_value, w_out, gain_ffn, w_gate, w_up, w_down, cotangent):
    half_rows = 2 * TOK_DEV
    stream_order = inverse_order(block_place)

    def to_stream(array):
        return array.reshape(BLOCKS, half_rows, -1)[stream_order].reshape(TOKENS, -1)

    def to_stored(array):
        return array.reshape(BLOCKS, half_rows, -1)[block_place].reshape(TOKENS, -1)
    positions = jnp.arange(TOKENS, dtype=jnp.int32)
    doc_ids, rel_pos = doc_info(positions, lengths)
    pad_docs = jnp.concatenate([jnp.full((WIN,), -1, jnp.int32), doc_ids])
    q_scale = HD ** (-0.5)

    def forward(in_rows, attn_scale, query_w, key_w, value_w, out_w, ffn_scale, gate_w, up_w, down_w):
        normed = low(norm_rows(in_rows, attn_scale))
        query_proj = low_back(matmul(normed, query_w)).reshape(TOKENS, H, HD)
        queries = low(rotate(query_proj, rel_pos) * q_scale)
        key_proj = low_back(matmul(normed, key_w))
        keys = low(rotate(key_proj[:, None, :], rel_pos)[:, 0])
        values_all = low(low_back(matmul(normed, value_w)))
        key_pad = jnp.concatenate([jnp.zeros((WIN, HD), jnp.float32), keys])
        value_pad = jnp.concatenate([jnp.zeros((WIN, HD), jnp.float32), values_all])

        def attend(block_index):
            row_start = block_index * half_rows
            query_block = lax.dynamic_slice_in_dim(queries, row_start, half_rows, 0)
            key_block = lax.dynamic_slice_in_dim(key_pad, row_start, WIN + half_rows, 0)
            value_block = lax.dynamic_slice_in_dim(value_pad, row_start, WIN + half_rows, 0)
            query_docs = lax.dynamic_slice_in_dim(doc_ids, row_start, half_rows, 0)
            key_docs = lax.dynamic_slice_in_dim(pad_docs, row_start, WIN + half_rows, 0)
            query_at = row_start + jnp.arange(half_rows, dtype=jnp.int32)
            key_at = row_start - WIN + jnp.arange(WIN + half_rows, dtype=jnp.int32)
            visible = (query_docs[:, None] == key_docs[None, :]) & (key_at[None, :] <= query_at[:, None]) & (key_at[None, :] > query_at[:, None] - WIN)
            scores = low_back(jnp.einsum('qhd,kd->hqk', query_block, key_block, precision=highest))
            scores = jnp.where(visible[None], scores, -1e+30)
            row_peak = lax.optimization_barrier(jnp.max(scores, -1, keepdims=True))
            weights = jnp.exp(scores - row_peak)
            probability = weights / lax.optimization_barrier(jnp.sum(weights, -1, keepdims=True))
            return jnp.einsum('hqk,kd->qhd', low(probability), value_block, precision=highest)
        mixed = lax.map(jax.checkpoint(attend), jnp.arange(BLOCKS, dtype=jnp.int32))
        attended = low(low_back(mixed.reshape(TOKENS, H * HD)))
        branch = low_back(matmul(attended, out_w))
        middle = in_rows + branch
        normed_two = low(norm_rows(middle, ffn_scale))
        gate_val = low_back(matmul(normed_two, gate_w))
        up_val = low_back(matmul(normed_two, up_w))
        hidden = low(jax.nn.gelu(gate_val, approximate=True) * up_val)
        return middle + low_back(matmul(hidden, down_w))
    stream_in = to_stream(tokens.astype(jnp.float32))
    output, pullback = jax.vjp(forward, stream_in, gain_attn.astype(jnp.float32), w_query.astype(jnp.float32), w_key.astype(jnp.float32), w_value.astype(jnp.float32), w_out.astype(jnp.float32), gain_ffn.astype(jnp.float32), w_gate.astype(jnp.float32), w_up.astype(jnp.float32), w_down.astype(jnp.float32))
    grads = pullback(to_stream(cotangent.astype(jnp.float32)))
    return (to_stored(output).astype(jnp.bfloat16), to_stored(grads[0]), grads[1], grads[2], grads[3], grads[4], grads[5], grads[6], grads[7], grads[8], grads[9])
```

```python
import functools

import jax
import jax.numpy as jnp
from jax import lax
from jax.experimental import pallas as pl
from jax.experimental.pallas import tpu as pltpu
from jax.sharding import PartitionSpec as P

H = 10
HD = 256
WIN = 2048
EPS = 1e-06
F32 = jnp.float32
BF16 = jnp.bfloat16
MESH = pl.DeviceIdType.MESH
ANY = pl.BlockSpec(memory_space=pl.ANY)
VMEM = pl.BlockSpec(memory_space=pltpu.VMEM)
HEADS = H // 2
QW = HEADS * HD
VMEM_LIMIT = 56 * 1024 * 1024
FAR = -1e30


def swap(x, axis, mask):
    return lax.ppermute(x, axis, [(i, i ^ mask) for i in range(lax.axis_size(axis))])


def join(own, other, bit, axis):
    return jnp.where(
        bit == 0,
        jnp.concatenate([own, other], axis),
        jnp.concatenate([other, own], axis),
    )


def half(x, which, axis=0):
    size = x.shape[axis] // 2
    return lax.dynamic_slice_in_dim(x, which * size, size, axis)


def dot(a, b):
    return jnp.dot(a, b, preferred_element_type=F32)


def dot_t(a, b):
    return lax.dot_general(a, b, (((1,), (1,)), ((), ())), preferred_element_type=F32)


def t_dot(a, b):
    return lax.dot_general(a, b, (((0,), (0,)), ((), ())), preferred_element_type=F32)


def inv_rms(x):
    return lax.rsqrt(jnp.mean(x * x, -1, keepdims=True) + EPS)


def norm_back(x, scale, grad):
    r = inv_rms(x)
    scaled = grad * scale
    lean = jnp.mean(scaled * x, -1, keepdims=True)
    return r * scaled - x * (r * r * r * lean), jnp.sum(grad * x * r, 0)


def takes(us):
    return pl.CostEstimate(flops=int(us * 1e9), bytes_accessed=0, transcendentals=0)


class Net:
    def __init__(self, send_sems, recv_sems):
        self.send_sems, self.recv_sems, self.used = send_sems, recv_sems, 0

    def push(self, src, dst, to):
        copy = pltpu.make_async_remote_copy(
            src_ref=src,
            dst_ref=dst,
            send_sem=self.send_sems.at[self.used],
            recv_sem=self.recv_sems.at[self.used],
            device_id=to,
            device_id_type=MESH,
        )
        self.used += 1
        return copy


def greet(partners):
    barrier = pltpu.get_barrier_semaphore()
    for to in partners:
        pl.semaphore_signal(barrier, inc=1, device_id=to, device_id_type=MESH)
    pl.semaphore_wait(barrier, len(partners))


def flip(x, mask):
    for bit in (1, 2, 4):
        if mask & bit:
            x = x + bit - 2 * bit * ((x // bit) % 2)
    return x


def where_am_i():
    return lax.axis_index("ctx"), lax.axis_index("fsdp")


def gather_kernel(
    qkv, out, gain, tokens, cot, w_qkv, w_out, gains, rows, cot_one, cot_three, send_sems, recv_sems, own_sems
):
    ctx, z = where_am_i()
    net = Net(send_sems, recv_sems)
    greet([(ctx, flip(z, m)) for m in (1, 2, 3)] + [(flip(ctx, m), z) for m in (1, 2, 4)])
    shard = qkv.shape[0]
    qkv_cols, half_cols = QW + HD, QW // 2

    def cols_of(ref, stride, first, count):
        return lambda h: ref.at[:, pl.ds(pl.multiple_of(h * stride + first, 128), count)]

    groups = [
        (cols_of(qkv, qkv_cols, QW, HD), w_qkv, shard, QW, HD),
        (lambda h: gain, gains, 8, 0, 128),
        (cols_of(qkv, qkv_cols, 0, half_cols), w_qkv, shard, 0, half_cols),
        (cols_of(qkv, qkv_cols, half_cols, half_cols), w_qkv, shard, half_cols, half_cols),
        (cols_of(out, QW, 0, half_cols), w_out, shard, 0, half_cols),
        (cols_of(out, QW, half_cols, half_cols), w_out, shard, half_cols, half_cols),
    ]

    def at(group, source, first, count):
        src, ref, unit, col, cols = group
        start = pl.multiple_of(source * 4 * unit + first, 8 if unit == 8 else 16)
        return ref.at[pl.ds(start, count), pl.ds(col, cols)]

    lines, locals_, sent = [], [], []

    def push(src, dst, to):
        copy = net.push(src, dst, to)
        copy.start()
        sent.append(copy)
        return copy

    token_rows = tokens.shape[0]
    token_dst = rows.at[pl.ds(pl.multiple_of((z % 2) * token_rows, 16), token_rows)]
    for i, group in enumerate(groups):
        unit = group[2]
        dst = at(group, ctx, z * unit, unit)
        lines.append([push(group[0](flip(z, m) % 2), dst, (ctx, flip(z, m))) for m in (2, 3, 1)])
        local = pltpu.make_async_copy(group[0](z % 2), dst, own_sems.at[i])
        local.start()
        locals_.append(local)
        if i == 3:
            token_copy = push(tokens, token_dst, (ctx, flip(z, 1)))
            token_local = pltpu.make_async_copy(tokens, token_dst, own_sems.at[len(groups)])
            token_local.start()
    mate, beyond = (ctx, flip(z, 1)), (ctx, flip(z, 3))
    inner = (z == 1) | (z == 2)
    cot_mate = push(cot, cot_one, mate)
    cot_beyond = net.push(cot, cot_three, beyond)

    @pl.when(inner)
    def _():
        cot_beyond.start()

    by_x, by_y, last = {}, {}, []
    diag = {}
    x_dev, y_dev, sib = (flip(ctx, 2), z), (flip(ctx, 4), z), (flip(ctx, 1), z)

    def same(group, source, first, count, to):
        return push(at(group, source, first, count), at(group, source, first, count), to)

    def spread_own(i):
        group = groups[i]
        locals_[i].wait()
        for copy in lines[i]:
            copy.wait_recv()
        count = 4 * group[2]
        by_x[i] = same(group, ctx, 0, count, x_dev)
        by_y[i] = same(group, ctx, 0, count, y_dev)
        last.append(same(group, ctx, 0, count, sib))

    def spread_near(i):
        group = groups[i]
        count = 4 * group[2]
        by_x[i].wait_recv()
        top = same(group, flip(ctx, 2), 0, count // 2, y_dev)
        last.append(same(group, flip(ctx, 2), 0, count, sib))
        by_y[i].wait_recv()
        low = same(group, flip(ctx, 4), count // 2, count // 2, x_dev)
        last.append(same(group, flip(ctx, 4), 0, count, sib))
        diag[i] = (top, low)

    def spread_far(i):
        group = groups[i]
        count = 4 * group[2]
        for k in range(2):
            diag[i][k].wait_recv()
            last.append(same(group, flip(ctx, 6), k * count // 2, count // 2, sib))

    for i in range(len(groups) + 2):
        if i < len(groups):
            spread_own(i)
        if 0 <= i - 1 < len(groups):
            spread_near(i - 1)
        if 0 <= i - 2 < len(groups):
            spread_far(i - 2)
    token_local.wait()
    token_copy.wait_recv()
    cot_mate.wait_recv()

    @pl.when(inner)
    def _():
        cot_beyond.wait_recv()
        cot_beyond.wait_send()

    for copy in last:
        copy.wait_recv()
    for copy in sent:
        copy.wait_send()


def gather_weights(w_query, w_key, w_value, w_out, gain_attn, gain_ffn, tokens, cotangent):
    shard, width = w_query.shape
    z = lax.axis_index("fsdp")
    ctx_total = lax.axis_size("ctx")
    pieces = []
    for h in range(2):
        pieces += [w_query[:, h * QW : (h + 1) * QW], (w_key, w_value)[h]]
    qkv = jnp.concatenate(pieces, 1)
    out = w_out.T
    gain = jnp.stack([gain_attn, gain_ffn]).astype(F32)
    if ctx_total != 8 or lax.axis_size("fsdp") != 4 or shard % 16:
        both = ("ctx", "fsdp")
        full = lax.all_gather(qkv, both, axis=0, tiled=True)
        full_out = lax.all_gather(out, both, axis=0, tiled=True)
        return (
            half(full, z % 2, 1),
            half(full_out, z % 2, 1),
            lax.all_gather(gain, both, axis=1, tiled=True),
            join(tokens, swap(tokens, "fsdp", 1), z % 2, 0),
            swap(cotangent, "fsdp", 1),
            swap(cotangent, "fsdp", 3),
        )
    gain = jnp.pad(gain, ((0, 6), (0, 128 - shard)))
    devices = 4 * ctx_total
    w_qkv, w_o, gains, rows, cot_one, cot_three = pl.pallas_call(
        gather_kernel,
        out_shape=[
            jax.ShapeDtypeStruct((width, QW + HD), BF16),
            jax.ShapeDtypeStruct((width, QW), BF16),
            jax.ShapeDtypeStruct((8 * devices, 128), F32),
            jax.ShapeDtypeStruct((2 * tokens.shape[0], width), BF16),
            jax.ShapeDtypeStruct(tokens.shape, BF16),
            jax.ShapeDtypeStruct(tokens.shape, BF16),
        ],
        in_specs=[ANY] * 5,
        out_specs=[ANY] * 6,
        scratch_shapes=[
            pltpu.SemaphoreType.DMA((75,)),
            pltpu.SemaphoreType.DMA((75,)),
            pltpu.SemaphoreType.DMA((7,)),
        ],
        compiler_params=pltpu.CompilerParams(collective_id=0, has_side_effects=True),
        cost_estimate=takes(80),
        name="gather_weights",
    )(qkv, out, gain, tokens, cotangent)
    gains = gains.reshape(devices, 8, 128)[:, :2, :shard].transpose(1, 0, 2).reshape(2, width)
    return w_qkv, w_o, gains, rows, cot_one, cot_three


def proj_kernel(rows, scale, cosine, sine, w, normed, out, kv):
    @pl.when(pl.program_id(0) == 0)
    def _():
        x = rows[...].astype(F32)
        normed[...] = (x * inv_rms(x) * scale[...]).astype(BF16)

    value = dot(normed[...], w[...])
    front, back = value[:, : HD // 2], value[:, HD // 2 :]
    c, s = cosine[0], sine[0]

    def put(ref):
        ref[:, : HD // 2] = (front * c - back * s).astype(BF16)
        ref[:, HD // 2 :] = (back * c + front * s).astype(BF16)

    pl.when(pl.program_id(0) < HEADS)(lambda: put(out))
    pl.when(pl.program_id(0) == HEADS)(lambda: put(kv))


def project(rows, scale, cosine, sine, w):
    count, width = rows.shape
    steps = HEADS + 1
    fixed = lambda i: (0, 0)
    table = pl.BlockSpec((1, count, HD // 2), lambda i: (i // HEADS, 0, 0))
    return pl.pallas_call(
        proj_kernel,
        grid=(steps,),
        out_shape=[
            jax.ShapeDtypeStruct((count, width), BF16),
            jax.ShapeDtypeStruct((count, QW), BF16),
            jax.ShapeDtypeStruct((count, HD), BF16),
        ],
        in_specs=[
            pl.BlockSpec((count, width), fixed),
            pl.BlockSpec((1, width), fixed),
            table,
            table,
            pl.BlockSpec((width, HD), lambda i: (0, i)),
        ],
        out_specs=[
            pl.BlockSpec((count, width), fixed),
            pl.BlockSpec((count, HD), lambda i: (0, jnp.minimum(i, HEADS - 1))),
            pl.BlockSpec((count, HD), fixed),
        ],
        compiler_params=pltpu.CompilerParams(vmem_limit_bytes=VMEM_LIMIT),
        cost_estimate=takes(10),
        name="project",
    )(rows, scale, cosine, sine, w)


def kv_gather_kernel(kv, cot_one, cot_three, store, cot_two, send_sems, recv_sems, own_sem):
    ctx, z = where_am_i()
    net = Net(send_sems, recv_sems)
    h, pair = z % 2, z // 2
    greet([(ctx, flip(z, m)) for m in (1, 2, 3)] + [(flip(ctx, m), z) for m in (1, 2, 4)])
    local = pltpu.make_async_copy(kv, store.at[pair, ctx, h], own_sem)
    local.start()
    mate, across = (ctx, flip(z, 1)), (ctx, flip(z, 2))
    x_dev, y_dev, sib = (flip(ctx, 2), z), (flip(ctx, 4), z), (flip(ctx, 1), z)
    own = net.push(kv, store.at[pair, ctx, h], mate)
    own.start()
    low = net.push(kv, store.at[0, ctx, h], across)
    low_mate = net.push(store.at[0, ctx, h], store.at[0, ctx, h], mate)

    @pl.when(pair == 0)
    def _():
        low.start()

    one_beyond = net.push(cot_one, cot_two, (ctx, flip(z, 3)))
    three_mate = net.push(cot_three, cot_two, mate)
    inner = (z == 1) | (z == 2)

    @pl.when(inner)
    def _():
        one_beyond.start()
        three_mate.start()

    local.wait()
    own.wait_recv()

    class Set:
        def __init__(self, which):
            def same(source, kind, to):
                if kind is None:
                    ref = store.at[which, source]
                else:
                    ref = store.at[which, source, kind]
                return net.push(ref, ref, to)

            self.near = [same(ctx, None, x_dev), same(ctx, None, y_dev), same(ctx, None, sib)]
            x_ctx, y_ctx, d_ctx = flip(ctx, 2), flip(ctx, 4), flip(ctx, 6)
            self.after_x = [same(x_ctx, 0, y_dev), same(x_ctx, None, sib)]
            self.after_y = [same(y_ctx, 1, x_dev), same(y_ctx, None, sib)]
            self.after_d = [same(d_ctx, 0, sib), same(d_ctx, 1, sib)]

        def first(self):
            for copy in self.near:
                copy.start()

        def second(self):
            self.near[0].wait_recv()
            for copy in self.after_x:
                copy.start()
            self.near[1].wait_recv()
            for copy in self.after_y:
                copy.start()

        def third(self):
            self.after_x[0].wait_recv()
            self.after_d[0].start()
            self.after_y[0].wait_recv()
            self.after_d[1].start()

        def finish(self):
            for copy in [self.near[2], self.after_x[1], self.after_y[1]] + self.after_d:
                copy.wait_recv()
            for copy in self.near + self.after_x + self.after_y + self.after_d:
                copy.wait_send()

    mine = Set(pair)
    lower = Set(0)
    mine.first()

    @pl.when(pair == 1)
    def _():
        low.wait_recv()
        low_mate.start()
        low_mate.wait_recv()
        lower.first()

    mine.second()

    @pl.when(pair == 1)
    def _():
        lower.second()

    mine.third()

    @pl.when(pair == 1)
    def _():
        lower.third()

    mine.finish()
    own.wait_send()

    @pl.when(pair == 1)
    def _():
        lower.finish()
        low_mate.wait_send()

    @pl.when(pair == 0)
    def _():
        low.wait_send()

    @pl.when(inner)
    def _():
        one_beyond.wait_recv()
        one_beyond.wait_send()
        three_mate.wait_send()

    @pl.when(jnp.logical_not(inner))
    def _():
        three_mate.wait_recv()


def gather_kv(kv, cot_one, cot_three, cotangent):
    ctx_total = lax.axis_size("ctx")
    rows = kv.shape[0]
    if ctx_total != 8 or lax.axis_size("fsdp") != 4:
        every = lax.all_gather(kv, ("fsdp", "ctx"), axis=0, tiled=False)
        every = every.reshape(2, 2, ctx_total, rows, HD).transpose(0, 2, 1, 3, 4)
        return every.reshape(2 * ctx_total, 2, rows, HD), swap(cotangent, "fsdp", 2)
    store, cot_two = pl.pallas_call(
        kv_gather_kernel,
        out_shape=[
            jax.ShapeDtypeStruct((2, ctx_total, 2, rows, HD), BF16),
            jax.ShapeDtypeStruct(cot_one.shape, BF16),
        ],
        in_specs=[ANY] * 3,
        out_specs=[ANY] * 2,
        scratch_shapes=[
            pltpu.SemaphoreType.DMA((23,)),
            pltpu.SemaphoreType.DMA((23,)),
            pltpu.SemaphoreType.DMA,
        ],
        compiler_params=pltpu.CompilerParams(collective_id=1, has_side_effects=True),
        cost_estimate=takes(30),
        name="gather_kv",
    )(kv, cot_one, cot_three)
    return store.reshape(2 * ctx_total, 2, rows, HD), cot_two


def chunks(rows, reach):
    skip = (reach * rows - WIN) // 128 * 128
    parts, at = [], 0
    for r in range(reach + 1):
        begin = max(0, skip - r * rows)
        if begin < rows:
            parts.append((r, begin, at, rows - begin))
            at += rows - begin
    return parts, at


def attend_kernel(reach, place, lowest, q, *refs):
    keys, values = refs[: reach + 1], refs[reach + 1 : 2 * reach + 2]
    prob, out, scores = refs[2 * reach + 2 :]
    rows = q.shape[0]
    parts, total = chunks(rows, reach)
    low = lowest[:, :1]
    peak = None
    for r, begin, at, count in parts:
        s = dot_t(q[...], keys[r][0, 0, begin:, :])
        key_at = lax.broadcasted_iota(jnp.int32, (rows, count), 1) + (r * rows + begin)
        visible = key_at >= low
        if r == reach:
            query_at = lax.broadcasted_iota(jnp.int32, (rows, count), 0) + reach * rows
            visible = visible & (key_at <= query_at)
        s = jnp.where(visible, s, FAR)
        scores[:, at : at + count] = s
        top = jnp.max(s, -1, keepdims=True)
        peak = top if peak is None else jnp.maximum(peak, top)
    weight_sum = jnp.zeros_like(peak)
    for r, begin, at, count in parts:
        e = jnp.exp(scores[:, at : at + count] - peak)
        scores[:, at : at + count] = e
        weight_sum = weight_sum + jnp.sum(e, -1, keepdims=True)
    share = 1.0 / weight_sum
    mixed = jnp.zeros((rows, HD), F32)
    for r, begin, at, count in parts:
        p = (scores[:, at : at + count] * share).astype(BF16)
        prob[0, :, at : at + count] = p
        mixed = mixed + dot(p, values[r][0, 0, begin:, :])
    out[...] = mixed.astype(BF16)


def window_specs(rows, reach):
    def spec(r, kind):
        return pl.BlockSpec((1, 1, rows, HD), lambda i, place: (place[r], kind, 0, 0))

    return [spec(r, kind) for kind in range(2) for r in range(reach + 1)]


def attend(place, lowest, qkv, store, reach):
    rows = qkv.shape[0]
    total = chunks(rows, reach)[1]
    column = pl.BlockSpec((rows, HD), lambda i, place: (0, i))
    return pl.pallas_call(
        functools.partial(attend_kernel, reach),
        grid_spec=pltpu.PrefetchScalarGridSpec(
            num_scalar_prefetch=1,
            grid=(HEADS,),
            in_specs=[pl.BlockSpec((rows, 128), lambda i, place: (0, 0)), column]
            + window_specs(rows, reach),
            out_specs=[
                pl.BlockSpec((1, rows, total), lambda i, place: (i, 0, 0)),
                column,
            ],
            scratch_shapes=[pltpu.VMEM((rows, total), F32)],
        ),
        out_shape=[
            jax.ShapeDtypeStruct((HEADS, rows, total), BF16),
            jax.ShapeDtypeStruct((rows, QW), BF16),
        ],
        compiler_params=pltpu.CompilerParams(vmem_limit_bytes=VMEM_LIMIT),
        cost_estimate=takes(21),
        name="attend",
    )(place, lowest, qkv, *([store] * (2 * reach + 2)))


def attend_back_kernel(reach, place, goes, prob, q, branch, w_out, cosine, sine, *refs):
    keys, values = refs[: reach + 1], refs[reach + 1 : 2 * reach + 2]
    grad_q, store, grad_probs, sums, blocks, sems = refs[2 * reach + 2 :]
    rows = q.shape[0]
    parts, total = chunks(rows, reach)
    head = pl.program_id(0)

    @pl.when(head == 0)
    def _():
        sums[...] = jnp.zeros_like(sums)

    grad_rows = dot(branch[...], w_out[...]).astype(BF16)
    query_rows = q[...]
    lean = jnp.zeros((rows, 1), F32)
    for r, begin, at, count in parts:
        dp = dot_t(grad_rows, values[r][0, 0, begin:, :])
        p = prob[0, :, at : at + count]
        grad_probs[:, at : at + count] = dp
        lean = lean + jnp.sum(dp * p.astype(F32), -1, keepdims=True)
        sums[1, at : at + count, :] += t_dot(p, grad_rows)
    turned = jnp.zeros((rows, HD), F32)
    for r, begin, at, count in parts:
        p = prob[0, :, at : at + count].astype(F32)
        ds = (p * (grad_probs[:, at : at + count] - lean)).astype(BF16)
        turned = turned + dot(ds, keys[r][0, 0, begin:, :])
        sums[0, at : at + count, :] += t_dot(ds, query_rows)
    front, back = turned[:, : HD // 2], turned[:, HD // 2 :]
    c, s = cosine[0], sine[0]
    grad_q[:, : HD // 2] = (front * c + back * s).astype(BF16)
    grad_q[:, HD // 2 :] = (back * c - front * s).astype(BF16)

    @pl.when(head == pl.num_programs(0) - 1)
    def _():
        blocks[reach + 1] = jnp.zeros((2, rows, HD), BF16)
        for r, begin, at, count in parts:
            for kind in range(2):
                if begin > 0:
                    blocks[r, kind, :begin, :] = jnp.zeros((begin, HD), BF16)
                blocks[r, kind, begin:, :] = sums[kind, at : at + count, :].astype(BF16)
        for r in range(parts[0][0]):
            blocks[r] = jnp.zeros((2, rows, HD), BF16)
        count = store.shape[0]

        def copy(i):
            return pltpu.make_async_copy(blocks.at[goes[i]], store.at[i], sems.at[i])

        for i in range(count):
            copy(i).start()
        for i in range(count):
            copy(i).wait()


def attend_back(place, goes, prob, qkv, branch, w_out, cosine, sine, store, reach):
    rows = qkv.shape[0]
    total = chunks(rows, reach)[1]
    column = pl.BlockSpec((rows, HD), lambda i, place, goes: (0, i))
    table = pl.BlockSpec((1, rows, HD // 2), lambda i, place, goes: (0, 0, 0))

    def spec(r, kind):
        return pl.BlockSpec((1, 1, rows, HD), lambda i, place, goes: (place[r], kind, 0, 0))

    return pl.pallas_call(
        functools.partial(attend_back_kernel, reach),
        grid_spec=pltpu.PrefetchScalarGridSpec(
            num_scalar_prefetch=2,
            grid=(HEADS,),
            in_specs=[
                pl.BlockSpec((1, rows, total), lambda i, place, goes: (i, 0, 0)),
                column,
                pl.BlockSpec(branch.shape, lambda i, place, goes: (0, 0)),
                pl.BlockSpec((w_out.shape[0], HD), lambda i, place, goes: (0, i)),
                table,
                table,
            ]
            + [spec(r, kind) for kind in range(2) for r in range(reach + 1)],
            out_specs=[column, ANY],
            scratch_shapes=[
                pltpu.VMEM((rows, total), F32),
                pltpu.VMEM((2, total, HD), F32),
                pltpu.VMEM((reach + 2, 2, rows, HD), BF16),
                pltpu.SemaphoreType.DMA((store.shape[0],)),
            ],
        ),
        out_shape=[
            jax.ShapeDtypeStruct((rows, QW), BF16),
            jax.ShapeDtypeStruct(store.shape, BF16),
        ],
        compiler_params=pltpu.CompilerParams(vmem_limit_bytes=VMEM_LIMIT),
        cost_estimate=takes(24),
        name="attend_back",
    )(place, goes, prob, qkv, branch, w_out, cosine, sine, *([store] * (2 * reach + 2)))


def out_norm_kernel(
    attended, tokens, scale, w_out, middle, own_rows, mate_rows, beyond_rows, wo, other, got, mine, send_sems, recv_sems, own_sems
):
    ctx, z = where_am_i()
    h = z % 2
    net = Net(send_sems, recv_sems)
    mate, beyond = (ctx, flip(z, 1)), (ctx, flip(z, 3))
    own, width = tokens.shape
    quarter = width // 4
    loads = []
    for k in range(4):
        part = pl.ds(k * quarter, quarter)
        loads.append(pltpu.make_async_copy(w_out.at[part], wo.at[part], own_sems.at[k]))
        loads[k].start()
    greet([mate, beyond])
    keep = attended[pl.ds(pl.multiple_of(h * own, 16), own), :]
    give = attended[pl.ds(pl.multiple_of((1 - h) * own, 16), own), :]
    crossing = []
    for k in range(4):
        part = pl.ds(k * quarter, quarter)
        loads[k].wait()
        other[k] = dot_t(give, wo[part, :]).astype(BF16)
        crossing.append(net.push(other.at[k], got.at[k], mate))
        crossing[k].start()
    for k in range(4):
        part = pl.ds(k * quarter, quarter)
        middle[:, part] = tokens[:, part].astype(F32) + dot_t(keep, wo[part, :])
    square = jnp.zeros((own, 1), F32)
    for k in range(4):
        part = pl.ds(k * quarter, quarter)
        crossing[k].wait_recv()
        value = middle[:, part] + got[k].astype(F32)
        middle[:, part] = value
        square = square + jnp.sum(value * value, -1, keepdims=True)
    r = lax.rsqrt(square / width + EPS)
    for k in range(4):
        part = pl.ds(k * quarter, quarter)
        mine[:, part] = (middle[:, part] * r * scale[:, part]).astype(BF16)
    to_mate = net.push(mine, mate_rows, mate)
    to_beyond = net.push(mine, beyond_rows, beyond)
    to_mate.start()
    inner = (z == 1) | (z == 2)
    pl.when(inner)(to_beyond.start)
    local = pltpu.make_async_copy(mine, own_rows, own_sems.at[4])
    local.start()
    for k in range(4):
        crossing[k].wait_send()
    local.wait()
    to_mate.wait()
    pl.when(inner)(to_beyond.wait)


def out_norm(attended, tokens, scale, w_out):
    own, width = tokens.shape
    line = jax.ShapeDtypeStruct((own, width), BF16)
    return pl.pallas_call(
        out_norm_kernel,
        out_shape=[jax.ShapeDtypeStruct((own, width), F32), line, line, line],
        in_specs=[VMEM] * 3 + [ANY],
        out_specs=[VMEM] + [ANY] * 3,
        scratch_shapes=[
            pltpu.VMEM(w_out.shape, BF16),
            pltpu.VMEM((4, own, width // 4), BF16),
            pltpu.VMEM((4, own, width // 4), BF16),
            pltpu.VMEM((own, width), BF16),
            pltpu.SemaphoreType.DMA((6,)),
            pltpu.SemaphoreType.DMA((6,)),
            pltpu.SemaphoreType.DMA((5,)),
        ],
        compiler_params=pltpu.CompilerParams(
            collective_id=3, has_side_effects=True, vmem_limit_bytes=VMEM_LIMIT
        ),
        cost_estimate=takes(55),
        name="out_norm",
    )(attended, tokens, scale, w_out)


def ffn_kernel(
    own_rows,
    mate_rows,
    beyond_rows,
    gate_w,
    up_w,
    rows_out,
    hidden_out,
    active_out,
    sloped_out,
    wg,
    wu,
    x,
    hidden,
    active,
    sloped,
    send_sems,
    recv_sems,
    own_sems,
    out_sems,
):
    ctx, z = where_am_i()
    net = Net(send_sems, recv_sems)
    mate, beyond = (ctx, flip(z, 1)), (ctx, flip(z, 3))
    own, width = own_rows.shape
    units = wg.shape[1]
    step = 384
    count = units // step
    inner = (z == 1) | (z == 2)
    pulls = []
    for m, src in ((0, own_rows), (1, mate_rows)):
        pulls.append(
            pltpu.make_async_copy(src, x.at[pl.ds(m * own, own)], own_sems.at[2 * count + m])
        )
        pulls[m].start()
    loads = []
    for c in range(count):
        span = pl.ds(c * step, step)
        pair = []
        for k, (src, dst) in enumerate(((gate_w, wg), (up_w, wu))):
            pair.append(
                pltpu.make_async_copy(src.at[:, span], dst.at[:, span], own_sems.at[2 * c + k])
            )
            pair[k].start()
        loads.append(pair)
    greet([mate, beyond])
    one_beyond = net.push(mate_rows, x.at[pl.ds(2 * own, own)], beyond)
    three_mate = net.push(beyond_rows, x.at[pl.ds(2 * own, own)], mate)
    two_mate = net.push(x.at[pl.ds(2 * own, own)], x.at[pl.ds(3 * own, own)], mate)
    three_local = pltpu.make_async_copy(
        beyond_rows, x.at[pl.ds(3 * own, own)], own_sems.at[2 * count + 2]
    )

    @pl.when(inner)
    def _():
        one_beyond.start()
        three_mate.start()
        three_local.start()

    def work(first, rows, c, ready):
        if ready is not None:
            for copy in ready:
                copy.wait()
        span = pl.ds(c * step, step)
        at = pl.ds(first, rows)
        gate = dot(x[at, :], wg[:, span])
        up = dot(x[at, :], wu[:, span])
        root, cubic = 0.7978845608028654, 0.044715
        square = gate * gate
        bent = jnp.tanh(root * (gate + cubic * square * gate))
        value = 0.5 * gate * (1.0 + bent)
        slope = 0.5 * (1.0 + bent) + 0.5 * gate * (1.0 - bent * bent) * root * (
            1.0 + 3.0 * cubic * square
        )
        hidden[at, span] = (value * up).astype(BF16)
        active[at, span] = value.astype(BF16)
        sloped[at, span] = (slope * up).astype(BF16)

    outs = []

    def flush(m):
        at = pl.ds(m * own, own)
        pairs = ((hidden, hidden_out), (active, active_out), (sloped, sloped_out), (x, rows_out))
        for k, (src, dst) in enumerate(pairs):
            copy = pltpu.make_async_copy(src.at[at], dst.at[at], out_sems.at[4 * m + k])
            copy.start()
            outs.append(copy)

    for copy in pulls:
        copy.wait()
    for c in range(count):
        work(0, 2 * own, c, loads[c])
    flush(0)
    flush(1)

    @pl.when(inner)
    def _():
        one_beyond.wait_recv()
        two_mate.start()

    @pl.when(jnp.logical_not(inner))
    def _():
        three_mate.wait_recv()

    for c in range(count):
        work(2 * own, own, c, None)
    flush(2)

    @pl.when(inner)
    def _():
        three_local.wait()

    @pl.when(jnp.logical_not(inner))
    def _():
        two_mate.wait_recv()

    for c in range(count):
        work(3 * own, own, c, None)
    flush(3)

    @pl.when(inner)
    def _():
        for copy in (one_beyond, three_mate, two_mate):
            copy.wait_send()

    for copy in outs:
        copy.wait()


def feed_forward(own_rows, mate_rows, beyond_rows, gate_w, up_w):
    own, width = own_rows.shape
    units = gate_w.shape[1]
    count = 4 * own
    inner_shape = jax.ShapeDtypeStruct((count, units), BF16)
    return pl.pallas_call(
        ffn_kernel,
        out_shape=[jax.ShapeDtypeStruct((count, width), BF16)] + [inner_shape] * 3,
        in_specs=[ANY] * 5,
        out_specs=[ANY] * 4,
        scratch_shapes=[
            pltpu.VMEM((width, units), BF16),
            pltpu.VMEM((width, units), BF16),
            pltpu.VMEM((count, width), BF16),
            pltpu.VMEM((count, units), BF16),
            pltpu.VMEM((count, units), BF16),
            pltpu.VMEM((count, units), BF16),
            pltpu.SemaphoreType.DMA((3,)),
            pltpu.SemaphoreType.DMA((3,)),
            pltpu.SemaphoreType.DMA((2 * (units // 384) + 3,)),
            pltpu.SemaphoreType.DMA((16,)),
        ],
        compiler_params=pltpu.CompilerParams(
            collective_id=6, has_side_effects=True, vmem_limit_bytes=VMEM_LIMIT
        ),
        cost_estimate=takes(52),
        name="feed_forward",
    )(own_rows, mate_rows, beyond_rows, gate_w, up_w)


def ffn_grad_kernel(c0, c1, c2, c3, down_w, active, sloped, cot, grad_gate, grad_up):
    own = c0.shape[0]

    @pl.when(pl.program_id(0) == 0)
    def _():
        for m, piece in enumerate((c0, c1, c2, c3)):
            cot[m * own : (m + 1) * own, :] = piece[...]

    grad = dot(cot[...], down_w[...])
    grad_gate[...] = (sloped[...].astype(F32) * grad).astype(BF16)
    grad_up[...] = (active[...].astype(F32) * grad).astype(BF16)


def ffn_specs(count, width, units):
    step = 384 if units % 384 == 0 else 128
    whole = pl.BlockSpec((count, width), lambda i: (0, 0))
    weight = pl.BlockSpec((width, step), lambda i: (0, i))
    column = pl.BlockSpec((count, step), lambda i: (0, i))
    return units // step, whole, weight, column


def feed_forward_grad(cots, down_w, active, sloped):
    own, width = cots[0].shape
    count, units = active.shape
    steps, whole, weight, column = ffn_specs(count, width, units)
    piece = pl.BlockSpec((own, width), lambda i: (0, 0))
    return pl.pallas_call(
        ffn_grad_kernel,
        grid=(steps,),
        out_shape=[jax.ShapeDtypeStruct((count, width), BF16)]
        + [jax.ShapeDtypeStruct((count, units), BF16)] * 2,
        in_specs=[piece] * 4 + [weight, column, column],
        out_specs=[whole, column, column],
        compiler_params=pltpu.CompilerParams(vmem_limit_bytes=VMEM_LIMIT),
        cost_estimate=takes(15),
        name="feed_forward_grad",
    )(*cots, down_w, active, sloped)


def ffn_back_kernel(
    grad_gate,
    grad_up,
    gate_w,
    up_w,
    down_w,
    hidden,
    rows_in,
    middle,
    cot,
    scale,
    gate_out,
    up_out,
    ffn_part,
    grad_middle,
    branch,
    grad_scale,
    gg,
    gu,
    wg,
    wu,
    x,
    parts,
    got,
    stage,
    mine,
    send_sems,
    recv_sems,
    own_sems,
    stage_sems,
):
    ctx, z = where_am_i()
    net = Net(send_sems, recv_sems)
    mate, beyond = (ctx, flip(z, 1)), (ctx, flip(z, 3))
    greet([mate, beyond])
    inner = (z == 1) | (z == 2)
    own, width = middle.shape
    units = gg.shape[1]
    quarter = width // 4
    order = (3, 2, 1, 0)
    loads = {}
    used = 0

    def load(name, src, dst):
        nonlocal used
        loads[name] = pltpu.make_async_copy(src, dst, own_sems.at[used])
        loads[name].start()
        used += 1

    for k, m in enumerate(order):
        span = pl.ds(m * own, own)
        load(("gg", m), grad_gate.at[span], gg.at[span])
        load(("gu", m), grad_up.at[span], gu.at[span])
        part = pl.ds(k * quarter, quarter)
        load(("wg", k), gate_w.at[part], wg.at[part])
        load(("wu", k), up_w.at[part], wu.at[part])
    load("x", rows_in, x)

    far = net.push(parts.at[3], got.at[0], mate)
    near = net.push(parts.at[2], got.at[1], mate)
    two_over = net.push(parts.at[2], got.at[2], beyond)
    three_over = net.push(parts.at[3], got.at[3], beyond)
    one_mate = net.push(parts.at[1], got.at[4], mate)

    def make(m):
        span = pl.ds(m * own, own)
        loads["gg", m].wait()
        loads["gu", m].wait()
        for k in range(4):
            part = pl.ds(k * quarter, quarter)
            if m == 3:
                loads["wg", k].wait()
                loads["wu", k].wait()
            value = dot_t(gg[span, :], wg[part, :]) + dot_t(gu[span, :], wu[part, :])
            parts[m, :, part] = value.astype(BF16)

    def add_to(m, k):
        parts[m] = (parts[m].astype(F32) + got[k].astype(F32)).astype(BF16)

    make(3)
    pl.when(jnp.logical_not(inner))(far.start)
    make(2)
    pl.when(jnp.logical_not(inner))(near.start)
    make(1)
    make(0)
    load("wd", down_w, wg)
    loads["x"].wait()

    def weight_grad(g, out):
        step = 256

        def copy(i):
            return pltpu.make_async_copy(
                stage.at[i % 2],
                out.at[pl.ds(pl.multiple_of(i * step, step), step)],
                stage_sems.at[i % 2],
            )

        def body(i, carry):
            @pl.when(i >= 2)
            def _():
                copy(i - 2).wait()

            at = pl.ds(pl.multiple_of(i * step, step), step)
            stage[i % 2] = t_dot(x[:, at], g[...]).astype(BF16)
            copy(i).start()
            return carry

        count = width // step
        lax.fori_loop(0, count, body, 0)
        copy(count - 2).wait()
        copy(count - 1).wait()

    @pl.when(inner)
    def _():
        far.wait_recv()
        add_to(2, 0)
        two_over.start()

    weight_grad(gg, gate_out)

    @pl.when(inner)
    def _():
        near.wait_recv()
        add_to(3, 1)
        three_over.start()
        two_over.wait_recv()
        add_to(1, 2)

    one_mate.start()
    weight_grad(gu, up_out)
    load("hidden", hidden, gu)
    one_mate.wait_recv()
    grad = parts[0].astype(F32) + got[4].astype(F32)
    grad_middle[...] = grad

    @pl.when(inner)
    def _():
        three_over.wait_recv()
        grad_middle[...] += got[3].astype(F32)

    grad = grad_middle[...]
    value = middle[...]
    r = inv_rms(value)
    scaled = grad * scale[...]
    lean = jnp.mean(scaled * value, -1, keepdims=True)
    grad_scale[...] = jnp.sum(grad * value * r, 0, keepdims=True)
    total = cot[...].astype(F32) + (r * scaled - value * (r * r * r * lean))
    grad_middle[...] = total
    mine[...] = total.astype(BF16)
    dst = branch.at[pl.ds(pl.multiple_of((z % 2) * own, 16), own)]
    last = net.push(mine, dst, mate)
    last.start()
    local = pltpu.make_async_copy(mine, dst, own_sems.at[used])
    local.start()
    one_mate.wait_send()

    @pl.when(inner)
    def _():
        two_over.wait_send()
        three_over.wait_send()

    @pl.when(jnp.logical_not(inner))
    def _():
        far.wait_send()
        near.wait_send()

    loads["wd"].wait()
    loads["hidden"].wait()
    out_copies = []
    for m in range(4):
        span = pl.ds(m * own, own)
        for k in range(4):
            part = pl.ds(k * quarter, quarter)
            parts[m, :, part] = dot_t(gu[span, :], wg[part, :]).astype(BF16)
        copy = pltpu.make_async_copy(parts.at[m], ffn_part.at[m], own_sems.at[used + 1 + m])
        copy.start()
        out_copies.append(copy)
    local.wait()
    last.wait_recv()
    last.wait_send()
    for copy in out_copies:
        copy.wait()


def feed_forward_back(grad_gate, grad_up, gate_w, up_w, down_w, hidden, rows_in, middle, cot, scale):
    own, width = middle.shape
    count, units = hidden.shape
    return pl.pallas_call(
        ffn_back_kernel,
        out_shape=[
            jax.ShapeDtypeStruct((width, units), BF16),
            jax.ShapeDtypeStruct((width, units), BF16),
            jax.ShapeDtypeStruct((4, own, width), BF16),
            jax.ShapeDtypeStruct((own, width), F32),
            jax.ShapeDtypeStruct((2 * own, width), BF16),
            jax.ShapeDtypeStruct((1, width), F32),
        ],
        in_specs=[ANY] * 7 + [VMEM] * 3,
        out_specs=[ANY, ANY, ANY, VMEM, ANY, VMEM],
        scratch_shapes=[
            pltpu.VMEM((count, units), BF16),
            pltpu.VMEM((count, units), BF16),
            pltpu.VMEM((width, units), BF16),
            pltpu.VMEM((width, units), BF16),
            pltpu.VMEM((count, width), BF16),
            pltpu.VMEM((4, own, width), BF16),
            pltpu.VMEM((5, own, width), BF16),
            pltpu.VMEM((2, 256, units), BF16),
            pltpu.VMEM((own, width), BF16),
            pltpu.SemaphoreType.DMA((6,)),
            pltpu.SemaphoreType.DMA((6,)),
            pltpu.SemaphoreType.DMA((24,)),
            pltpu.SemaphoreType.DMA((2,)),
        ],
        compiler_params=pltpu.CompilerParams(
            collective_id=5, has_side_effects=True, vmem_limit_bytes=60 * 1024 * 1024
        ),
        cost_estimate=takes(100),
        name="feed_forward_back",
    )(grad_gate, grad_up, gate_w, up_w, down_w, hidden, rows_in, middle, cot, scale)


def fold(ref, other):
    ref[...] = (ref[...].astype(F32) + other[...].astype(F32)).astype(BF16)


class KvSum:
    def __init__(self, net, parts, out, mine, got_sib, got_diag, got_x, got_y, got_z, give, sems):
        ctx, z = where_am_i()
        self.h, self.upper = z % 2, z // 2 == 1
        self.refs = (out, mine, got_sib, got_diag, got_x, got_y, got_z, give)
        x_dev, y_dev, sib = (flip(ctx, 2), z), (flip(ctx, 4), z), (flip(ctx, 1), z)
        self.load, self.over, self.diag, self.near = {}, {}, {}, {}
        for s in range(2):
            for i, m in enumerate((6, 2, 4, 0)):
                self.load[s, i] = pltpu.make_async_copy(
                    parts.at[s, flip(ctx, m)], mine.at[s, i], sems.at[4 * s + i]
                )
                self.over[s, i] = net.push(
                    parts.at[s, flip(flip(ctx, 1), m)], got_sib.at[s, i], sib
                )
            self.diag[s] = [
                net.push(mine.at[s, 0, 0], got_diag.at[s, 0], y_dev),
                net.push(mine.at[s, 0, 1], got_diag.at[s, 1], x_dev),
            ]
            self.near[s] = [
                net.push(mine.at[s, 1], got_x.at[s], x_dev),
                net.push(mine.at[s, 2], got_y.at[s], y_dev),
            ]
        self.to_mate = net.push(give.at[0], got_z.at[0], (ctx, flip(z, 1)))
        self.to_low = net.push(give.at[1], got_z.at[1], (ctx, flip(z, 2)))
        self.to_low_mate = net.push(give.at[2], got_z.at[2], (ctx, flip(z, 3)))

    def both(self, stage):
        stage(0)
        pl.when(self.upper)(lambda: stage(1))

    def start(self, s):
        for i in range(4):
            self.over[s, i].start()
            self.load[s, i].start()

    def chip_sums(self, s):
        mine, got_sib = self.refs[1:3]
        for i in range(4):
            self.load[s, i].wait()
            self.over[s, i].wait_recv()
            fold(mine.at[s, i], got_sib.at[s, i])
            if i == 0:
                for copy in self.diag[s]:
                    copy.start()

    def forward(self, s):
        mine, got_diag = self.refs[1], self.refs[3]
        for k in range(2):
            self.diag[s][k].wait_recv()
            fold(mine.at[s, 1 + k, k], got_diag.at[s, k])
            self.near[s][k].start()

    def total(self, s, kind):
        mine, got_x, got_y = self.refs[1], self.refs[4], self.refs[5]
        value = mine[s, 3, kind].astype(F32) + got_x[s, kind].astype(F32)
        return value + got_y[s, kind].astype(F32)

    def across(self):
        out, give, h = self.refs[0], self.refs[7], self.h
        for copy in self.near[0]:
            copy.wait_recv()

        @pl.when(jnp.logical_not(self.upper))
        def _():
            give[0] = self.total(0, 1 - h).astype(BF16)
            out[...] = self.total(0, h)

        @pl.when(self.upper)
        def _():
            give[1] = self.total(0, h).astype(BF16)
            give[2] = self.total(0, 1 - h).astype(BF16)
            self.to_low.start()
            self.to_low_mate.start()
            for copy in self.near[1]:
                copy.wait_recv()
            give[0] = self.total(1, 1 - h).astype(BF16)
            out[...] = self.total(1, h)

        self.to_mate.start()

    def finish(self):
        out, got_z = self.refs[0], self.refs[6]
        self.to_mate.wait_recv()
        out[...] += got_z[0].astype(F32)

        @pl.when(jnp.logical_not(self.upper))
        def _():
            self.to_low.wait_recv()
            self.to_low_mate.wait_recv()
            out[...] += got_z[1].astype(F32) + got_z[2].astype(F32)

        def sent(s):
            for i in range(4):
                self.over[s, i].wait_send()
            for copy in self.diag[s] + self.near[s]:
                copy.wait_send()

        self.both(sent)
        self.to_mate.wait_send()

        @pl.when(self.upper)
        def _():
            self.to_low.wait_send()
            self.to_low_mate.wait_send()

    @staticmethod
    def scratch(rows):
        block = (2, rows, HD)
        return [
            pltpu.VMEM((2, 4) + block, BF16),
            pltpu.VMEM((2, 4) + block, BF16),
            pltpu.VMEM((2, 2, rows, HD), BF16),
            pltpu.VMEM((2,) + block, BF16),
            pltpu.VMEM((2,) + block, BF16),
            pltpu.VMEM((3, rows, HD), BF16),
            pltpu.VMEM((3, rows, HD), BF16),
            pltpu.SemaphoreType.DMA((8,)),
        ]

    copies = 19


class WeightSum:
    def __init__(self, net, widths, parts, out, mine, got_sib, got_diag, got_x, got_y, got_z, total, sems):
        ctx, z = where_am_i()
        self.net, self.z = net, z
        self.ctx = ctx
        self.parts, self.out, self.sems = parts, out, sems
        self.refs = (mine, got_sib, got_diag, got_x, got_y, got_z, total)
        self.x_dev, self.y_dev, self.sib = (flip(ctx, 2), z), (flip(ctx, 4), z), (flip(ctx, 1), z)
        self.rows = mine.shape[1]
        self.copies = {}
        self.spans, col = [], 0
        for count in widths:
            self.spans.append(pl.ds(col, count))
            col += count

    def add_to(self, ref, other, count):
        step = 32

        def body(i, carry):
            at = pl.ds(pl.multiple_of(i * step, step), step)
            ref[at, :] = (ref[at, :].astype(F32) + other[at, :].astype(F32)).astype(BF16)
            return carry

        lax.fori_loop(0, count // step, body, 0)

    def start(self, g):
        mine, got_sib = self.refs[:2]
        span, rows, ctx = self.spans[g], self.rows, self.ctx

        def block_rows(source):
            return pl.ds(pl.multiple_of(source * rows, 16), rows)

        for i, m in enumerate((6, 2, 4, 0)):
            load = pltpu.make_async_copy(
                self.parts.at[block_rows(flip(ctx, m)), span],
                mine.at[i, :, span],
                self.sems.at[4 * g + i],
            )
            over = self.net.push(
                self.parts.at[block_rows(flip(flip(ctx, 1), m)), span],
                got_sib.at[i, :, span],
                self.sib,
            )
            load.start()
            over.start()
            self.copies[g, i] = (load, over)

    def chip_sums(self, g):
        mine, got_sib, got_diag = self.refs[:3]
        span, rows = self.spans[g], self.rows
        cut = rows // 2
        for i in range(4):
            load, over = self.copies[g, i]
            load.wait()
            over.wait_recv()
            self.add_to(mine.at[i, :, span], got_sib.at[i, :, span], rows)
            if i == 0:
                pair = []
                for k, to in enumerate((self.y_dev, self.x_dev)):
                    part = pl.ds(k * cut, cut)
                    pair.append(self.net.push(mine.at[0, part, span], got_diag.at[part, span], to))
                    pair[k].start()
                self.copies[g, "diag"] = pair

    def forward(self, g):
        mine, _, got_diag, got_x, got_y = self.refs[:5]
        span = self.spans[g]
        cut = self.rows // 2
        pair = []
        for k, (got, to) in enumerate(((got_x, self.x_dev), (got_y, self.y_dev))):
            part = pl.ds(k * cut, cut)
            self.copies[g, "diag"][k].wait_recv()
            self.add_to(mine.at[1 + k, part, span], got_diag.at[part, span], cut)
            pair.append(self.net.push(mine.at[1 + k, :, span], got.at[:, span], to))
            pair[k].start()
        self.copies[g, "near"] = pair

    def line(self, g):
        mine, _, _, got_x, got_y, got_z, total = self.refs
        span, rows, z = self.spans[g], self.rows, self.z
        unit = rows // 4
        for copy in self.copies[g, "near"]:
            copy.wait_recv()
        step = 16

        def body(i, carry):
            at = pl.ds(pl.multiple_of(i * step, step), step)
            value = mine[3, at, span].astype(F32) + got_x[at, span].astype(F32)
            total[at, span] = (value + got_y[at, span].astype(F32)).astype(BF16)
            return carry

        lax.fori_loop(0, rows // step, body, 0)
        sends = []
        for k, m in enumerate((1, 2, 3)):
            start_row = pl.multiple_of(flip(z, m) * unit, 16)
            copy = self.net.push(
                total.at[pl.ds(start_row, unit), span],
                got_z.at[k, :, span],
                (self.ctx, flip(z, m)),
            )
            copy.start()
            sends.append(copy)
        self.copies[g, "line"] = sends

    def finish(self, g):
        got_z, total = self.refs[5:]
        span, unit = self.spans[g], self.rows // 4
        for copy in self.copies[g, "line"]:
            copy.wait_recv()
        own_row = pl.multiple_of(self.z * unit, 16)
        h = self.z % 2
        own_cols = total[pl.ds(own_row, unit), span].astype(F32)
        self.out[h, :, span] = own_cols + got_z[1, :, span].astype(F32)
        self.out[1 - h, :, span] = got_z[0, :, span].astype(F32) + got_z[2, :, span].astype(F32)
        for i in range(4):
            self.copies[g, i][1].wait_send()
        for name in ("diag", "near", "line"):
            for copy in self.copies[g, name]:
                copy.wait_send()

    @staticmethod
    def scratch(rows, shard, columns, groups):
        return [
            pltpu.VMEM((4, rows, columns), BF16),
            pltpu.VMEM((4, rows, columns), BF16),
            pltpu.VMEM((rows, columns), BF16),
            pltpu.VMEM((rows, columns), BF16),
            pltpu.VMEM((rows, columns), BF16),
            pltpu.VMEM((3, shard, columns), BF16),
            pltpu.VMEM((rows, columns), BF16),
            pltpu.SemaphoreType.DMA((4 * groups,)),
        ]


def everyone():
    ctx, z = where_am_i()
    return [(ctx, flip(z, m)) for m in (1, 2, 3)] + [(flip(ctx, m), z) for m in (1, 2, 4)]


def first_sums_kernel(widths, kv_parts, w_parts, line_parts, middle, kv_out, w_out, output, *scratch):
    ctx, z = where_am_i()
    kv_scratch, scratch = scratch[:8], scratch[8:]
    w_scratch, scratch = scratch[:8], scratch[8:]
    parts, got, send_sems, recv_sems, own_sems = scratch
    net = Net(send_sems, recv_sems)
    greet(everyone())
    mate, beyond = (ctx, flip(z, 1)), (ctx, flip(z, 3))
    inner = (z == 1) | (z == 2)
    outer = jnp.logical_not(inner)
    kv = KvSum(net, kv_parts, kv_out, *kv_scratch)
    weights = WeightSum(net, widths, w_parts, w_out, *w_scratch)
    far = net.push(line_parts.at[3], got.at[0], mate)
    near = net.push(line_parts.at[2], got.at[1], mate)
    two_over = net.push(parts.at[2], got.at[2], beyond)
    three_over = net.push(parts.at[3], got.at[3], beyond)
    one_mate = net.push(parts.at[1], got.at[4], mate)
    kv.both(kv.start)

    @pl.when(outer)
    def _():
        far.start()
        near.start()

    for g in range(len(widths)):
        weights.start(g)
    loads = []
    for m in range(4):
        loads.append(pltpu.make_async_copy(line_parts.at[m], parts.at[m], own_sems.at[m]))
        loads[m].start()
    kv.both(kv.chip_sums)
    weights.chip_sums(0)
    kv.both(kv.forward)
    weights.chip_sums(1)
    weights.forward(0)
    for copy in loads:
        copy.wait()

    @pl.when(inner)
    def _():
        far.wait_recv()
        fold(parts.at[2], got.at[0])
        two_over.start()

    kv.across()
    weights.forward(1)
    weights.line(0)

    @pl.when(inner)
    def _():
        near.wait_recv()
        fold(parts.at[3], got.at[1])
        three_over.start()
        two_over.wait_recv()
        fold(parts.at[1], got.at[2])

    one_mate.start()
    weights.line(1)
    kv.finish()
    weights.finish(0)
    weights.finish(1)
    one_mate.wait_recv()

    @pl.when(outer)
    def _():
        total = middle[...] + parts[0].astype(F32)
        output[...] = (total + got[4].astype(F32)).astype(BF16)
        far.wait_send()
        near.wait_send()

    @pl.when(inner)
    def _():
        three_over.wait_recv()
        total = middle[...] + parts[0].astype(F32) + got[3].astype(F32)
        output[...] = (total + got[4].astype(F32)).astype(BF16)
        two_over.wait_send()
        three_over.wait_send()

    one_mate.wait_send()


def plain_axes(shard):
    return lax.axis_size("ctx") != 8 or lax.axis_size("fsdp") != 4 or shard % 16


def plain_weight_sum(parts):
    z = lax.axis_index("fsdp")
    empty = jnp.zeros_like(parts)
    both = jnp.where(z % 2 == 0, jnp.stack([parts, empty]), jnp.stack([empty, parts]))
    summed = lax.psum_scatter(both, "ctx", scatter_dimension=1, tiled=True)
    return lax.psum_scatter(summed, "fsdp", scatter_dimension=1, tiled=True).astype(F32)


def first_sums(kv_parts, w_parts, line_parts, middle, shard):
    total, _, rows, _ = kv_parts.shape
    ctx_total = total // 2
    kv_parts = kv_parts.reshape(2, ctx_total, 2, rows, HD)
    own, width = middle.shape
    if plain_axes(shard):
        flat = kv_parts.transpose(0, 2, 1, 3, 4).reshape(4 * ctx_total * rows, HD)
        z_sum = lax.psum_scatter(flat, "fsdp", scatter_dimension=0, tiled=True)
        kv = lax.psum_scatter(z_sum, "ctx", scatter_dimension=0, tiled=True).astype(F32)
        out = middle + line_parts[0].astype(F32)
        for m in (1, 2, 3):
            out = out + swap(line_parts[m], "fsdp", m).astype(F32)
        return kv, plain_weight_sum(w_parts), out.astype(BF16)
    block = width // ctx_total
    widths = (QW // 2, QW // 2)
    copies = KvSum.copies + 11 * len(widths) + 5
    return pl.pallas_call(
        functools.partial(first_sums_kernel, widths),
        out_shape=[
            jax.ShapeDtypeStruct((rows, HD), F32),
            jax.ShapeDtypeStruct((2, shard, QW), F32),
            jax.ShapeDtypeStruct((own, width), BF16),
        ],
        in_specs=[ANY] * 3 + [VMEM],
        out_specs=[VMEM] * 3,
        scratch_shapes=KvSum.scratch(rows)
        + WeightSum.scratch(block, shard, QW, len(widths))
        + [
            pltpu.VMEM((4, own, width), BF16),
            pltpu.VMEM((4 + 1, own, width), BF16),
            pltpu.SemaphoreType.DMA((copies,)),
            pltpu.SemaphoreType.DMA((copies,)),
            pltpu.SemaphoreType.DMA((4,)),
        ],
        compiler_params=pltpu.CompilerParams(
            collective_id=2, has_side_effects=True, vmem_limit_bytes=60 * 1024 * 1024
        ),
        cost_estimate=takes(65),
        name="first_sums",
    )(kv_parts, w_parts, line_parts, middle)


def last_sums_kernel(widths, w_parts, grad_rows, tokens, scale, grad_middle, ffn_scale_grad, w_out, grad_tokens, scales, *scratch):
    ctx, z = where_am_i()
    w_scratch, scratch = scratch[:8], scratch[8:]
    give, got, scale_got, send_sems, recv_sems = scratch
    h = z % 2
    net = Net(send_sems, recv_sems)
    own = tokens.shape[0]
    greet(everyone())
    weights = WeightSum(net, widths, w_parts, w_out, *w_scratch)
    give[...] = grad_rows[pl.ds(pl.multiple_of((1 - h) * own, 16), own), :].astype(BF16)
    mate = net.push(give, got, (ctx, flip(z, 1)))
    mate.start()
    n = len(widths)
    for g in range(n):
        weights.start(g)
    partners = [(ctx, flip(z, 1)), (ctx, flip(z, 2))] + [(flip(ctx, m), z) for m in (1, 2, 4)]
    trade = []

    def trade_send(k):
        trade.append(net.push(scales, scale_got.at[k], partners[k]))
        trade[k].start()

    def trade_add(k):
        trade[k].wait()
        scales[...] += scale_got[k]

    def norm_part():
        mate.wait_recv()
        value = tokens[...].astype(F32)
        grad = grad_rows[pl.ds(pl.multiple_of(h * own, 16), own), :] + got[...].astype(F32)
        r = inv_rms(value)
        scaled = grad * scale[...]
        lean = jnp.mean(scaled * value, -1, keepdims=True)
        grad_tokens[...] = grad_middle[...] + (r * scaled - value * (r * r * r * lean))
        scales[...] = jnp.zeros_like(scales)
        scales[0:1, :] = jnp.sum(grad * value * r, 0, keepdims=True)
        scales[1:2, :] = ffn_scale_grad[...]
        trade_send(0)

    def trade_next(k):
        trade_add(k)
        if k + 1 < len(partners):
            trade_send(k + 1)

    weights.chip_sums(0)
    weights.chip_sums(1)
    weights.forward(0)
    weights.chip_sums(2)
    weights.forward(1)
    norm_part()
    weights.line(0)
    weights.forward(2)
    trade_next(0)
    weights.line(1)
    trade_next(1)
    weights.line(2)
    trade_next(2)
    weights.finish(0)
    trade_next(3)
    weights.finish(1)
    trade_next(4)
    weights.finish(2)
    mate.wait_send()


def last_sums(w_parts, grad_rows, tokens, scale, grad_middle, ffn_scale_grad, shard):
    own, width = tokens.shape
    columns = w_parts.shape[1]
    if plain_axes(shard):
        h = lax.axis_index("fsdp") % 2
        other = swap(half(grad_rows, 1 - h).astype(BF16), "fsdp", 1).astype(F32)
        grad, scale_grad = norm_back(tokens.astype(F32), scale, half(grad_rows, h) + other)
        scales = jnp.concatenate([scale_grad[None], ffn_scale_grad])
        return plain_weight_sum(w_parts), grad_middle + grad, lax.psum(scales, ("ctx", "fsdp"))
    block = 4 * shard
    widths = (QW // 2, QW // 2, HD)
    copies = 11 * len(widths) + 1 + 5
    weights, grad, scales = pl.pallas_call(
        functools.partial(last_sums_kernel, widths),
        out_shape=[
            jax.ShapeDtypeStruct((2, shard, columns), F32),
            jax.ShapeDtypeStruct((own, width), F32),
            jax.ShapeDtypeStruct((8, width), F32),
        ],
        in_specs=[ANY] + [VMEM] * 5,
        out_specs=[VMEM] * 3,
        scratch_shapes=WeightSum.scratch(block, shard, columns, len(widths))
        + [
            pltpu.VMEM((own, width), BF16),
            pltpu.VMEM((own, width), BF16),
            pltpu.VMEM((5, 8, width), F32),
            pltpu.SemaphoreType.DMA((copies,)),
            pltpu.SemaphoreType.DMA((copies,)),
        ],
        compiler_params=pltpu.CompilerParams(
            collective_id=4, has_side_effects=True, vmem_limit_bytes=60 * 1024 * 1024
        ),
        cost_estimate=takes(60),
        name="last_sums",
    )(w_parts, grad_rows, tokens, scale, grad_middle, ffn_scale_grad)
    return weights, grad, scales[:2]


def local(
    tokens,
    lengths,
    block_place,
    gain_attn,
    w_query,
    w_key,
    w_value,
    w_out,
    gain_ffn,
    w_gate,
    w_up,
    w_down,
    cotangent,
):
    own_rows, width = tokens.shape
    rows = 2 * own_rows
    ctx_total = lax.axis_size("ctx")
    ctx, z = where_am_i()
    h, pair = z % 2, z // 2
    shard = w_query.shape[0]
    reach = -(-WIN // rows)

    def place_of(stored):
        hit = jnp.arange(block_place.shape[0])[None, :] == stored[:, None]
        return jnp.sum(jnp.where(hit, block_place[None, :], 0), 1)

    own_pos = place_of((2 * ctx + pair)[None])[0]
    query_at = own_pos * rows + jnp.arange(rows, dtype=jnp.int32)
    passed = query_at[:, None] >= jnp.cumsum(lengths)[None, :]
    doc_start = jnp.sum(jnp.where(passed, lengths[None, :], 0), 1)
    rel_pos = query_at - doc_start
    window_start = (own_pos - reach) * rows
    lowest = jnp.maximum(doc_start, query_at - WIN + 1) - window_start
    lowest = jnp.broadcast_to(lowest[:, None], (rows, 128)).astype(jnp.int32)
    holders = jnp.arange(ctx_total)
    held = jnp.concatenate([place_of(2 * holders), place_of(2 * holders + 1)])
    held = jnp.where((pair == 1) | (jnp.arange(2 * ctx_total) < ctx_total), held, -1000)
    want = own_pos - reach + jnp.arange(reach + 1)
    hit = held[None, :] == want[:, None]
    numbers = jnp.arange(2 * ctx_total)
    own_index = pair * ctx_total + ctx
    place = jnp.where(jnp.any(hit, 1), jnp.sum(jnp.where(hit, numbers, 0), 1), own_index)
    place = place.astype(jnp.int32)
    goes = held - (own_pos - reach)
    goes = jnp.where((goes >= 0) & (goes <= reach), goes, reach + 1).astype(jnp.int32)
    half_dim = HD // 2
    frequency = jnp.exp(jnp.arange(half_dim, dtype=F32) * (-jnp.log(10000.0) / half_dim))
    angles = rel_pos.astype(F32)[:, None] * frequency
    cosine, sine = jnp.cos(angles), jnp.sin(angles)
    q_scale = HD ** (-0.5)
    kv_cosine, kv_sine = jnp.where(h == 0, cosine, 1.0), jnp.where(h == 0, sine, 0.0)
    cosine = jnp.stack([cosine * q_scale, kv_cosine])
    sine = jnp.stack([sine * q_scale, kv_sine])

    w_qkv, w_o, gains, rows_in, cot_one, cot_three = gather_weights(
        w_query, w_key, w_value, w_out, gain_attn, gain_ffn, tokens, cotangent
    )
    w_qkv, w_o, w_gate, w_up, w_down = lax.optimization_barrier(
        (w_qkv, w_o, w_gate, w_up, w_down.T)
    )
    gate_w = lax.all_gather(w_gate, "ctx", axis=0, tiled=True)
    up_w = lax.all_gather(w_up, "ctx", axis=0, tiled=True)
    down_w = lax.all_gather(w_down, "ctx", axis=0, tiled=True)
    attn_scale, ffn_scale = gains[:1], gains[1:]
    normed, queries, kv = project(rows_in, attn_scale, cosine, sine, w_qkv)
    store, cot_two = gather_kv(kv, cot_one, cot_three, cotangent)
    outer = lax.ppermute(cot_two, "fsdp", [(1, 0), (2, 3)])
    if ctx_total == 8:
        cot_three = jnp.where((z == 1) | (z == 2), cot_three, outer)
    cots = (cotangent, cot_one, cot_two, cot_three)
    prob, attended = attend(place, lowest, queries, store, reach)
    middle, own_normed, mate_normed, beyond_normed = out_norm(attended, tokens, ffn_scale, w_o)

    ffn_in, hidden, active, sloped = feed_forward(
        own_normed, mate_normed, beyond_normed, gate_w, up_w
    )
    ffn_cot, grad_gate, grad_up = feed_forward_grad(cots, down_w, active, sloped)

    def sum_ctx(g):
        return lax.psum_scatter(g, "ctx", scatter_dimension=0, tiled=True).astype(F32)

    down_part = t_dot(ffn_cot, hidden).astype(BF16)
    down_part, grad_gate, grad_up = lax.optimization_barrier((down_part, grad_gate, grad_up))
    grad_down = sum_ctx(down_part).T
    gate_part, up_part, ffn_part, grad_middle, grad_branch, grad_ffn_scale = feed_forward_back(
        grad_gate, grad_up, gate_w, up_w, down_w, hidden, ffn_in, middle, cotangent, ffn_scale
    )
    grad_gate_w = sum_ctx(gate_part)
    grad_up_w = sum_ctx(up_part)
    grad_out_part = t_dot(grad_branch, attended).astype(BF16)
    grad_out_part, grad_down = lax.optimization_barrier((grad_out_part, grad_down))

    grad_q, kv_parts = attend_back(
        place, goes, prob, queries, grad_branch, w_o, cosine, sine, store, reach
    )
    grad_kv, out_sum, output = first_sums(kv_parts, grad_out_part, ffn_part, middle, shard)
    grad_kv, grad_gate_w = lax.optimization_barrier((grad_kv, grad_gate_w))
    front, back = grad_kv[:, :half_dim], grad_kv[:, half_dim:]
    grad_kv = jnp.concatenate(
        [front * kv_cosine + back * kv_sine, back * kv_cosine - front * kv_sine], 1
    ).astype(BF16)
    grad_qkv = jnp.concatenate([grad_q, grad_kv], 1)
    w_parts = t_dot(normed, grad_qkv).astype(BF16)
    grad_rows = dot_t(grad_qkv, w_qkv)
    summed, grad_tokens, scales = last_sums(
        w_parts, grad_rows, tokens, attn_scale, grad_middle, grad_ffn_scale, shard
    )
    first_col = (ctx * lax.axis_size("fsdp") + z) * shard
    scales = lax.dynamic_slice_in_dim(scales, first_col, shard, 1)
    grad_out_w = jnp.concatenate([out_sum[0], out_sum[1]], 1).T
    grad_query_w = jnp.concatenate([summed[0, :, :QW], summed[1, :, :QW]], 1)
    return (
        output,
        grad_tokens,
        scales[0],
        grad_query_w,
        summed[0, :, QW:],
        summed[1, :, QW:],
        grad_out_w,
        scales[1],
        grad_gate_w,
        grad_up_w,
        grad_down,
    )


def solution(mesh):
    in_specs = (
        P(("ctx", "fsdp"), None),
        P(),
        P(),
        P(("ctx", "fsdp")),
        P(("ctx", "fsdp"), None),
        P(("ctx", "fsdp"), None),
        P(("ctx", "fsdp"), None),
        P(None, ("ctx", "fsdp")),
        P(("ctx", "fsdp")),
        P("ctx", "fsdp"),
        P("ctx", "fsdp"),
        P("fsdp", "ctx"),
        P(("ctx", "fsdp"), None),
    )
    out_specs = (
        P(("ctx", "fsdp"), None),
        P(("ctx", "fsdp"), None),
        P(("ctx", "fsdp")),
        P(("ctx", "fsdp"), None),
        P(("ctx", "fsdp"), None),
        P(("ctx", "fsdp"), None),
        P(None, ("ctx", "fsdp")),
        P(("ctx", "fsdp")),
        P("ctx", "fsdp"),
        P("ctx", "fsdp"),
        P("fsdp", "ctx"),
    )
    return jax.shard_map(local, mesh=mesh, in_specs=in_specs, out_specs=out_specs, check_vma=False)
```

```python
import functools

import jax
import jax.numpy as jnp
from jax import lax
from jax.experimental import pallas as pl
from jax.experimental.pallas import tpu as pltpu
from jax.sharding import PartitionSpec as P

H = 10
HD = 256
WIN = 2048
EPS = 1e-06
F32 = jnp.float32
BF16 = jnp.bfloat16
MESH = pl.DeviceIdType.MESH
ANY = pl.BlockSpec(memory_space=pl.ANY)
VMEM = pl.BlockSpec(memory_space=pltpu.VMEM)
HEADS = H // 2
QW = HEADS * HD
VMEM_LIMIT = 56 * 1024 * 1024
FAR = -1e30


def swap(x, axis, mask):
    return lax.ppermute(x, axis, [(i, i ^ mask) for i in range(lax.axis_size(axis))])


def join(own, other, bit, axis):
    return jnp.where(
        bit == 0,
        jnp.concatenate([own, other], axis),
        jnp.concatenate([other, own], axis),
    )


def half(x, which, axis=0):
    size = x.shape[axis] // 2
    return lax.dynamic_slice_in_dim(x, which * size, size, axis)


def dot(a, b):
    return jnp.dot(a, b, preferred_element_type=F32)


def dot_t(a, b):
    return lax.dot_general(a, b, (((1,), (1,)), ((), ())), preferred_element_type=F32)


def t_dot(a, b):
    return lax.dot_general(a, b, (((0,), (0,)), ((), ())), preferred_element_type=F32)


def inv_rms(x):
    return lax.rsqrt(jnp.mean(x * x, -1, keepdims=True) + EPS)


def norm_back(x, scale, grad):
    r = inv_rms(x)
    scaled = grad * scale
    lean = jnp.mean(scaled * x, -1, keepdims=True)
    return r * scaled - x * (r * r * r * lean), jnp.sum(grad * x * r, 0)


def takes(us):
    return pl.CostEstimate(flops=int(us * 1e9), bytes_accessed=0, transcendentals=0)


class Net:
    def __init__(self, send_sems, recv_sems):
        self.send_sems, self.recv_sems, self.used = send_sems, recv_sems, 0

    def push(self, src, dst, to):
        copy = pltpu.make_async_remote_copy(
            src_ref=src,
            dst_ref=dst,
            send_sem=self.send_sems.at[self.used],
            recv_sem=self.recv_sems.at[self.used],
            device_id=to,
            device_id_type=MESH,
        )
        self.used += 1
        return copy


def greet(partners):
    barrier = pltpu.get_barrier_semaphore()
    for to in partners:
        pl.semaphore_signal(barrier, inc=1, device_id=to, device_id_type=MESH)
    pl.semaphore_wait(barrier, len(partners))


def flip(x, mask):
    for bit in (1, 2, 4):
        if mask & bit:
            x = x + bit - 2 * bit * ((x // bit) % 2)
    return x


def where_am_i():
    return lax.axis_index("ctx"), lax.axis_index("fsdp")


def gather_kernel(
    qkv, out, gain, tokens, cot, w_qkv, w_out, gains, rows, cot_one, cot_three, send_sems, recv_sems, own_sems
):
    ctx, z = where_am_i()
    net = Net(send_sems, recv_sems)
    greet([(ctx, flip(z, m)) for m in (1, 2, 3)] + [(flip(ctx, m), z) for m in (1, 2, 4)])
    shard = qkv.shape[0]
    qkv_cols, half_cols = QW + HD, QW // 2

    def cols_of(ref, stride, first, count):
        return lambda h: ref.at[:, pl.ds(pl.multiple_of(h * stride + first, 128), count)]

    groups = [
        (cols_of(qkv, qkv_cols, QW, HD), w_qkv, shard, QW, HD),
        (lambda h: gain, gains, 8, 0, 128),
        (cols_of(qkv, qkv_cols, 0, half_cols), w_qkv, shard, 0, half_cols),
        (cols_of(qkv, qkv_cols, half_cols, half_cols), w_qkv, shard, half_cols, half_cols),
        (cols_of(out, QW, 0, half_cols), w_out, shard, 0, half_cols),
        (cols_of(out, QW, half_cols, half_cols), w_out, shard, half_cols, half_cols),
    ]

    def at(group, source, first, count):
        src, ref, unit, col, cols = group
        start = pl.multiple_of(source * 4 * unit + first, 8 if unit == 8 else 16)
        return ref.at[pl.ds(start, count), pl.ds(col, cols)]

    lines, locals_, sent = [], [], []

    def push(src, dst, to):
        copy = net.push(src, dst, to)
        copy.start()
        sent.append(copy)
        return copy

    token_rows = tokens.shape[0]
    token_dst = rows.at[pl.ds(pl.multiple_of((z % 2) * token_rows, 16), token_rows)]
    for i, group in enumerate(groups):
        unit = group[2]
        dst = at(group, ctx, z * unit, unit)
        lines.append([push(group[0](flip(z, m) % 2), dst, (ctx, flip(z, m))) for m in (2, 3, 1)])
        local = pltpu.make_async_copy(group[0](z % 2), dst, own_sems.at[i])
        local.start()
        locals_.append(local)
        if i == 3:
            token_copy = push(tokens, token_dst, (ctx, flip(z, 1)))
            token_local = pltpu.make_async_copy(tokens, token_dst, own_sems.at[len(groups)])
            token_local.start()
    mate, beyond = (ctx, flip(z, 1)), (ctx, flip(z, 3))
    inner = (z == 1) | (z == 2)
    cot_mate = push(cot, cot_one, mate)
    cot_beyond = net.push(cot, cot_three, beyond)

    @pl.when(inner)
    def _():
        cot_beyond.start()

    by_x, by_y, last = {}, {}, []
    diag = {}
    x_dev, y_dev, sib = (flip(ctx, 2), z), (flip(ctx, 4), z), (flip(ctx, 1), z)

    def same(group, source, first, count, to):
        return push(at(group, source, first, count), at(group, source, first, count), to)

    def spread_own(i):
        group = groups[i]
        locals_[i].wait()
        for copy in lines[i]:
            copy.wait_recv()
        count = 4 * group[2]
        by_x[i] = same(group, ctx, 0, count, x_dev)
        by_y[i] = same(group, ctx, 0, count, y_dev)
        last.append(same(group, ctx, 0, count, sib))

    def spread_near(i):
        group = groups[i]
        count = 4 * group[2]
        by_x[i].wait_recv()
        top = same(group, flip(ctx, 2), 0, count // 2, y_dev)
        last.append(same(group, flip(ctx, 2), 0, count, sib))
        by_y[i].wait_recv()
        low = same(group, flip(ctx, 4), count // 2, count // 2, x_dev)
        last.append(same(group, flip(ctx, 4), 0, count, sib))
        diag[i] = (top, low)

    def spread_far(i):
        group = groups[i]
        count = 4 * group[2]
        for k in range(2):
            diag[i][k].wait_recv()
            last.append(same(group, flip(ctx, 6), k * count // 2, count // 2, sib))

    for i in range(len(groups) + 2):
        if i < len(groups):
            spread_own(i)
        if 0 <= i - 1 < len(groups):
            spread_near(i - 1)
        if 0 <= i - 2 < len(groups):
            spread_far(i - 2)
    token_local.wait()
    token_copy.wait_recv()
    cot_mate.wait_recv()

    @pl.when(inner)
    def _():
        cot_beyond.wait_recv()
        cot_beyond.wait_send()

    for copy in last:
        copy.wait_recv()
    for copy in sent:
        copy.wait_send()


def gather_weights(w_query, w_key, w_value, w_out, gain_attn, gain_ffn, tokens, cotangent):
    shard, width = w_query.shape
    z = lax.axis_index("fsdp")
    ctx_total = lax.axis_size("ctx")
    pieces = []
    for h in range(2):
        pieces += [w_query[:, h * QW : (h + 1) * QW], (w_key, w_value)[h]]
    qkv = jnp.concatenate(pieces, 1)
    out = w_out.T
    gain = jnp.stack([gain_attn, gain_ffn]).astype(F32)
    gain = jnp.pad(gain, ((0, 6), (0, 128 - shard)))
    if ctx_total != 8 or lax.axis_size("fsdp") != 4 or shard % 16:
        both = ("ctx", "fsdp")
        full = lax.all_gather(qkv, both, axis=0, tiled=True)
        full_out = lax.all_gather(out, both, axis=0, tiled=True)
        return (
            half(full, z % 2, 1),
            half(full_out, z % 2, 1),
            lax.all_gather(gain, both, axis=0, tiled=True),
            join(tokens, swap(tokens, "fsdp", 1), z % 2, 0),
            swap(cotangent, "fsdp", 1),
            swap(cotangent, "fsdp", 3),
        )
    devices = 4 * ctx_total
    w_qkv, w_o, gains, rows, cot_one, cot_three = pl.pallas_call(
        gather_kernel,
        out_shape=[
            jax.ShapeDtypeStruct((width, QW + HD), BF16),
            jax.ShapeDtypeStruct((width, QW), BF16),
            jax.ShapeDtypeStruct((8 * devices, 128), F32),
            jax.ShapeDtypeStruct((2 * tokens.shape[0], width), BF16),
            jax.ShapeDtypeStruct(tokens.shape, BF16),
            jax.ShapeDtypeStruct(tokens.shape, BF16),
        ],
        in_specs=[ANY] * 5,
        out_specs=[ANY] * 6,
        scratch_shapes=[
            pltpu.SemaphoreType.DMA((75,)),
            pltpu.SemaphoreType.DMA((75,)),
            pltpu.SemaphoreType.DMA((7,)),
        ],
        compiler_params=pltpu.CompilerParams(collective_id=0, has_side_effects=True),
        cost_estimate=takes(80),
        name="gather_weights",
    )(qkv, out, gain, tokens, cotangent)
    return w_qkv, w_o, gains, rows, cot_one, cot_three


def proj_kernel(shard, rows, gains, cosine, sine, w, normed, out, kv, scales):
    @pl.when(pl.program_id(0) == 0)
    def _():
        for i in range(gains.shape[0] // 8):
            scales[:, i * shard : (i + 1) * shard] = gains[8 * i : 8 * i + 8, :shard]
        x = rows[...].astype(F32)
        normed[...] = (x * inv_rms(x) * scales[0:1, :]).astype(BF16)

    value = dot(normed[...], w[...])
    front, back = value[:, : HD // 2], value[:, HD // 2 :]
    c, s = cosine[0], sine[0]

    def put(ref):
        ref[:, : HD // 2] = (front * c - back * s).astype(BF16)
        ref[:, HD // 2 :] = (back * c + front * s).astype(BF16)

    pl.when(pl.program_id(0) < HEADS)(lambda: put(out))
    pl.when(pl.program_id(0) == HEADS)(lambda: put(kv))


def project(rows, gains, shard, cosine, sine, w):
    count, width = rows.shape
    steps = HEADS + 1
    fixed = lambda i: (0, 0)
    table = pl.BlockSpec((1, count, HD // 2), lambda i: (i // HEADS, 0, 0))
    return pl.pallas_call(
        functools.partial(proj_kernel, shard),
        grid=(steps,),
        out_shape=[
            jax.ShapeDtypeStruct((count, width), BF16),
            jax.ShapeDtypeStruct((count, QW), BF16),
            jax.ShapeDtypeStruct((count, HD), BF16),
            jax.ShapeDtypeStruct((8, width), F32),
        ],
        in_specs=[
            pl.BlockSpec((count, width), fixed),
            pl.BlockSpec(gains.shape, fixed),
            table,
            table,
            pl.BlockSpec((width, HD), lambda i: (0, i)),
        ],
        out_specs=[
            pl.BlockSpec((count, width), fixed),
            pl.BlockSpec((count, HD), lambda i: (0, jnp.minimum(i, HEADS - 1))),
            pl.BlockSpec((count, HD), fixed),
            pl.BlockSpec((8, width), fixed),
        ],
        compiler_params=pltpu.CompilerParams(vmem_limit_bytes=VMEM_LIMIT),
        cost_estimate=takes(10),
        name="project",
    )(rows, gains, cosine, sine, w)


def kv_gather_kernel(kv, store, send_sems, recv_sems, own_sem):
    ctx, z = where_am_i()
    net = Net(send_sems, recv_sems)
    h, pair = z % 2, z // 2
    greet([(ctx, flip(z, m)) for m in (1, 2)] + [(flip(ctx, m), z) for m in (1, 2, 4)])
    local = pltpu.make_async_copy(kv, store.at[pair, ctx, h], own_sem)
    local.start()
    mate, across = (ctx, flip(z, 1)), (ctx, flip(z, 2))
    x_dev, y_dev, sib = (flip(ctx, 2), z), (flip(ctx, 4), z), (flip(ctx, 1), z)
    own = net.push(kv, store.at[pair, ctx, h], mate)
    own.start()
    low = net.push(kv, store.at[0, ctx, h], across)
    low_mate = net.push(store.at[0, ctx, h], store.at[0, ctx, h], mate)

    @pl.when(pair == 0)
    def _():
        low.start()

    local.wait()
    own.wait_recv()

    class Set:
        def __init__(self, which):
            def same(source, kind, to):
                if kind is None:
                    ref = store.at[which, source]
                else:
                    ref = store.at[which, source, kind]
                return net.push(ref, ref, to)

            self.near = [same(ctx, None, x_dev), same(ctx, None, y_dev), same(ctx, None, sib)]
            x_ctx, y_ctx, d_ctx = flip(ctx, 2), flip(ctx, 4), flip(ctx, 6)
            self.after_x = [same(x_ctx, 0, y_dev), same(x_ctx, None, sib)]
            self.after_y = [same(y_ctx, 1, x_dev), same(y_ctx, None, sib)]
            self.after_d = [same(d_ctx, 0, sib), same(d_ctx, 1, sib)]

        def first(self):
            for copy in self.near:
                copy.start()

        def second(self):
            self.near[0].wait_recv()
            for copy in self.after_x:
                copy.start()
            self.near[1].wait_recv()
            for copy in self.after_y:
                copy.start()

        def third(self):
            self.after_x[0].wait_recv()
            self.after_d[0].start()
            self.after_y[0].wait_recv()
            self.after_d[1].start()

        def finish(self):
            for copy in [self.near[2], self.after_x[1], self.after_y[1]] + self.after_d:
                copy.wait_recv()
            for copy in self.near + self.after_x + self.after_y + self.after_d:
                copy.wait_send()

    mine = Set(pair)
    lower = Set(0)
    mine.first()

    @pl.when(pair == 1)
    def _():
        low.wait_recv()
        low_mate.start()
        low_mate.wait_recv()
        lower.first()

    mine.second()

    @pl.when(pair == 1)
    def _():
        lower.second()

    mine.third()

    @pl.when(pair == 1)
    def _():
        lower.third()

    mine.finish()
    own.wait_send()

    @pl.when(pair == 1)
    def _():
        lower.finish()
        low_mate.wait_send()

    @pl.when(pair == 0)
    def _():
        low.wait_send()


def gather_kv(kv):
    ctx_total = lax.axis_size("ctx")
    rows = kv.shape[0]
    if ctx_total != 8 or lax.axis_size("fsdp") != 4:
        every = lax.all_gather(kv, ("fsdp", "ctx"), axis=0, tiled=False)
        every = every.reshape(2, 2, ctx_total, rows, HD).transpose(0, 2, 1, 3, 4)
        return every.reshape(2 * ctx_total, 2, rows, HD)
    store = pl.pallas_call(
        kv_gather_kernel,
        out_shape=jax.ShapeDtypeStruct((2, ctx_total, 2, rows, HD), BF16),
        in_specs=[ANY],
        out_specs=ANY,
        scratch_shapes=[
            pltpu.SemaphoreType.DMA((21,)),
            pltpu.SemaphoreType.DMA((21,)),
            pltpu.SemaphoreType.DMA,
        ],
        compiler_params=pltpu.CompilerParams(collective_id=1, has_side_effects=True),
        cost_estimate=takes(30),
        name="gather_kv",
    )(kv)
    return store.reshape(2 * ctx_total, 2, rows, HD)


def chunks(rows, reach):
    skip = (reach * rows - WIN) // 128 * 128
    parts, at = [], 0
    for r in range(reach + 1):
        begin = max(0, skip - r * rows)
        if begin < rows:
            parts.append((r, begin, at, rows - begin))
            at += rows - begin
    return parts, at


def attend_kernel(reach, place, lowest, q, *refs):
    keys, values = refs[: reach + 1], refs[reach + 1 : 2 * reach + 2]
    prob, out, scores = refs[2 * reach + 2 :]
    rows = q.shape[0]
    parts, total = chunks(rows, reach)
    low = lowest[:, :1]
    peak = None
    for r, begin, at, count in parts:
        s = dot_t(q[...], keys[r][0, 0, begin:, :])
        key_at = lax.broadcasted_iota(jnp.int32, (rows, count), 1) + (r * rows + begin)
        visible = key_at >= low
        if r == reach:
            query_at = lax.broadcasted_iota(jnp.int32, (rows, count), 0) + reach * rows
            visible = visible & (key_at <= query_at)
        s = jnp.where(visible, s, FAR)
        scores[:, at : at + count] = s
        top = jnp.max(s, -1, keepdims=True)
        peak = top if peak is None else jnp.maximum(peak, top)
    weight_sum = jnp.zeros_like(peak)
    for r, begin, at, count in parts:
        e = jnp.exp(scores[:, at : at + count] - peak)
        scores[:, at : at + count] = e
        weight_sum = weight_sum + jnp.sum(e, -1, keepdims=True)
    share = 1.0 / weight_sum
    mixed = jnp.zeros((rows, HD), F32)
    for r, begin, at, count in parts:
        p = (scores[:, at : at + count] * share).astype(BF16)
        prob[0, :, at : at + count] = p
        mixed = mixed + dot(p, values[r][0, 0, begin:, :])
    out[...] = mixed.astype(BF16)


def window_specs(rows, reach):
    def spec(r, kind):
        return pl.BlockSpec((1, 1, rows, HD), lambda i, place: (place[r], kind, 0, 0))

    return [spec(r, kind) for kind in range(2) for r in range(reach + 1)]


def attend(place, lowest, qkv, store, reach):
    rows = qkv.shape[0]
    total = chunks(rows, reach)[1]
    column = pl.BlockSpec((rows, HD), lambda i, place: (0, i))
    return pl.pallas_call(
        functools.partial(attend_kernel, reach),
        grid_spec=pltpu.PrefetchScalarGridSpec(
            num_scalar_prefetch=1,
            grid=(HEADS,),
            in_specs=[pl.BlockSpec((rows, 128), lambda i, place: (0, 0)), column]
            + window_specs(rows, reach),
            out_specs=[
                pl.BlockSpec((1, rows, total), lambda i, place: (i, 0, 0)),
                column,
            ],
            scratch_shapes=[pltpu.VMEM((rows, total), F32)],
        ),
        out_shape=[
            jax.ShapeDtypeStruct((HEADS, rows, total), BF16),
            jax.ShapeDtypeStruct((rows, QW), BF16),
        ],
        compiler_params=pltpu.CompilerParams(vmem_limit_bytes=VMEM_LIMIT),
        cost_estimate=takes(21),
        name="attend",
    )(place, lowest, qkv, *([store] * (2 * reach + 2)))


def attend_back_kernel(reach, place, goes, prob, q, branch, w_out, cosine, sine, *refs):
    keys, values = refs[: reach + 1], refs[reach + 1 : 2 * reach + 2]
    grad_q, store, grad_probs, sums, blocks, sems = refs[2 * reach + 2 :]
    rows = q.shape[0]
    parts, total = chunks(rows, reach)
    head = pl.program_id(0)

    @pl.when(head == 0)
    def _():
        sums[...] = jnp.zeros_like(sums)

    grad_rows = dot(branch[...], w_out[...]).astype(BF16)
    query_rows = q[...]
    lean = jnp.zeros((rows, 1), F32)
    for r, begin, at, count in parts:
        dp = dot_t(grad_rows, values[r][0, 0, begin:, :])
        p = prob[0, :, at : at + count]
        grad_probs[:, at : at + count] = dp
        lean = lean + jnp.sum(dp * p.astype(F32), -1, keepdims=True)
        sums[1, at : at + count, :] += t_dot(p, grad_rows)
    turned = jnp.zeros((rows, HD), F32)
    for r, begin, at, count in parts:
        p = prob[0, :, at : at + count].astype(F32)
        ds = (p * (grad_probs[:, at : at + count] - lean)).astype(BF16)
        turned = turned + dot(ds, keys[r][0, 0, begin:, :])
        sums[0, at : at + count, :] += t_dot(ds, query_rows)
    front, back = turned[:, : HD // 2], turned[:, HD // 2 :]
    c, s = cosine[0], sine[0]
    grad_q[:, : HD // 2] = (front * c + back * s).astype(BF16)
    grad_q[:, HD // 2 :] = (back * c - front * s).astype(BF16)

    @pl.when(head == pl.num_programs(0) - 1)
    def _():
        blocks[reach + 1] = jnp.zeros((2, rows, HD), BF16)
        for r, begin, at, count in parts:
            for kind in range(2):
                if begin > 0:
                    blocks[r, kind, :begin, :] = jnp.zeros((begin, HD), BF16)
                blocks[r, kind, begin:, :] = sums[kind, at : at + count, :].astype(BF16)
        for r in range(parts[0][0]):
            blocks[r] = jnp.zeros((2, rows, HD), BF16)
        count = store.shape[0]

        def copy(i):
            return pltpu.make_async_copy(blocks.at[goes[i]], store.at[i], sems.at[i])

        for i in range(count):
            copy(i).start()
        for i in range(count):
            copy(i).wait()


def attend_back(place, goes, prob, qkv, branch, w_out, cosine, sine, store, reach):
    rows = qkv.shape[0]
    total = chunks(rows, reach)[1]
    column = pl.BlockSpec((rows, HD), lambda i, place, goes: (0, i))
    table = pl.BlockSpec((1, rows, HD // 2), lambda i, place, goes: (0, 0, 0))

    def spec(r, kind):
        return pl.BlockSpec((1, 1, rows, HD), lambda i, place, goes: (place[r], kind, 0, 0))

    return pl.pallas_call(
        functools.partial(attend_back_kernel, reach),
        grid_spec=pltpu.PrefetchScalarGridSpec(
            num_scalar_prefetch=2,
            grid=(HEADS,),
            in_specs=[
                pl.BlockSpec((1, rows, total), lambda i, place, goes: (i, 0, 0)),
                column,
                pl.BlockSpec(branch.shape, lambda i, place, goes: (0, 0)),
                pl.BlockSpec((w_out.shape[0], HD), lambda i, place, goes: (0, i)),
                table,
                table,
            ]
            + [spec(r, kind) for kind in range(2) for r in range(reach + 1)],
            out_specs=[column, ANY],
            scratch_shapes=[
                pltpu.VMEM((rows, total), F32),
                pltpu.VMEM((2, total, HD), F32),
                pltpu.VMEM((reach + 2, 2, rows, HD), BF16),
                pltpu.SemaphoreType.DMA((store.shape[0],)),
            ],
        ),
        out_shape=[
            jax.ShapeDtypeStruct((rows, QW), BF16),
            jax.ShapeDtypeStruct(store.shape, BF16),
        ],
        compiler_params=pltpu.CompilerParams(vmem_limit_bytes=VMEM_LIMIT),
        cost_estimate=takes(24),
        name="attend_back",
    )(place, goes, prob, qkv, branch, w_out, cosine, sine, *([store] * (2 * reach + 2)))


def out_norm_kernel(
    attended, tokens, scale, w_out, middle, own_rows, mate_rows, beyond_rows, wo, other, got, mine, send_sems, recv_sems, own_sems
):
    ctx, z = where_am_i()
    h = z % 2
    net = Net(send_sems, recv_sems)
    mate, beyond = (ctx, flip(z, 1)), (ctx, flip(z, 3))
    own, width = tokens.shape
    step = 512
    steps = width // step
    loads = []
    for k in range(steps):
        part = pl.ds(k * step, step)
        loads.append(pltpu.make_async_copy(w_out.at[part], wo.at[part], own_sems.at[k]))
        loads[k].start()
    greet([mate, beyond])
    keep = attended[pl.ds(pl.multiple_of(h * own, 16), own), :]
    give = attended[pl.ds(pl.multiple_of((1 - h) * own, 16), own), :]
    crossing = []
    for k in range(steps):
        part = pl.ds(k * step, step)
        loads[k].wait()
        other[k] = dot_t(give, wo[part, :]).astype(BF16)
        crossing.append(net.push(other.at[k], got.at[k], mate))
        crossing[k].start()
    for k in range(steps):
        part = pl.ds(k * step, step)
        middle[:, part] = tokens[:, part].astype(F32) + dot_t(keep, wo[part, :])
    square = jnp.zeros((own, 1), F32)
    for k in range(steps):
        part = pl.ds(k * step, step)
        crossing[k].wait_recv()
        value = middle[:, part] + got[k].astype(F32)
        middle[:, part] = value
        square = square + jnp.sum(value * value, -1, keepdims=True)
    r = lax.rsqrt(square / width + EPS)
    for k in range(steps):
        part = pl.ds(k * step, step)
        mine[:, part] = (middle[:, part] * r * scale[1:2, part]).astype(BF16)
    to_mate = net.push(mine, mate_rows, mate)
    to_beyond = net.push(mine, beyond_rows, beyond)
    to_mate.start()
    inner = (z == 1) | (z == 2)
    pl.when(inner)(to_beyond.start)
    local = pltpu.make_async_copy(mine, own_rows, own_sems.at[steps])
    local.start()
    for k in range(steps):
        crossing[k].wait_send()
    local.wait()
    to_mate.wait()
    pl.when(inner)(to_beyond.wait)


def out_norm(attended, tokens, scale, w_out):
    own, width = tokens.shape
    line = jax.ShapeDtypeStruct((own, width), BF16)
    return pl.pallas_call(
        out_norm_kernel,
        out_shape=[jax.ShapeDtypeStruct((own, width), F32), line, line, line],
        in_specs=[VMEM] * 3 + [ANY],
        out_specs=[VMEM] + [ANY] * 3,
        scratch_shapes=[
            pltpu.VMEM(w_out.shape, BF16),
            pltpu.VMEM((width // 512, own, 512), BF16),
            pltpu.VMEM((width // 512, own, 512), BF16),
            pltpu.VMEM((own, width), BF16),
            pltpu.SemaphoreType.DMA((width // 512 + 2,)),
            pltpu.SemaphoreType.DMA((width // 512 + 2,)),
            pltpu.SemaphoreType.DMA((width // 512 + 1,)),
        ],
        compiler_params=pltpu.CompilerParams(
            collective_id=3, has_side_effects=True, vmem_limit_bytes=VMEM_LIMIT
        ),
        cost_estimate=takes(55),
        name="out_norm",
    )(attended, tokens, scale, w_out)


def ffn_kernel(
    own_rows,
    mate_rows,
    beyond_rows,
    gate_up_w,
    rows_out,
    hidden_out,
    active_out,
    sloped_out,
    wg,
    wu,
    x,
    hidden,
    active,
    sloped,
    send_sems,
    recv_sems,
    own_sems,
    out_sems,
):
    ctx, z = where_am_i()
    net = Net(send_sems, recv_sems)
    mate, beyond = (ctx, flip(z, 1)), (ctx, flip(z, 3))
    own, width = own_rows.shape
    units = wg.shape[1]
    spans = [pl.ds(c, min(512, units - c)) for c in range(0, units, 512)]
    count = len(spans)
    inner = (z == 1) | (z == 2)
    pulls = []
    for m, src in ((0, own_rows), (1, mate_rows)):
        pulls.append(
            pltpu.make_async_copy(src, x.at[pl.ds(m * own, own)], own_sems.at[2 * count + m])
        )
        pulls[m].start()
    loads = []
    for c in range(count):
        span = spans[c]
        pair = []
        for k, dst in enumerate((wg, wu)):
            src = gate_up_w.at[:, pl.ds(k * units + span.start, span.size)]
            pair.append(pltpu.make_async_copy(src, dst.at[:, span], own_sems.at[2 * c + k]))
            pair[k].start()
        loads.append(pair)
    greet([mate, beyond])
    one_beyond = net.push(mate_rows, x.at[pl.ds(2 * own, own)], beyond)
    three_mate = net.push(beyond_rows, x.at[pl.ds(2 * own, own)], mate)
    two_mate = net.push(x.at[pl.ds(2 * own, own)], x.at[pl.ds(3 * own, own)], mate)
    three_local = pltpu.make_async_copy(
        beyond_rows, x.at[pl.ds(3 * own, own)], own_sems.at[2 * count + 2]
    )

    @pl.when(inner)
    def _():
        one_beyond.start()
        three_mate.start()
        three_local.start()

    def work(first, rows, c, ready):
        if ready is not None:
            for copy in ready:
                copy.wait()
        span = spans[c]
        at = pl.ds(first, rows)
        gate = dot(x[at, :], wg[:, span])
        up = dot(x[at, :], wu[:, span])
        root, cubic = 0.7978845608028654, 0.044715
        square = gate * gate
        bent = jnp.tanh(root * (gate + cubic * square * gate))
        value = 0.5 * gate * (1.0 + bent)
        slope = 0.5 * (1.0 + bent) + 0.5 * gate * (1.0 - bent * bent) * root * (
            1.0 + 3.0 * cubic * square
        )
        hidden[at, span] = (value * up).astype(BF16)
        active[at, span] = value.astype(BF16)
        sloped[at, span] = (slope * up).astype(BF16)

    outs = []

    def flush(m):
        at = pl.ds(m * own, own)
        pairs = ((hidden, hidden_out), (active, active_out), (sloped, sloped_out), (x, rows_out))
        for k, (src, dst) in enumerate(pairs):
            copy = pltpu.make_async_copy(src.at[at], dst.at[at], out_sems.at[4 * m + k])
            copy.start()
            outs.append(copy)

    for copy in pulls:
        copy.wait()
    for c in range(count):
        work(0, 2 * own, c, loads[c])
    flush(0)
    flush(1)

    @pl.when(inner)
    def _():
        one_beyond.wait_recv()
        two_mate.start()

    @pl.when(jnp.logical_not(inner))
    def _():
        three_mate.wait_recv()

    for c in range(count):
        work(2 * own, own, c, None)
    flush(2)

    @pl.when(inner)
    def _():
        three_local.wait()

    @pl.when(jnp.logical_not(inner))
    def _():
        two_mate.wait_recv()

    for c in range(count):
        work(3 * own, own, c, None)
    flush(3)

    @pl.when(inner)
    def _():
        for copy in (one_beyond, three_mate, two_mate):
            copy.wait_send()

    for copy in outs:
        copy.wait()


def feed_forward(own_rows, mate_rows, beyond_rows, gate_up_w):
    own, width = own_rows.shape
    units = gate_up_w.shape[1] // 2
    count = 4 * own
    inner_shape = jax.ShapeDtypeStruct((count, units), BF16)
    return pl.pallas_call(
        ffn_kernel,
        out_shape=[jax.ShapeDtypeStruct((count, width), BF16)] + [inner_shape] * 3,
        in_specs=[ANY] * 4,
        out_specs=[ANY] * 4,
        scratch_shapes=[
            pltpu.VMEM((width, units), BF16),
            pltpu.VMEM((width, units), BF16),
            pltpu.VMEM((count, width), BF16),
            pltpu.VMEM((count, units), BF16),
            pltpu.VMEM((count, units), BF16),
            pltpu.VMEM((count, units), BF16),
            pltpu.SemaphoreType.DMA((3,)),
            pltpu.SemaphoreType.DMA((3,)),
            pltpu.SemaphoreType.DMA((2 * (-(-units // 512)) + 3,)),
            pltpu.SemaphoreType.DMA((16,)),
        ],
        compiler_params=pltpu.CompilerParams(
            collective_id=6, has_side_effects=True, vmem_limit_bytes=VMEM_LIMIT
        ),
        cost_estimate=takes(52),
        name="feed_forward",
    )(own_rows, mate_rows, beyond_rows, gate_up_w)


def ffn_grad_kernel(c0, c1, c2, c3, down_w, active, sloped, cot, grad_gate, grad_up):
    own = c0.shape[0]

    @pl.when(pl.program_id(0) == 0)
    def _():
        for m, piece in enumerate((c0, c1, c2, c3)):
            cot[m * own : (m + 1) * own, :] = piece[...]

    grad = dot(cot[...], down_w[...])
    grad_gate[...] = (sloped[...].astype(F32) * grad).astype(BF16)
    grad_up[...] = (active[...].astype(F32) * grad).astype(BF16)


def ffn_specs(count, width, units):
    step = 512
    whole = pl.BlockSpec((count, width), lambda i: (0, 0))
    weight = pl.BlockSpec((width, step), lambda i: (0, i))
    column = pl.BlockSpec((count, step), lambda i: (0, i))
    return -(-units // step), whole, weight, column


def feed_forward_grad(cots, down_w, active, sloped):
    own, width = cots[0].shape
    count, units = active.shape
    steps, whole, weight, column = ffn_specs(count, width, units)
    piece = pl.BlockSpec((own, width), lambda i: (0, 0))
    return pl.pallas_call(
        ffn_grad_kernel,
        grid=(steps,),
        out_shape=[jax.ShapeDtypeStruct((count, width), BF16)]
        + [jax.ShapeDtypeStruct((count, units), BF16)] * 2,
        in_specs=[piece] * 4 + [weight, column, column],
        out_specs=[whole, column, column],
        compiler_params=pltpu.CompilerParams(vmem_limit_bytes=VMEM_LIMIT),
        cost_estimate=takes(15),
        name="feed_forward_grad",
    )(*cots, down_w, active, sloped)


def ffn_back_kernel(
    grad_gate,
    grad_up,
    gate_up_w,
    down_w,
    hidden,
    rows_in,
    middle,
    cot,
    scale,
    grad_w,
    gate_sum_out,
    ffn_near,
    ffn_far,
    grad_middle,
    branch,
    grad_scale,
    gg,
    gu,
    wg,
    wu,
    x,
    parts,
    got,
    stage,
    mine,
    blocks,
    got_diag,
    got_x,
    got_y,
    send_sems,
    recv_sems,
    own_sems,
    stage_sems,
    give_sems,
    take_sems,
    sum_sems,
):
    ctx, z = where_am_i()
    net = Net(send_sems, recv_sems)
    mate, beyond = (ctx, flip(z, 1)), (ctx, flip(z, 3))
    x_dev, y_dev = (flip(ctx, 2), z), (flip(ctx, 4), z)
    inside_sum = lax.axis_size("ctx") == 8
    greet([mate, beyond, (flip(ctx, 1), z)] + ([x_dev, y_dev] if inside_sum else []))
    inner = (z == 1) | (z == 2)
    own, width = middle.shape
    units = gg.shape[1]
    step = 512
    steps = width // step
    order = (3, 2, 1, 0)
    loads = {}
    used = 0

    def load(name, src, dst):
        nonlocal used
        loads[name] = pltpu.make_async_copy(src, dst, own_sems.at[used])
        loads[name].start()
        used += 1

    for k in range(steps):
        if k < 4:
            m = order[k]
            span = pl.ds(m * own, own)
            load(("gg", m), grad_gate.at[span], gg.at[span])
            load(("gu", m), grad_up.at[span], gu.at[span])
        part = pl.ds(k * step, step)
        load(("wg", k), gate_up_w.at[part, pl.ds(0, units)], wg.at[part])
        load(("wu", k), gate_up_w.at[part, pl.ds(units, units)], wu.at[part])
    load("x", rows_in, x)

    far = net.push(parts.at[3], got.at[0], mate)
    near = net.push(parts.at[2], got.at[1], mate)
    two_over = net.push(parts.at[2], got.at[2], beyond)
    three_over = net.push(parts.at[3], got.at[3], beyond)
    one_mate = net.push(parts.at[1], got.at[4], mate)

    def make(m):
        span = pl.ds(m * own, own)
        loads["gg", m].wait()
        loads["gu", m].wait()
        for k in range(steps):
            part = pl.ds(k * step, step)
            if m == 3:
                loads["wg", k].wait()
                loads["wu", k].wait()
            value = dot_t(gg[span, :], wg[part, :]) + dot_t(gu[span, :], wu[part, :])
            parts[m, :, part] = value.astype(BF16)

    def add_to(m, k):
        parts[m] = (parts[m].astype(F32) + got[k].astype(F32)).astype(BF16)

    make(3)
    pl.when(jnp.logical_not(inner))(far.start)
    make(2)
    pl.when(jnp.logical_not(inner))(near.start)
    make(1)
    make(0)
    load("wd", down_w, wg)
    loads["x"].wait()

    block = 2 * width // lax.axis_size("ctx")
    chips = width // block
    chunk, col_step = stage.shape[1], stage.shape[2]
    sib = (flip(ctx, 1), z)
    core = ctx % 2
    side = block // 2
    slices = units // col_step
    inside = chunk // block
    rounds = width // chunk * slices

    def chip_copies(which, i):
        n = i % slices
        cols = pl.ds(pl.multiple_of(n * col_step, 128), col_step)
        keeps, gives = [], []
        for part in range(inside):
            k = i // slices * inside + part
            sem = (which * chips + k) * slices + n
            rows = pl.ds(pl.multiple_of((which * chips + k) * side, 16), side)
            mine_at = pl.ds(pl.multiple_of(part * block + core * side, 16), side)
            give_at = pl.ds(pl.multiple_of(part * block + (1 - core) * side, 16), side)
            keeps.append(
                pltpu.make_async_copy(
                    stage.at[i % 2, mine_at], wu.at[rows, cols], stage_sems.at[sem]
                )
            )
            gives.append(
                pltpu.make_async_remote_copy(
                    src_ref=stage.at[i % 2, give_at],
                    dst_ref=blocks.at[rows, cols],
                    send_sem=give_sems.at[sem],
                    recv_sem=take_sems.at[sem],
                    device_id=sib,
                    device_id_type=MESH,
                )
            )
        return keeps, gives

    def weight_grad(g, which):
        def done(i):
            keeps, gives = chip_copies(which, i)
            for copy in keeps:
                copy.wait()
            for copy in gives:
                copy.wait_send()

        def body(i, carry):
            pl.when(i >= 2)(lambda: done(i - 2))
            rows = pl.ds(pl.multiple_of(i // slices * chunk, 128), chunk)
            cols = pl.ds(pl.multiple_of(i % slices * col_step, 128), col_step)
            stage[i % 2] = t_dot(x[:, rows], g[:, cols]).astype(BF16)
            keeps, gives = chip_copies(which, i)
            for copy in keeps + gives:
                copy.start()
            return carry

        lax.fori_loop(0, rounds, body, 0)
        done(rounds - 2)
        done(rounds - 1)

    def add_cores(which):
        first = which * chips * side

        def arrived(i, carry):
            for copy in chip_copies(which, i)[1]:
                copy.wait_recv()
            return carry

        lax.fori_loop(0, rounds, arrived, 0)
        unit = 16

        def body(i, carry):
            at = pl.ds(pl.multiple_of(first + i * unit, unit), unit)
            wu[at, :] = (wu[at, :].astype(F32) + blocks[at, :].astype(F32)).astype(BF16)
            return carry

        lax.fori_loop(0, chips * side // unit, body, 0)
        if inside_sum and which == 0:
            return None
        first_col = 0 if inside_sum else which * units
        copy = pltpu.make_async_copy(
            wu.at[pl.ds(first, chips * side)],
            grad_w.at[:, pl.ds(first_col, units)],
            sum_sems.at[which],
        )
        copy.start()
        return copy

    chip_copies_of_gate = []

    def gate_block(m, first, count):
        start = flip(ctx // 2, m) * side + first
        return wu.at[pl.ds(pl.multiple_of(start, 16), count)]

    def gate_diag():
        for k, to in enumerate((y_dev, x_dev)):
            copy = net.push(
                gate_block(3, k * side // 2, side // 2),
                got_diag.at[pl.ds(k * side // 2, side // 2)],
                to,
            )
            copy.start()
            chip_copies_of_gate.append(copy)

    def rows_loop(count, one):
        unit = 16

        def body(i, carry):
            one(i * unit, unit)
            return carry

        lax.fori_loop(0, count // unit, body, 0)

    def gate_near():
        for k, (to, got_from) in enumerate(((x_dev, got_x), (y_dev, got_y))):
            chip_copies_of_gate[k].wait_recv()
            start = flip(ctx // 2, 1 + k) * side + k * side // 2

            def one(first, unit):
                at = pl.ds(pl.multiple_of(start + first, unit), unit)
                other = got_diag[pl.ds(pl.multiple_of(k * side // 2 + first, unit), unit), :]
                wu[at, :] = (wu[at, :].astype(F32) + other.astype(F32)).astype(BF16)

            rows_loop(side // 2, one)
            copy = net.push(gate_block(1 + k, 0, side), got_from, to)
            copy.start()
            chip_copies_of_gate.append(copy)

    def gate_total():
        for copy in chip_copies_of_gate[2:]:
            copy.wait_recv()

        def one(first, unit):
            at = pl.ds(pl.multiple_of(first, unit), unit)
            own_at = pl.ds(pl.multiple_of(ctx // 2 * side + first, unit), unit)
            value = wu[own_at, :].astype(F32) + got_x[at, :].astype(F32)
            got_diag[at, :] = (value + got_y[at, :].astype(F32)).astype(BF16)

        rows_loop(side, one)
        copy = pltpu.make_async_copy(got_diag, gate_sum_out, sum_sems.at[0])
        copy.start()
        for other in chip_copies_of_gate:
            other.wait_send()
        copy.wait()

    @pl.when(inner)
    def _():
        far.wait_recv()
        add_to(2, 0)
        two_over.start()

    weight_grad(gg, 0)

    @pl.when(inner)
    def _():
        near.wait_recv()
        add_to(3, 1)
        three_over.start()
        two_over.wait_recv()
        add_to(1, 2)

    one_mate.start()
    gate_sum = add_cores(0)
    if inside_sum:
        gate_diag()
    weight_grad(gu, 1)
    if inside_sum:
        gate_near()
    load("hidden", hidden, gu)
    load("cot", cot, x.at[pl.ds(0, own)])
    up_sum = add_cores(1)
    one_mate.wait_recv()
    pl.when(inner)(three_over.wait_recv)
    loads["cot"].wait()

    def norm_rows(i, scale_sum):
        at = pl.ds(pl.multiple_of(i * 16, 16), 16)
        grad = parts[0, at, :].astype(F32) + got[4, at, :].astype(F32)
        grad = grad + jnp.where(inner, got[3, at, :].astype(F32), 0.0)
        value = middle[at, :]
        r = inv_rms(value)
        scaled = grad * scale[1:2, :]
        lean = jnp.mean(scaled * value, -1, keepdims=True)
        total = x[at, :].astype(F32) + (r * scaled - value * (r * r * r * lean))
        grad_middle[at, :] = total
        mine[at, :] = total.astype(BF16)
        return scale_sum + jnp.sum(grad * value * r, 0, keepdims=True)

    grad_scale[...] = lax.fori_loop(0, own // 16, norm_rows, jnp.zeros((1, width), F32))
    dst = branch.at[pl.ds(pl.multiple_of((z % 2) * own, 16), own)]
    last = net.push(mine, dst, mate)
    last.start()
    local = pltpu.make_async_copy(mine, dst, own_sems.at[used])
    local.start()
    one_mate.wait_send()

    @pl.when(inner)
    def _():
        two_over.wait_send()
        three_over.wait_send()

    @pl.when(jnp.logical_not(inner))
    def _():
        far.wait_send()
        near.wait_send()

    loads["wd"].wait()
    loads["hidden"].wait()
    out_copies = []
    for m in order:
        span = pl.ds(m * own, own)
        for k in range(steps):
            part = pl.ds(k * step, step)
            parts[m, :, part] = dot_t(gu[span, :], wg[part, :]).astype(BF16)
        dst = ffn_near.at[m] if m < 2 else ffn_far.at[m - 2]
        copy = pltpu.make_async_copy(parts.at[m], dst, own_sems.at[used + 1 + m])
        copy.start()
        out_copies.append(copy)
    local.wait()
    if inside_sum:
        gate_total()
    else:
        gate_sum.wait()
    up_sum.wait()
    last.wait_recv()
    last.wait_send()
    for copy in out_copies:
        copy.wait()


def feed_forward_back(grad_gate, grad_up, gate_up_w, down_w, hidden, rows_in, middle, cot, scale):
    own, width = middle.shape
    count, units = hidden.shape
    block = 2 * width // lax.axis_size("ctx")
    chunk = block if block % 128 == 0 else 640
    inside_sum = lax.axis_size("ctx") == 8
    rounds = width // block * (units // 640)
    return pl.pallas_call(
        ffn_back_kernel,
        out_shape=[
            jax.ShapeDtypeStruct((width // 2, units if inside_sum else 2 * units), BF16),
            jax.ShapeDtypeStruct((block // 2, units), BF16),
            jax.ShapeDtypeStruct((2, own, width), BF16),
            jax.ShapeDtypeStruct((2, own, width), BF16),
            jax.ShapeDtypeStruct((own, width), F32),
            jax.ShapeDtypeStruct((2 * own, width), BF16),
            jax.ShapeDtypeStruct((1, width), F32),
        ],
        in_specs=[ANY] * 6 + [VMEM, ANY, VMEM],
        out_specs=[ANY, ANY, ANY, ANY, VMEM, ANY, VMEM],
        scratch_shapes=[
            pltpu.VMEM((count, units), BF16),
            pltpu.VMEM((count, units), BF16),
            pltpu.VMEM((width, units), BF16),
            pltpu.VMEM((width, units), BF16),
            pltpu.VMEM((count, width), BF16),
            pltpu.VMEM((4, own, width), BF16),
            pltpu.VMEM((5, own, width), BF16),
            pltpu.VMEM((2, chunk, 640), BF16),
            pltpu.VMEM((own, width), BF16),
            pltpu.VMEM((width, units), BF16),
            pltpu.VMEM((block // 2, units), BF16),
            pltpu.VMEM((block // 2, units), BF16),
            pltpu.VMEM((block // 2, units), BF16),
            pltpu.SemaphoreType.DMA((10,)),
            pltpu.SemaphoreType.DMA((10,)),
            pltpu.SemaphoreType.DMA((8 + 2 * (width // 512) + 9,)),
            pltpu.SemaphoreType.DMA((2 * rounds,)),
            pltpu.SemaphoreType.DMA((2 * rounds,)),
            pltpu.SemaphoreType.DMA((2 * rounds,)),
            pltpu.SemaphoreType.DMA((2,)),
        ],
        compiler_params=pltpu.CompilerParams(
            collective_id=5, has_side_effects=True, vmem_limit_bytes=62 * 1024 * 1024
        ),
        cost_estimate=takes(100),
        name="feed_forward_back",
    )(grad_gate, grad_up, gate_up_w, down_w, hidden, rows_in, middle, cot, scale)


def fold(ref, other):
    ref[...] = (ref[...].astype(F32) + other[...].astype(F32)).astype(BF16)


class KvSum:
    def __init__(self, net, parts, out, mine, got_sib, got_diag, got_x, got_y, got_z, give, sems):
        ctx, z = where_am_i()
        self.h, self.upper = z % 2, z // 2 == 1
        self.refs = (out, mine, got_sib, got_diag, got_x, got_y, got_z, give)
        x_dev, y_dev, sib = (flip(ctx, 2), z), (flip(ctx, 4), z), (flip(ctx, 1), z)
        self.load, self.over, self.diag, self.near = {}, {}, {}, {}
        for s in range(2):
            for i, m in enumerate((6, 2, 4, 0)):
                self.load[s, i] = pltpu.make_async_copy(
                    parts.at[s, flip(ctx, m)], mine.at[s, i], sems.at[4 * s + i]
                )
                self.over[s, i] = net.push(
                    parts.at[s, flip(flip(ctx, 1), m)], got_sib.at[s, i], sib
                )
            self.diag[s] = [
                net.push(mine.at[s, 0, 0], got_diag.at[s, 0], y_dev),
                net.push(mine.at[s, 0, 1], got_diag.at[s, 1], x_dev),
            ]
            self.near[s] = [
                net.push(mine.at[s, 1], got_x.at[s], x_dev),
                net.push(mine.at[s, 2], got_y.at[s], y_dev),
            ]
        self.to_mate = net.push(give.at[0], got_z.at[0], (ctx, flip(z, 1)))
        self.to_low = net.push(give.at[1], got_z.at[1], (ctx, flip(z, 2)))
        self.to_low_mate = net.push(give.at[2], got_z.at[2], (ctx, flip(z, 3)))

    def both(self, stage):
        stage(0)
        pl.when(self.upper)(lambda: stage(1))

    def start(self, s):
        for i in range(4):
            self.over[s, i].start()
            self.load[s, i].start()

    def chip_sums(self, s):
        mine, got_sib = self.refs[1:3]
        for i in range(4):
            self.load[s, i].wait()
            self.over[s, i].wait_recv()
            fold(mine.at[s, i], got_sib.at[s, i])
            if i == 0:
                for copy in self.diag[s]:
                    copy.start()

    def forward(self, s):
        mine, got_diag = self.refs[1], self.refs[3]
        for k in range(2):
            self.diag[s][k].wait_recv()
            fold(mine.at[s, 1 + k, k], got_diag.at[s, k])
            self.near[s][k].start()

    def total(self, s, kind):
        mine, got_x, got_y = self.refs[1], self.refs[4], self.refs[5]
        value = mine[s, 3, kind].astype(F32) + got_x[s, kind].astype(F32)
        return value + got_y[s, kind].astype(F32)

    def across(self):
        out, give, h = self.refs[0], self.refs[7], self.h
        for copy in self.near[0]:
            copy.wait_recv()

        @pl.when(jnp.logical_not(self.upper))
        def _():
            give[0] = self.total(0, 1 - h).astype(BF16)
            out[...] = self.total(0, h)

        @pl.when(self.upper)
        def _():
            give[1] = self.total(0, h).astype(BF16)
            give[2] = self.total(0, 1 - h).astype(BF16)
            self.to_low.start()
            self.to_low_mate.start()
            for copy in self.near[1]:
                copy.wait_recv()
            give[0] = self.total(1, 1 - h).astype(BF16)
            out[...] = self.total(1, h)

        self.to_mate.start()

    def finish(self):
        out, got_z = self.refs[0], self.refs[6]
        self.to_mate.wait_recv()
        out[...] += got_z[0].astype(F32)

        @pl.when(jnp.logical_not(self.upper))
        def _():
            self.to_low.wait_recv()
            self.to_low_mate.wait_recv()
            out[...] += got_z[1].astype(F32) + got_z[2].astype(F32)

        def sent(s):
            for i in range(4):
                self.over[s, i].wait_send()
            for copy in self.diag[s] + self.near[s]:
                copy.wait_send()

        self.both(sent)
        self.to_mate.wait_send()

        @pl.when(self.upper)
        def _():
            self.to_low.wait_send()
            self.to_low_mate.wait_send()

    @staticmethod
    def scratch(rows):
        block = (2, rows, HD)
        return [
            pltpu.VMEM((2, 4) + block, BF16),
            pltpu.VMEM((2, 4) + block, BF16),
            pltpu.VMEM((2, 2, rows, HD), BF16),
            pltpu.VMEM((2,) + block, BF16),
            pltpu.VMEM((2,) + block, BF16),
            pltpu.VMEM((3, rows, HD), BF16),
            pltpu.VMEM((3, rows, HD), BF16),
            pltpu.SemaphoreType.DMA((8,)),
        ]

    copies = 19


class WeightSum:
    def __init__(self, net, widths, parts, put, mine, got_sib, got_diag, got_x, got_y, got_z, total, sems):
        ctx, z = where_am_i()
        self.net, self.z = net, z
        self.ctx = ctx
        self.parts, self.put, self.sems = parts, put, sems
        self.refs = (mine, got_sib, got_diag, got_x, got_y, got_z, total)
        self.x_dev, self.y_dev, self.sib = (flip(ctx, 2), z), (flip(ctx, 4), z), (flip(ctx, 1), z)
        self.rows = mine.shape[1]
        self.copies = {}
        self.spans, col = [], 0
        for count in widths:
            self.spans.append(pl.ds(col, count))
            col += count

    def add_to(self, ref, other, count):
        step = 32

        def body(i, carry):
            at = pl.ds(pl.multiple_of(i * step, step), step)
            ref[at, :] = (ref[at, :].astype(F32) + other[at, :].astype(F32)).astype(BF16)
            return carry

        lax.fori_loop(0, count // step, body, 0)

    def start(self, g):
        mine, got_sib = self.refs[:2]
        span, rows, ctx = self.spans[g], self.rows, self.ctx

        def block_rows(source):
            return pl.ds(pl.multiple_of(source * rows, 16), rows)

        for i, m in enumerate((6, 2, 4, 0)):
            load = pltpu.make_async_copy(
                self.parts.at[block_rows(flip(ctx, m)), span],
                mine.at[i, :, span],
                self.sems.at[4 * g + i],
            )
            over = self.net.push(
                self.parts.at[block_rows(flip(flip(ctx, 1), m)), span],
                got_sib.at[i, :, span],
                self.sib,
            )
            load.start()
            over.start()
            self.copies[g, i] = (load, over)

    def chip_sums(self, g):
        mine, got_sib, got_diag = self.refs[:3]
        span, rows = self.spans[g], self.rows
        cut = rows // 2
        for i in range(4):
            load, over = self.copies[g, i]
            if load is not None:
                load.wait()
            over.wait_recv()
            self.add_to(mine.at[i, :, span], got_sib.at[i, :, span], rows)
            if i == 0:
                pair = []
                for k, to in enumerate((self.y_dev, self.x_dev)):
                    part = pl.ds(k * cut, cut)
                    pair.append(self.net.push(mine.at[0, part, span], got_diag.at[part, span], to))
                    pair[k].start()
                self.copies[g, "diag"] = pair

    def forward(self, g):
        mine, _, got_diag, got_x, got_y = self.refs[:5]
        span = self.spans[g]
        cut = self.rows // 2
        pair = []
        for k, (got, to) in enumerate(((got_x, self.x_dev), (got_y, self.y_dev))):
            part = pl.ds(k * cut, cut)
            self.copies[g, "diag"][k].wait_recv()
            self.add_to(mine.at[1 + k, part, span], got_diag.at[part, span], cut)
            pair.append(self.net.push(mine.at[1 + k, :, span], got.at[:, span], to))
            pair[k].start()
        self.copies[g, "near"] = pair

    def line(self, g):
        mine, _, _, got_x, got_y, got_z, total = self.refs
        span, rows, z = self.spans[g], self.rows, self.z
        unit = rows // 4
        for copy in self.copies[g, "near"]:
            copy.wait_recv()
        step = 16

        def body(i, carry):
            at = pl.ds(pl.multiple_of(i * step, step), step)
            value = mine[3, at, span].astype(F32) + got_x[at, span].astype(F32)
            total[at, span] = (value + got_y[at, span].astype(F32)).astype(BF16)
            return carry

        lax.fori_loop(0, rows // step, body, 0)
        sends = []
        for k, m in enumerate((1, 2, 3)):
            start_row = pl.multiple_of(flip(z, m) * unit, 16)
            copy = self.net.push(
                total.at[pl.ds(start_row, unit), span],
                got_z.at[k, :, span],
                (self.ctx, flip(z, m)),
            )
            copy.start()
            sends.append(copy)
        self.copies[g, "line"] = sends

    def finish(self, g):
        got_z, total = self.refs[5:]
        span, unit = self.spans[g], self.rows // 4
        for copy in self.copies[g, "line"]:
            copy.wait_recv()
        own_row = pl.multiple_of(self.z * unit, 16)
        h = self.z % 2
        own_cols = total[pl.ds(own_row, unit), span].astype(F32) + got_z[1, :, span].astype(F32)
        self.put(h, span, own_cols)
        self.put(1 - h, span, got_z[0, :, span].astype(F32) + got_z[2, :, span].astype(F32))
        for i in range(4):
            self.copies[g, i][1].wait_send()
        for name in ("diag", "near", "line"):
            for copy in self.copies[g, name]:
                copy.wait_send()

    @staticmethod
    def scratch(rows, shard, columns, groups):
        return [
            pltpu.VMEM((4, rows, columns), BF16),
            pltpu.VMEM((4, rows, columns), BF16),
            pltpu.VMEM((rows, columns), BF16),
            pltpu.VMEM((rows, columns), BF16),
            pltpu.VMEM((rows, columns), BF16),
            pltpu.VMEM((3, shard, columns), BF16),
            pltpu.VMEM((rows, columns), BF16),
            pltpu.SemaphoreType.DMA((4 * groups,)),
        ]


def everyone():
    ctx, z = where_am_i()
    return [(ctx, flip(z, m)) for m in (1, 2, 3)] + [(flip(ctx, m), z) for m in (1, 2, 4)]


def first_sums_kernel(kv_parts, near_parts, far_parts, come, middle, kv_out, output, *scratch):
    ctx, z = where_am_i()
    kv_scratch, scratch = scratch[:8], scratch[8:]
    parts, got, send_sems, recv_sems, own_sems = scratch
    net = Net(send_sems, recv_sems)
    greet(everyone())
    mate, beyond = (ctx, flip(z, 1)), (ctx, flip(z, 3))
    inner = (z == 1) | (z == 2)
    outer = jnp.logical_not(inner)
    kv = KvSum(net, kv_parts, kv_out, *kv_scratch)
    two_over = net.push(parts.at[2], got.at[2], beyond)
    three_over = net.push(parts.at[3], got.at[3], beyond)
    one_mate = net.push(parts.at[1], got.at[4], mate)
    loads = []
    for m in range(4):
        src = near_parts.at[m] if m < 2 else far_parts.at[m - 2]
        loads.append(pltpu.make_async_copy(src, parts.at[m], own_sems.at[m]))
        loads[m].start()
    for k in range(2):
        loads.append(pltpu.make_async_copy(come.at[1 - k], got.at[k], own_sems.at[4 + k]))
        loads[4 + k].start()
    kv.both(kv.start)
    for copy in loads:
        copy.wait()

    @pl.when(inner)
    def _():
        fold(parts.at[2], got.at[0])
        two_over.start()
        fold(parts.at[3], got.at[1])
        three_over.start()

    kv.both(kv.chip_sums)
    kv.both(kv.forward)

    @pl.when(inner)
    def _():
        two_over.wait_recv()
        fold(parts.at[1], got.at[2])

    one_mate.start()
    kv.across()
    kv.finish()
    one_mate.wait_recv()

    @pl.when(outer)
    def _():
        total = middle[...] + parts[0].astype(F32)
        output[...] = (total + got[4].astype(F32)).astype(BF16)

    @pl.when(inner)
    def _():
        three_over.wait_recv()
        total = middle[...] + parts[0].astype(F32) + got[3].astype(F32)
        output[...] = (total + got[4].astype(F32)).astype(BF16)
        two_over.wait_send()
        three_over.wait_send()

    one_mate.wait_send()


def plain_axes(shard):
    return lax.axis_size("ctx") != 8 or lax.axis_size("fsdp") != 4 or shard % 16


def plain_weight_sum(parts):
    z = lax.axis_index("fsdp")
    empty = jnp.zeros_like(parts)
    both = jnp.where(z % 2 == 0, jnp.stack([parts, empty]), jnp.stack([empty, parts]))
    summed = lax.psum_scatter(both, "ctx", scatter_dimension=1, tiled=True)
    return lax.psum_scatter(summed, "fsdp", scatter_dimension=1, tiled=True).astype(F32)


def first_sums(kv_parts, near_parts, far_parts, middle, shard):
    total, _, rows, _ = kv_parts.shape
    ctx_total = total // 2
    kv_parts = kv_parts.reshape(2, ctx_total, 2, rows, HD)
    own, width = middle.shape
    if plain_axes(shard):
        flat = kv_parts.transpose(0, 2, 1, 3, 4).reshape(4 * ctx_total * rows, HD)
        z_sum = lax.psum_scatter(flat, "fsdp", scatter_dimension=0, tiled=True)
        kv = lax.psum_scatter(z_sum, "ctx", scatter_dimension=0, tiled=True).astype(F32)
        out = middle + near_parts[0].astype(F32)
        for m in (1, 2, 3):
            part = near_parts[m] if m < 2 else far_parts[m - 2]
            out = out + swap(part, "fsdp", m).astype(F32)
        return kv, out.astype(BF16)
    copies = KvSum.copies + 3
    come = lax.ppermute(far_parts, "fsdp", [(0, 1), (3, 2)])
    return pl.pallas_call(
        first_sums_kernel,
        out_shape=[
            jax.ShapeDtypeStruct((rows, HD), F32),
            jax.ShapeDtypeStruct((own, width), BF16),
        ],
        in_specs=[ANY] * 4 + [VMEM],
        out_specs=[VMEM] * 2,
        scratch_shapes=KvSum.scratch(rows)
        + [
            pltpu.VMEM((4, own, width), BF16),
            pltpu.VMEM((4 + 1, own, width), BF16),
            pltpu.SemaphoreType.DMA((copies,)),
            pltpu.SemaphoreType.DMA((copies,)),
            pltpu.SemaphoreType.DMA((6,)),
        ],
        compiler_params=pltpu.CompilerParams(
            collective_id=2, has_side_effects=True, vmem_limit_bytes=60 * 1024 * 1024
        ),
        cost_estimate=takes(45),
        name="first_sums",
    )(kv_parts, near_parts, far_parts, come, middle)


def last_sums_kernel(
    widths, out_widths, out_parts, w_qkv, grad_q, grad_kv, cosine, sine, normed, tokens, scale, grad_middle, ffn_scale_grad, *refs
):
    ctx, z = where_am_i()
    q_out, k_out, v_out, o_out, grad_tokens, scales = refs[:6]
    w_scratch, o_scratch, scratch = refs[6:14], refs[14:22], refs[22:]
    give_w, product, w, grads, grad_own, give, got, scale_got, send_sems, recv_sems, own_sems = scratch
    h, core, chip = z % 2, ctx % 2, ctx // 2
    net = Net(send_sems, recv_sems)
    own, width = tokens.shape
    step = 512
    steps = width // step
    loads = []
    for k in range(steps):
        part = pl.ds(k * step, step)
        loads.append(pltpu.make_async_copy(w_qkv.at[part], w.at[part], own_sems.at[k]))
        loads[k].start()
    greet(everyone())

    def put_out(which, span, value):
        o_out[:, pl.ds(pl.multiple_of(which * QW + span.start, 128), span.size)] = value

    outs = WeightSum(net, out_widths, out_parts, put_out, *o_scratch)
    outs.start(0)
    outs.start(1)
    grads[:, :QW] = grad_q[...]
    front, back = grad_kv[:, : HD // 2], grad_kv[:, HD // 2 :]
    c, s = cosine[...], sine[...]
    grads[:, QW : QW + HD // 2] = (front * c + back * s).astype(BF16)
    grads[:, QW + HD // 2 :] = (back * c - front * s).astype(BF16)

    def put(which, span, value):
        if span.start < QW:
            q_out[:, pl.ds(pl.multiple_of(which * QW + span.start, 128), span.size)] = value
            return

        @pl.when(which == 0)
        def _():
            k_out[...] = value

        @pl.when(which == 1)
        def _():
            v_out[...] = value

    weights = WeightSum(net, widths, None, put, *w_scratch)
    mine, got_sib = w_scratch[:2]
    side = mine.shape[1]

    def produce(g):
        span = weights.spans[g]
        for i, m in enumerate((3, 1, 2, 0)):
            cols = pl.ds(pl.multiple_of(flip(chip, m) * 2 * side, 128), 2 * side)
            product[:, : span.size] = t_dot(normed[:, cols], grads[:, span]).astype(BF16)
            keep_at = pl.ds(pl.multiple_of(core * side, 16), side)
            give_at = pl.ds(pl.multiple_of((1 - core) * side, 16), side)
            mine[i, :, span] = product[keep_at, : span.size]
            give_w[i, :, span] = product[give_at, : span.size]
            over = net.push(give_w.at[i, :, span], got_sib.at[i, :, span], weights.sib)
            over.start()
            weights.copies[g, i] = (None, over)

    n = len(widths)
    produce(0)
    other_grads = grads[pl.ds(pl.multiple_of((1 - h) * own, 16), own), :]
    crossing = []
    for k in range(steps):
        loads[k].wait()
        give[k] = dot_t(other_grads, w[pl.ds(k * step, step), :]).astype(BF16)
        crossing.append(net.push(give.at[k], got.at[k], (ctx, flip(z, 1))))
        crossing[k].start()
    partners = [(ctx, flip(z, 1)), (ctx, flip(z, 2))] + [(flip(ctx, m), z) for m in (1, 2, 4)]
    trade = []

    def trade_send(k):
        trade.append(net.push(scales, scale_got.at[k], partners[k]))
        trade[k].start()

    def trade_add(k):
        trade[k].wait()
        scales[...] += scale_got[k]

    def own_part():
        own_grads = grads[pl.ds(pl.multiple_of(h * own, 16), own), :]
        for k in range(steps):
            part = pl.ds(k * step, step)
            grad_own[:, part] = dot_t(own_grads, w[part, :])

    def norm_part():
        value = tokens[...].astype(F32)
        for k in range(steps):
            crossing[k].wait_recv()
            grad_own[:, pl.ds(k * step, step)] += got[k].astype(F32)
        grad = grad_own[...]
        r = inv_rms(value)
        scaled = grad * scale[0:1, :]
        lean = jnp.mean(scaled * value, -1, keepdims=True)
        grad_tokens[...] = grad_middle[...] + (r * scaled - value * (r * r * r * lean))
        scales[...] = jnp.zeros_like(scales)
        scales[0:1, :] = jnp.sum(grad * value * r, 0, keepdims=True)
        scales[1:2, :] = ffn_scale_grad[...]
        trade_send(0)

    def trade_next(k):
        trade_add(k)
        if k + 1 < len(partners):
            trade_send(k + 1)

    outs.chip_sums(0)
    produce(1)
    outs.chip_sums(1)
    outs.forward(0)
    weights.chip_sums(0)
    produce(2)
    outs.forward(1)
    weights.chip_sums(1)
    own_part()
    weights.forward(0)
    outs.line(0)
    weights.chip_sums(2)
    norm_part()
    weights.forward(1)
    outs.line(1)
    trade_next(0)
    weights.forward(2)
    outs.finish(0)
    weights.line(0)
    trade_next(1)
    outs.finish(1)
    weights.line(1)
    trade_next(2)
    weights.line(2)
    trade_next(3)
    weights.finish(0)
    trade_next(4)
    weights.finish(1)
    weights.finish(2)
    for copy in crossing:
        copy.wait_send()


def last_sums(out_parts, w_qkv, grad_q, grad_kv, cosine, sine, normed, tokens, scale, grad_middle, ffn_scale_grad, shard):
    own, width = tokens.shape
    columns = w_qkv.shape[1]
    if plain_axes(shard):
        h = lax.axis_index("fsdp") % 2
        front, back = grad_kv[:, : HD // 2], grad_kv[:, HD // 2 :]
        c, s = cosine, sine
        grad_kv = jnp.concatenate([front * c + back * s, back * c - front * s], 1).astype(BF16)
        grads = jnp.concatenate([grad_q, grad_kv], 1)
        both = plain_weight_sum(t_dot(normed, grads).astype(BF16))
        grad_rows = dot_t(grads, w_qkv)
        other = swap(half(grad_rows, 1 - h).astype(BF16), "fsdp", 1).astype(F32)
        grad, scale_grad = norm_back(tokens.astype(F32), scale[:1], half(grad_rows, h) + other)
        scales = jnp.concatenate([scale_grad[None], ffn_scale_grad])
        queries = jnp.concatenate([both[0, :, :QW], both[1, :, :QW]], 1)
        scales = lax.psum(scales, ("ctx", "fsdp"))
        outs = plain_weight_sum(out_parts)
        outs = jnp.concatenate([outs[0], outs[1]], 1)
        return queries, both[0, :, QW:], both[1, :, QW:], outs, grad_middle + grad, scales
    block = 4 * shard
    rows = normed.shape[0]
    widths = (QW // 2, QW // 2, HD)
    steps = width // 512
    out_widths = (QW // 2, QW // 2)
    copies = 11 * (len(widths) + len(out_widths)) + steps + 5
    *weights, scales = pl.pallas_call(
        functools.partial(last_sums_kernel, widths, out_widths),
        out_shape=[
            jax.ShapeDtypeStruct((shard, 2 * QW), F32),
            jax.ShapeDtypeStruct((shard, HD), F32),
            jax.ShapeDtypeStruct((shard, HD), F32),
            jax.ShapeDtypeStruct((shard, 2 * QW), F32),
            jax.ShapeDtypeStruct((own, width), F32),
            jax.ShapeDtypeStruct((8, width), F32),
        ],
        in_specs=[ANY] * 2 + [VMEM] * 9,
        out_specs=[VMEM] * 6,
        scratch_shapes=WeightSum.scratch(block, shard, columns, len(widths))
        + WeightSum.scratch(block, shard, QW, len(out_widths))
        + [
            pltpu.VMEM((4, block, columns), BF16),
            pltpu.VMEM((2 * block, QW // 2), BF16),
            pltpu.VMEM((width, columns), BF16),
            pltpu.VMEM((rows, columns), BF16),
            pltpu.VMEM((own, width), F32),
            pltpu.VMEM((steps, own, 512), BF16),
            pltpu.VMEM((steps, own, 512), BF16),
            pltpu.VMEM((5, 8, width), F32),
            pltpu.SemaphoreType.DMA((copies,)),
            pltpu.SemaphoreType.DMA((copies,)),
            pltpu.SemaphoreType.DMA((steps,)),
        ],
        compiler_params=pltpu.CompilerParams(
            collective_id=4, has_side_effects=True, vmem_limit_bytes=60 * 1024 * 1024
        ),
        cost_estimate=takes(60),
        name="last_sums",
    )(out_parts, w_qkv, grad_q, grad_kv, cosine, sine, normed, tokens, scale, grad_middle, ffn_scale_grad)
    return *weights, scales[:2]


def local(
    tokens,
    lengths,
    block_place,
    gain_attn,
    w_query,
    w_key,
    w_value,
    w_out,
    gain_ffn,
    w_gate,
    w_up,
    w_down,
    cotangent,
):
    own_rows, width = tokens.shape
    rows = 2 * own_rows
    ctx_total = lax.axis_size("ctx")
    ctx, z = where_am_i()
    h, pair = z % 2, z // 2
    shard = w_query.shape[0]
    reach = -(-WIN // rows)

    def place_of(stored):
        hit = jnp.arange(block_place.shape[0])[None, :] == stored[:, None]
        return jnp.sum(jnp.where(hit, block_place[None, :], 0), 1)

    own_pos = place_of((2 * ctx + pair)[None])[0]
    query_at = own_pos * rows + jnp.arange(rows, dtype=jnp.int32)
    passed = query_at[:, None] >= jnp.cumsum(lengths)[None, :]
    doc_start = jnp.sum(jnp.where(passed, lengths[None, :], 0), 1)
    rel_pos = query_at - doc_start
    window_start = (own_pos - reach) * rows
    lowest = jnp.maximum(doc_start, query_at - WIN + 1) - window_start
    lowest = jnp.broadcast_to(lowest[:, None], (rows, 128)).astype(jnp.int32)
    holders = jnp.arange(ctx_total)
    held = jnp.concatenate([place_of(2 * holders), place_of(2 * holders + 1)])
    held = jnp.where((pair == 1) | (jnp.arange(2 * ctx_total) < ctx_total), held, -1000)
    want = own_pos - reach + jnp.arange(reach + 1)
    hit = held[None, :] == want[:, None]
    numbers = jnp.arange(2 * ctx_total)
    own_index = pair * ctx_total + ctx
    place = jnp.where(jnp.any(hit, 1), jnp.sum(jnp.where(hit, numbers, 0), 1), own_index)
    place = place.astype(jnp.int32)
    goes = held - (own_pos - reach)
    goes = jnp.where((goes >= 0) & (goes <= reach), goes, reach + 1).astype(jnp.int32)
    half_dim = HD // 2
    frequency = jnp.exp(jnp.arange(half_dim, dtype=F32) * (-jnp.log(10000.0) / half_dim))
    angles = rel_pos.astype(F32)[:, None] * frequency
    cosine, sine = jnp.cos(angles), jnp.sin(angles)
    q_scale = HD ** (-0.5)
    kv_cosine, kv_sine = jnp.where(h == 0, cosine, 1.0), jnp.where(h == 0, sine, 0.0)
    cosine = jnp.stack([cosine * q_scale, kv_cosine])
    sine = jnp.stack([sine * q_scale, kv_sine])

    gate_up_shard = jnp.concatenate([w_gate, w_up], 1)
    down_shard = w_down.T
    w_qkv, w_o, gains, rows_in, cot_one, cot_three = gather_weights(
        w_query, w_key, w_value, w_out, gain_attn, gain_ffn, tokens, cotangent
    )
    w_qkv, w_o, gate_up_shard, down_shard = lax.optimization_barrier(
        (w_qkv, w_o, gate_up_shard, down_shard)
    )
    gate_up_w = lax.all_gather(gate_up_shard, "ctx", axis=0, tiled=True)
    down_w = lax.all_gather(down_shard, "ctx", axis=0, tiled=True)
    normed, queries, kv, scales = project(rows_in, gains, shard, cosine, sine, w_qkv)
    inner = (z == 1) | (z == 2)
    across = lax.ppermute(cot_one, "fsdp", [(1, 2), (2, 1)])
    outward = lax.ppermute(cot_three, "fsdp", [(1, 0), (2, 3)])
    store = gather_kv(kv)
    store, across, outward = lax.optimization_barrier((store, across, outward))
    farther = lax.ppermute(across, "fsdp", [(1, 0), (2, 3)])
    prob, attended = attend(place, lowest, queries, store, reach)
    attended, farther = lax.optimization_barrier((attended, farther))
    cots = (
        cotangent,
        cot_one,
        jnp.where(inner, across, outward),
        jnp.where(inner, cot_three, farther),
    )
    middle, own_normed, mate_normed, beyond_normed = out_norm(attended, tokens, scales, w_o)

    ffn_in, hidden, active, sloped = feed_forward(
        own_normed, mate_normed, beyond_normed, gate_up_w
    )
    ffn_cot, grad_gate, grad_up = feed_forward_grad(cots, down_w, active, sloped)

    def sum_ctx(g):
        return lax.psum_scatter(g, "ctx", scatter_dimension=0, tiled=True).astype(F32)

    down_part = t_dot(ffn_cot, hidden).astype(BF16)
    down_part, grad_gate, grad_up = lax.optimization_barrier((down_part, grad_gate, grad_up))
    grad_down = sum_ctx(down_part).T
    gate_up_part, gate_sum, near_parts, far_parts, grad_middle, grad_branch, grad_ffn_scale = feed_forward_back(
        grad_gate, grad_up, gate_up_w, down_w, hidden, ffn_in, middle, cotangent, scales
    )
    same_core = [list(range(core, ctx_total, 2)) for core in range(2)]
    grad_up_w = lax.psum_scatter(
        gate_up_part, "ctx", scatter_dimension=0, axis_index_groups=same_core, tiled=True
    ).astype(F32)
    if ctx_total == 8:
        grad_gate_w = gate_sum.astype(F32)
    else:
        units = w_gate.shape[1]
        grad_gate_w, grad_up_w = grad_up_w[:, :units], grad_up_w[:, units:]
    grad_out_part = t_dot(grad_branch, attended).astype(BF16)
    grad_branch, grad_down = lax.optimization_barrier((grad_branch, grad_down))

    grad_q, kv_parts = attend_back(
        place, goes, prob, queries, grad_branch, w_o, cosine, sine, store, reach
    )
    grad_kv, output = first_sums(kv_parts, near_parts, far_parts, middle, shard)
    grad_query_w, grad_key_w, grad_value_w, grad_out_w, grad_tokens, scale_sums = last_sums(
        grad_out_part,
        w_qkv,
        grad_q,
        grad_kv,
        kv_cosine,
        kv_sine,
        normed,
        tokens,
        scales,
        grad_middle,
        grad_ffn_scale,
        shard,
    )
    first_col = (ctx * lax.axis_size("fsdp") + z) * shard
    scale_sums = lax.dynamic_slice_in_dim(scale_sums, first_col, shard, 1)
    return (
        output,
        grad_tokens,
        scale_sums[0],
        grad_query_w,
        grad_key_w,
        grad_value_w,
        grad_out_w.T,
        scale_sums[1],
        grad_gate_w,
        grad_up_w,
        grad_down,
    )


def solution(mesh):
    in_specs = (
        P(("ctx", "fsdp"), None),
        P(),
        P(),
        P(("ctx", "fsdp")),
        P(("ctx", "fsdp"), None),
        P(("ctx", "fsdp"), None),
        P(("ctx", "fsdp"), None),
        P(None, ("ctx", "fsdp")),
        P(("ctx", "fsdp")),
        P("ctx", "fsdp"),
        P("ctx", "fsdp"),
        P("fsdp", "ctx"),
        P(("ctx", "fsdp"), None),
    )
    out_specs = (
        P(("ctx", "fsdp"), None),
        P(("ctx", "fsdp"), None),
        P(("ctx", "fsdp")),
        P(("ctx", "fsdp"), None),
        P(("ctx", "fsdp"), None),
        P(("ctx", "fsdp"), None),
        P(None, ("ctx", "fsdp")),
        P(("ctx", "fsdp")),
        P("ctx", "fsdp"),
        P("ctx", "fsdp"),
        P("fsdp", "ctx"),
    )
    return jax.shard_map(local, mesh=mesh, in_specs=in_specs, out_specs=out_specs, check_vma=False)
```

```python
import functools

import jax
import jax.numpy as jnp
from jax import lax
from jax.experimental import pallas as pl
from jax.experimental.pallas import tpu as pltpu
from jax.sharding import PartitionSpec as P

H = 10
HD = 256
WIN = 2048
EPS = 1e-06
F32 = jnp.float32
BF16 = jnp.bfloat16
MESH = pl.DeviceIdType.MESH
ANY = pl.BlockSpec(memory_space=pl.ANY)
VMEM = pl.BlockSpec(memory_space=pltpu.VMEM)
HEADS = H // 2
QW = HEADS * HD
VMEM_LIMIT = 56 * 1024 * 1024
FAR = -1e30


def swap(x, axis, mask):
    return lax.ppermute(x, axis, [(i, i ^ mask) for i in range(lax.axis_size(axis))])


def join(own, other, bit, axis):
    return jnp.where(
        bit == 0,
        jnp.concatenate([own, other], axis),
        jnp.concatenate([other, own], axis),
    )


def half(x, which, axis=0):
    size = x.shape[axis] // 2
    return lax.dynamic_slice_in_dim(x, which * size, size, axis)


def dot(a, b):
    return jnp.dot(a, b, preferred_element_type=F32)


def dot_t(a, b):
    return lax.dot_general(a, b, (((1,), (1,)), ((), ())), preferred_element_type=F32)


def t_dot(a, b):
    return lax.dot_general(a, b, (((0,), (0,)), ((), ())), preferred_element_type=F32)


def inv_rms(x):
    return lax.rsqrt(jnp.mean(x * x, -1, keepdims=True) + EPS)


def norm_back(x, scale, grad):
    r = inv_rms(x)
    scaled = grad * scale
    lean = jnp.mean(scaled * x, -1, keepdims=True)
    return r * scaled - x * (r * r * r * lean), jnp.sum(grad * x * r, 0)


def takes(us):
    return pl.CostEstimate(flops=int(us * 1e9), bytes_accessed=0, transcendentals=0)


class Net:
    def __init__(self, send_sems, recv_sems):
        self.send_sems, self.recv_sems, self.used = send_sems, recv_sems, 0

    def push(self, src, dst, to):
        copy = pltpu.make_async_remote_copy(
            src_ref=src,
            dst_ref=dst,
            send_sem=self.send_sems.at[self.used],
            recv_sem=self.recv_sems.at[self.used],
            device_id=to,
            device_id_type=MESH,
        )
        self.used += 1
        return copy


def greet(partners):
    barrier = pltpu.get_barrier_semaphore()
    for to in partners:
        pl.semaphore_signal(barrier, inc=1, device_id=to, device_id_type=MESH)
    pl.semaphore_wait(barrier, len(partners))


def flip(x, mask):
    for bit in (1, 2, 4):
        if mask & bit:
            x = x + bit - 2 * bit * ((x // bit) % 2)
    return x


def where_am_i():
    return lax.axis_index("ctx"), lax.axis_index("fsdp")


def gather_kernel(
    qkv, out, gain, tokens, cot, w_qkv, w_out, gains, rows, cot_one, cot_three, send_sems, recv_sems, own_sems
):
    ctx, z = where_am_i()
    net = Net(send_sems, recv_sems)
    greet([(ctx, flip(z, m)) for m in (1, 2, 3)] + [(flip(ctx, m), z) for m in (1, 2, 4)])
    shard = qkv.shape[0]
    qkv_cols, half_cols = QW + HD, QW // 2

    def cols_of(ref, stride, first, count):
        return lambda h: ref.at[:, pl.ds(pl.multiple_of(h * stride + first, 128), count)]

    groups = [
        (cols_of(qkv, qkv_cols, QW, HD), w_qkv, shard, QW, HD),
        (lambda h: gain, gains, 8, 0, 128),
        (cols_of(qkv, qkv_cols, 0, half_cols), w_qkv, shard, 0, half_cols),
        (cols_of(qkv, qkv_cols, half_cols, half_cols), w_qkv, shard, half_cols, half_cols),
        (cols_of(out, QW, 0, half_cols), w_out, shard, 0, half_cols),
        (cols_of(out, QW, half_cols, half_cols), w_out, shard, half_cols, half_cols),
    ]

    def at(group, source, first, count):
        src, ref, unit, col, cols = group
        start = pl.multiple_of(source * 4 * unit + first, 8 if unit == 8 else 16)
        return ref.at[pl.ds(start, count), pl.ds(col, cols)]

    lines, locals_, sent = [], [], []

    def push(src, dst, to):
        copy = net.push(src, dst, to)
        copy.start()
        sent.append(copy)
        return copy

    token_rows = tokens.shape[0]
    token_dst = rows.at[pl.ds(pl.multiple_of((z % 2) * token_rows, 16), token_rows)]
    for i, group in enumerate(groups):
        unit = group[2]
        dst = at(group, ctx, z * unit, unit)
        lines.append([push(group[0](flip(z, m) % 2), dst, (ctx, flip(z, m))) for m in (2, 3, 1)])
        local = pltpu.make_async_copy(group[0](z % 2), dst, own_sems.at[i])
        local.start()
        locals_.append(local)
        if i == 3:
            token_copy = push(tokens, token_dst, (ctx, flip(z, 1)))
            token_local = pltpu.make_async_copy(tokens, token_dst, own_sems.at[len(groups)])
            token_local.start()
    mate, beyond = (ctx, flip(z, 1)), (ctx, flip(z, 3))
    inner = (z == 1) | (z == 2)
    cot_mate = push(cot, cot_one, mate)
    cot_beyond = net.push(cot, cot_three, beyond)

    @pl.when(inner)
    def _():
        cot_beyond.start()

    by_x, by_y, last = {}, {}, []
    diag = {}
    x_dev, y_dev, sib = (flip(ctx, 2), z), (flip(ctx, 4), z), (flip(ctx, 1), z)

    def same(group, source, first, count, to):
        return push(at(group, source, first, count), at(group, source, first, count), to)

    def spread_own(i):
        group = groups[i]
        locals_[i].wait()
        for copy in lines[i]:
            copy.wait_recv()
        count = 4 * group[2]
        by_x[i] = same(group, ctx, 0, count, x_dev)
        by_y[i] = same(group, ctx, 0, count, y_dev)
        last.append(same(group, ctx, 0, count, sib))

    def spread_near(i):
        group = groups[i]
        count = 4 * group[2]
        by_x[i].wait_recv()
        top = same(group, flip(ctx, 2), 0, count // 2, y_dev)
        last.append(same(group, flip(ctx, 2), 0, count, sib))
        by_y[i].wait_recv()
        low = same(group, flip(ctx, 4), count // 2, count // 2, x_dev)
        last.append(same(group, flip(ctx, 4), 0, count, sib))
        diag[i] = (top, low)

    def spread_far(i):
        group = groups[i]
        count = 4 * group[2]
        for k in range(2):
            diag[i][k].wait_recv()
            last.append(same(group, flip(ctx, 6), k * count // 2, count // 2, sib))

    for i in range(len(groups) + 2):
        if i < len(groups):
            spread_own(i)
        if 0 <= i - 1 < len(groups):
            spread_near(i - 1)
        if 0 <= i - 2 < len(groups):
            spread_far(i - 2)
    token_local.wait()
    token_copy.wait_recv()
    cot_mate.wait_recv()

    @pl.when(inner)
    def _():
        cot_beyond.wait_recv()
        cot_beyond.wait_send()

    for copy in last:
        copy.wait_recv()
    for copy in sent:
        copy.wait_send()


def gather_weights(w_query, w_key, w_value, w_out, gain_attn, gain_ffn, tokens, cotangent):
    shard, width = w_query.shape
    z = lax.axis_index("fsdp")
    ctx_total = lax.axis_size("ctx")
    pieces = []
    for h in range(2):
        pieces += [w_query[:, h * QW : (h + 1) * QW], (w_key, w_value)[h]]
    qkv = jnp.concatenate(pieces, 1)
    out = w_out.T
    gain = jnp.stack([gain_attn, gain_ffn]).astype(F32)
    gain = jnp.pad(gain, ((0, 6), (0, 128 - shard)))
    if ctx_total != 8 or lax.axis_size("fsdp") != 4 or shard % 16:
        both = ("ctx", "fsdp")
        full = lax.all_gather(qkv, both, axis=0, tiled=True)
        full_out = lax.all_gather(out, both, axis=0, tiled=True)
        return (
            half(full, z % 2, 1),
            half(full_out, z % 2, 1),
            lax.all_gather(gain, both, axis=0, tiled=True),
            join(tokens, swap(tokens, "fsdp", 1), z % 2, 0),
            swap(cotangent, "fsdp", 1),
            swap(cotangent, "fsdp", 3),
        )
    devices = 4 * ctx_total
    w_qkv, w_o, gains, rows, cot_one, cot_three = pl.pallas_call(
        gather_kernel,
        out_shape=[
            jax.ShapeDtypeStruct((width, QW + HD), BF16),
            jax.ShapeDtypeStruct((width, QW), BF16),
            jax.ShapeDtypeStruct((8 * devices, 128), F32),
            jax.ShapeDtypeStruct((2 * tokens.shape[0], width), BF16),
            jax.ShapeDtypeStruct(tokens.shape, BF16),
            jax.ShapeDtypeStruct(tokens.shape, BF16),
        ],
        in_specs=[ANY] * 5,
        out_specs=[ANY] * 6,
        scratch_shapes=[
            pltpu.SemaphoreType.DMA((75,)),
            pltpu.SemaphoreType.DMA((75,)),
            pltpu.SemaphoreType.DMA((7,)),
        ],
        compiler_params=pltpu.CompilerParams(collective_id=0, has_side_effects=True),
        cost_estimate=takes(80),
        name="gather_weights",
    )(qkv, out, gain, tokens, cotangent)
    return w_qkv, w_o, gains, rows, cot_one, cot_three


def proj_kernel(shard, rows, gains, cosine, sine, w, normed, out, kv, scales):
    @pl.when(pl.program_id(0) == 0)
    def _():
        for i in range(gains.shape[0] // 8):
            scales[:, i * shard : (i + 1) * shard] = gains[8 * i : 8 * i + 8, :shard]
        x = rows[...].astype(F32)
        normed[...] = (x * inv_rms(x) * scales[0:1, :]).astype(BF16)

    value = dot(normed[...], w[...])
    front, back = value[:, : HD // 2], value[:, HD // 2 :]
    c, s = cosine[0], sine[0]

    def put(ref):
        ref[:, : HD // 2] = (front * c - back * s).astype(BF16)
        ref[:, HD // 2 :] = (back * c + front * s).astype(BF16)

    pl.when(pl.program_id(0) < HEADS)(lambda: put(out))
    pl.when(pl.program_id(0) == HEADS)(lambda: put(kv))


def project(rows, gains, shard, cosine, sine, w):
    count, width = rows.shape
    steps = HEADS + 1
    fixed = lambda i: (0, 0)
    table = pl.BlockSpec((1, count, HD // 2), lambda i: (i // HEADS, 0, 0))
    return pl.pallas_call(
        functools.partial(proj_kernel, shard),
        grid=(steps,),
        out_shape=[
            jax.ShapeDtypeStruct((count, width), BF16),
            jax.ShapeDtypeStruct((count, QW), BF16),
            jax.ShapeDtypeStruct((count, HD), BF16),
            jax.ShapeDtypeStruct((8, width), F32),
        ],
        in_specs=[
            pl.BlockSpec((count, width), fixed),
            pl.BlockSpec(gains.shape, fixed),
            table,
            table,
            pl.BlockSpec((width, HD), lambda i: (0, i)),
        ],
        out_specs=[
            pl.BlockSpec((count, width), fixed),
            pl.BlockSpec((count, HD), lambda i: (0, jnp.minimum(i, HEADS - 1))),
            pl.BlockSpec((count, HD), fixed),
            pl.BlockSpec((8, width), fixed),
        ],
        compiler_params=pltpu.CompilerParams(vmem_limit_bytes=VMEM_LIMIT),
        cost_estimate=takes(10),
        name="project",
    )(rows, gains, cosine, sine, w)


def kv_gather_kernel(kv, store, send_sems, recv_sems, own_sem):
    ctx, z = where_am_i()
    net = Net(send_sems, recv_sems)
    h, pair = z % 2, z // 2
    greet([(ctx, flip(z, m)) for m in (1, 2)] + [(flip(ctx, m), z) for m in (1, 2, 4)])
    local = pltpu.make_async_copy(kv, store.at[pair, ctx, h], own_sem)
    local.start()
    mate, across = (ctx, flip(z, 1)), (ctx, flip(z, 2))
    x_dev, y_dev, sib = (flip(ctx, 2), z), (flip(ctx, 4), z), (flip(ctx, 1), z)
    own = net.push(kv, store.at[pair, ctx, h], mate)
    own.start()
    low = net.push(kv, store.at[0, ctx, h], across)
    low_mate = net.push(store.at[0, ctx, h], store.at[0, ctx, h], mate)

    @pl.when(pair == 0)
    def _():
        low.start()

    local.wait()
    own.wait_recv()

    class Set:
        def __init__(self, which):
            def same(source, kind, to):
                if kind is None:
                    ref = store.at[which, source]
                else:
                    ref = store.at[which, source, kind]
                return net.push(ref, ref, to)

            self.near = [same(ctx, None, x_dev), same(ctx, None, y_dev), same(ctx, None, sib)]
            x_ctx, y_ctx, d_ctx = flip(ctx, 2), flip(ctx, 4), flip(ctx, 6)
            self.after_x = [same(x_ctx, 0, y_dev), same(x_ctx, None, sib)]
            self.after_y = [same(y_ctx, 1, x_dev), same(y_ctx, None, sib)]
            self.after_d = [same(d_ctx, 0, sib), same(d_ctx, 1, sib)]

        def first(self):
            for copy in self.near:
                copy.start()

        def second(self):
            self.near[0].wait_recv()
            for copy in self.after_x:
                copy.start()
            self.near[1].wait_recv()
            for copy in self.after_y:
                copy.start()

        def third(self):
            self.after_x[0].wait_recv()
            self.after_d[0].start()
            self.after_y[0].wait_recv()
            self.after_d[1].start()

        def finish(self):
            for copy in [self.near[2], self.after_x[1], self.after_y[1]] + self.after_d:
                copy.wait_recv()
            for copy in self.near + self.after_x + self.after_y + self.after_d:
                copy.wait_send()

    mine = Set(pair)
    lower = Set(0)
    mine.first()

    @pl.when(pair == 1)
    def _():
        low.wait_recv()
        low_mate.start()
        low_mate.wait_recv()
        lower.first()

    mine.second()

    @pl.when(pair == 1)
    def _():
        lower.second()

    mine.third()

    @pl.when(pair == 1)
    def _():
        lower.third()

    mine.finish()
    own.wait_send()

    @pl.when(pair == 1)
    def _():
        lower.finish()
        low_mate.wait_send()

    @pl.when(pair == 0)
    def _():
        low.wait_send()


def gather_kv(kv):
    ctx_total = lax.axis_size("ctx")
    rows = kv.shape[0]
    if ctx_total != 8 or lax.axis_size("fsdp") != 4:
        every = lax.all_gather(kv, ("fsdp", "ctx"), axis=0, tiled=False)
        every = every.reshape(2, 2, ctx_total, rows, HD).transpose(0, 2, 1, 3, 4)
        return every.reshape(2 * ctx_total, 2, rows, HD)
    store = pl.pallas_call(
        kv_gather_kernel,
        out_shape=jax.ShapeDtypeStruct((2, ctx_total, 2, rows, HD), BF16),
        in_specs=[ANY],
        out_specs=ANY,
        scratch_shapes=[
            pltpu.SemaphoreType.DMA((21,)),
            pltpu.SemaphoreType.DMA((21,)),
            pltpu.SemaphoreType.DMA,
        ],
        compiler_params=pltpu.CompilerParams(collective_id=1, has_side_effects=True),
        cost_estimate=takes(30),
        name="gather_kv",
    )(kv)
    return store.reshape(2 * ctx_total, 2, rows, HD)


def chunks(rows, reach):
    skip = (reach * rows - WIN) // 128 * 128
    parts, at = [], 0
    for r in range(reach + 1):
        begin = max(0, skip - r * rows)
        if begin < rows:
            parts.append((r, begin, at, rows - begin))
            at += rows - begin
    return parts, at


def attend_kernel(reach, place, lowest, q, *refs):
    keys, values = refs[: reach + 1], refs[reach + 1 : 2 * reach + 2]
    prob, out, scores = refs[2 * reach + 2 :]
    rows = q.shape[0]
    parts, total = chunks(rows, reach)
    low = lowest[:, :1]
    peak = None
    for r, begin, at, count in parts:
        s = dot_t(q[...], keys[r][0, 0, begin:, :])
        key_at = lax.broadcasted_iota(jnp.int32, (rows, count), 1) + (r * rows + begin)
        visible = key_at >= low
        if r == reach:
            query_at = lax.broadcasted_iota(jnp.int32, (rows, count), 0) + reach * rows
            visible = visible & (key_at <= query_at)
        s = jnp.where(visible, s, FAR)
        scores[:, at : at + count] = s
        top = jnp.max(s, -1, keepdims=True)
        peak = top if peak is None else jnp.maximum(peak, top)
    weight_sum = jnp.zeros_like(peak)
    for r, begin, at, count in parts:
        e = jnp.exp(scores[:, at : at + count] - peak)
        scores[:, at : at + count] = e
        weight_sum = weight_sum + jnp.sum(e, -1, keepdims=True)
    share = 1.0 / weight_sum
    mixed = jnp.zeros((rows, HD), F32)
    for r, begin, at, count in parts:
        p = (scores[:, at : at + count] * share).astype(BF16)
        prob[0, :, at : at + count] = p
        mixed = mixed + dot(p, values[r][0, 0, begin:, :])
    out[...] = mixed.astype(BF16)


def window_specs(rows, reach):
    def spec(r, kind):
        return pl.BlockSpec((1, 1, rows, HD), lambda i, place: (place[r], kind, 0, 0))

    return [spec(r, kind) for kind in range(2) for r in range(reach + 1)]


def attend(place, lowest, qkv, store, reach):
    rows = qkv.shape[0]
    total = chunks(rows, reach)[1]
    column = pl.BlockSpec((rows, HD), lambda i, place: (0, i))
    return pl.pallas_call(
        functools.partial(attend_kernel, reach),
        grid_spec=pltpu.PrefetchScalarGridSpec(
            num_scalar_prefetch=1,
            grid=(HEADS,),
            in_specs=[pl.BlockSpec((rows, 128), lambda i, place: (0, 0)), column]
            + window_specs(rows, reach),
            out_specs=[
                pl.BlockSpec((1, rows, total), lambda i, place: (i, 0, 0)),
                column,
            ],
            scratch_shapes=[pltpu.VMEM((rows, total), F32)],
        ),
        out_shape=[
            jax.ShapeDtypeStruct((HEADS, rows, total), BF16),
            jax.ShapeDtypeStruct((rows, QW), BF16),
        ],
        compiler_params=pltpu.CompilerParams(vmem_limit_bytes=VMEM_LIMIT),
        cost_estimate=takes(21),
        name="attend",
    )(place, lowest, qkv, *([store] * (2 * reach + 2)))


def attend_back_kernel(reach, place, goes, prob, q, branch, w_out, cosine, sine, *refs):
    keys, values = refs[: reach + 1], refs[reach + 1 : 2 * reach + 2]
    grad_q, store, grad_probs, sums, blocks, sems = refs[2 * reach + 2 :]
    rows = q.shape[0]
    parts, total = chunks(rows, reach)
    head = pl.program_id(0)

    @pl.when(head == 0)
    def _():
        sums[...] = jnp.zeros_like(sums)

    grad_rows = dot(branch[...], w_out[...]).astype(BF16)
    query_rows = q[...]
    lean = jnp.zeros((rows, 1), F32)
    for r, begin, at, count in parts:
        dp = dot_t(grad_rows, values[r][0, 0, begin:, :])
        p = prob[0, :, at : at + count]
        grad_probs[:, at : at + count] = dp
        lean = lean + jnp.sum(dp * p.astype(F32), -1, keepdims=True)
        sums[1, at : at + count, :] += t_dot(p, grad_rows)
    turned = jnp.zeros((rows, HD), F32)
    for r, begin, at, count in parts:
        p = prob[0, :, at : at + count].astype(F32)
        ds = (p * (grad_probs[:, at : at + count] - lean)).astype(BF16)
        turned = turned + dot(ds, keys[r][0, 0, begin:, :])
        sums[0, at : at + count, :] += t_dot(ds, query_rows)
    front, back = turned[:, : HD // 2], turned[:, HD // 2 :]
    c, s = cosine[0], sine[0]
    grad_q[:, : HD // 2] = (front * c + back * s).astype(BF16)
    grad_q[:, HD // 2 :] = (back * c - front * s).astype(BF16)

    @pl.when(head == pl.num_programs(0) - 1)
    def _():
        blocks[reach + 1] = jnp.zeros((2, rows, HD), BF16)
        for r, begin, at, count in parts:
            for kind in range(2):
                if begin > 0:
                    blocks[r, kind, :begin, :] = jnp.zeros((begin, HD), BF16)
                blocks[r, kind, begin:, :] = sums[kind, at : at + count, :].astype(BF16)
        for r in range(parts[0][0]):
            blocks[r] = jnp.zeros((2, rows, HD), BF16)
        count = store.shape[0]

        def copy(i):
            return pltpu.make_async_copy(blocks.at[goes[i]], store.at[i], sems.at[i])

        for i in range(count):
            copy(i).start()
        for i in range(count):
            copy(i).wait()


def attend_back(place, goes, prob, qkv, branch, w_out, cosine, sine, store, reach):
    rows = qkv.shape[0]
    total = chunks(rows, reach)[1]
    column = pl.BlockSpec((rows, HD), lambda i, place, goes: (0, i))
    table = pl.BlockSpec((1, rows, HD // 2), lambda i, place, goes: (0, 0, 0))

    def spec(r, kind):
        return pl.BlockSpec((1, 1, rows, HD), lambda i, place, goes: (place[r], kind, 0, 0))

    return pl.pallas_call(
        functools.partial(attend_back_kernel, reach),
        grid_spec=pltpu.PrefetchScalarGridSpec(
            num_scalar_prefetch=2,
            grid=(HEADS,),
            in_specs=[
                pl.BlockSpec((1, rows, total), lambda i, place, goes: (i, 0, 0)),
                column,
                pl.BlockSpec(branch.shape, lambda i, place, goes: (0, 0)),
                pl.BlockSpec((w_out.shape[0], HD), lambda i, place, goes: (0, i)),
                table,
                table,
            ]
            + [spec(r, kind) for kind in range(2) for r in range(reach + 1)],
            out_specs=[column, ANY],
            scratch_shapes=[
                pltpu.VMEM((rows, total), F32),
                pltpu.VMEM((2, total, HD), F32),
                pltpu.VMEM((reach + 2, 2, rows, HD), BF16),
                pltpu.SemaphoreType.DMA((store.shape[0],)),
            ],
        ),
        out_shape=[
            jax.ShapeDtypeStruct((rows, QW), BF16),
            jax.ShapeDtypeStruct(store.shape, BF16),
        ],
        compiler_params=pltpu.CompilerParams(vmem_limit_bytes=VMEM_LIMIT),
        cost_estimate=takes(24),
        name="attend_back",
    )(place, goes, prob, qkv, branch, w_out, cosine, sine, *([store] * (2 * reach + 2)))


def out_norm_kernel(
    attended, tokens, scale, w_out, middle, own_rows, mate_rows, beyond_rows, wo, other, got, mine, send_sems, recv_sems, own_sems
):
    ctx, z = where_am_i()
    h = z % 2
    net = Net(send_sems, recv_sems)
    mate, beyond = (ctx, flip(z, 1)), (ctx, flip(z, 3))
    own, width = tokens.shape
    step = 512
    steps = width // step
    loads = []
    for k in range(steps):
        part = pl.ds(k * step, step)
        loads.append(pltpu.make_async_copy(w_out.at[part], wo.at[part], own_sems.at[k]))
        loads[k].start()
    greet([mate, beyond])
    keep = attended[pl.ds(pl.multiple_of(h * own, 16), own), :]
    give = attended[pl.ds(pl.multiple_of((1 - h) * own, 16), own), :]
    crossing = []
    for k in range(steps):
        part = pl.ds(k * step, step)
        loads[k].wait()
        other[k] = dot_t(give, wo[part, :]).astype(BF16)
        crossing.append(net.push(other.at[k], got.at[k], mate))
        crossing[k].start()
    for k in range(steps):
        part = pl.ds(k * step, step)
        middle[:, part] = tokens[:, part].astype(F32) + dot_t(keep, wo[part, :])
    square = jnp.zeros((own, 1), F32)
    for k in range(steps):
        part = pl.ds(k * step, step)
        crossing[k].wait_recv()
        value = middle[:, part] + got[k].astype(F32)
        middle[:, part] = value
        square = square + jnp.sum(value * value, -1, keepdims=True)
    r = lax.rsqrt(square / width + EPS)
    for k in range(steps):
        part = pl.ds(k * step, step)
        mine[:, part] = (middle[:, part] * r * scale[1:2, part]).astype(BF16)
    to_mate = net.push(mine, mate_rows, mate)
    to_beyond = net.push(mine, beyond_rows, beyond)
    to_mate.start()
    inner = (z == 1) | (z == 2)
    pl.when(inner)(to_beyond.start)
    local = pltpu.make_async_copy(mine, own_rows, own_sems.at[steps])
    local.start()
    for k in range(steps):
        crossing[k].wait_send()
    local.wait()
    to_mate.wait()
    pl.when(inner)(to_beyond.wait)


def out_norm(attended, tokens, scale, w_out):
    own, width = tokens.shape
    line = jax.ShapeDtypeStruct((own, width), BF16)
    return pl.pallas_call(
        out_norm_kernel,
        out_shape=[jax.ShapeDtypeStruct((own, width), F32), line, line, line],
        in_specs=[VMEM] * 3 + [ANY],
        out_specs=[VMEM] + [ANY] * 3,
        scratch_shapes=[
            pltpu.VMEM(w_out.shape, BF16),
            pltpu.VMEM((width // 512, own, 512), BF16),
            pltpu.VMEM((width // 512, own, 512), BF16),
            pltpu.VMEM((own, width), BF16),
            pltpu.SemaphoreType.DMA((width // 512 + 2,)),
            pltpu.SemaphoreType.DMA((width // 512 + 2,)),
            pltpu.SemaphoreType.DMA((width // 512 + 1,)),
        ],
        compiler_params=pltpu.CompilerParams(
            collective_id=3, has_side_effects=True, vmem_limit_bytes=VMEM_LIMIT
        ),
        cost_estimate=takes(55),
        name="out_norm",
    )(attended, tokens, scale, w_out)


def ffn_kernel(
    own_rows,
    mate_rows,
    beyond_rows,
    gate_up_w,
    rows_out,
    hidden_out,
    active_out,
    sloped_out,
    wg,
    wu,
    x,
    hidden,
    active,
    sloped,
    send_sems,
    recv_sems,
    own_sems,
    out_sems,
):
    ctx, z = where_am_i()
    net = Net(send_sems, recv_sems)
    mate, beyond = (ctx, flip(z, 1)), (ctx, flip(z, 3))
    own, width = own_rows.shape
    units = wg.shape[1]
    spans = [pl.ds(c, min(512, units - c)) for c in range(0, units, 512)]
    count = len(spans)
    inner = (z == 1) | (z == 2)
    pulls = []
    for m, src in ((0, own_rows), (1, mate_rows)):
        pulls.append(
            pltpu.make_async_copy(src, x.at[pl.ds(m * own, own)], own_sems.at[2 * count + m])
        )
        pulls[m].start()
    loads = []
    for c in range(count):
        span = spans[c]
        pair = []
        for k, dst in enumerate((wg, wu)):
            src = gate_up_w.at[:, pl.ds(k * units + span.start, span.size)]
            pair.append(pltpu.make_async_copy(src, dst.at[:, span], own_sems.at[2 * c + k]))
            pair[k].start()
        loads.append(pair)
    greet([mate, beyond])
    one_beyond = net.push(mate_rows, x.at[pl.ds(2 * own, own)], beyond)
    three_mate = net.push(beyond_rows, x.at[pl.ds(2 * own, own)], mate)
    two_mate = net.push(x.at[pl.ds(2 * own, own)], x.at[pl.ds(3 * own, own)], mate)
    three_local = pltpu.make_async_copy(
        beyond_rows, x.at[pl.ds(3 * own, own)], own_sems.at[2 * count + 2]
    )

    @pl.when(inner)
    def _():
        one_beyond.start()
        three_mate.start()
        three_local.start()

    def work(first, rows, c, ready):
        if ready is not None:
            for copy in ready:
                copy.wait()
        span = spans[c]
        at = pl.ds(first, rows)
        gate = dot(x[at, :], wg[:, span])
        up = dot(x[at, :], wu[:, span])
        root, cubic = 0.7978845608028654, 0.044715
        square = gate * gate
        bent = jnp.tanh(root * (gate + cubic * square * gate))
        value = 0.5 * gate * (1.0 + bent)
        slope = 0.5 * (1.0 + bent) + 0.5 * gate * (1.0 - bent * bent) * root * (
            1.0 + 3.0 * cubic * square
        )
        hidden[at, span] = (value * up).astype(BF16)
        active[at, span] = value.astype(BF16)
        sloped[at, span] = (slope * up).astype(BF16)

    outs = []

    def flush(m):
        at = pl.ds(m * own, own)
        pairs = ((hidden, hidden_out), (active, active_out), (sloped, sloped_out), (x, rows_out))
        for k, (src, dst) in enumerate(pairs):
            copy = pltpu.make_async_copy(src.at[at], dst.at[at], out_sems.at[4 * m + k])
            copy.start()
            outs.append(copy)

    for copy in pulls:
        copy.wait()
    for c in range(count):
        work(0, 2 * own, c, loads[c])
    flush(0)
    flush(1)

    @pl.when(inner)
    def _():
        one_beyond.wait_recv()
        two_mate.start()

    @pl.when(jnp.logical_not(inner))
    def _():
        three_mate.wait_recv()

    for c in range(count):
        work(2 * own, own, c, None)
    flush(2)

    @pl.when(inner)
    def _():
        three_local.wait()

    @pl.when(jnp.logical_not(inner))
    def _():
        two_mate.wait_recv()

    for c in range(count):
        work(3 * own, own, c, None)
    flush(3)

    @pl.when(inner)
    def _():
        for copy in (one_beyond, three_mate, two_mate):
            copy.wait_send()

    for copy in outs:
        copy.wait()


def feed_forward(own_rows, mate_rows, beyond_rows, gate_up_w):
    own, width = own_rows.shape
    units = gate_up_w.shape[1] // 2
    count = 4 * own
    inner_shape = jax.ShapeDtypeStruct((count, units), BF16)
    return pl.pallas_call(
        ffn_kernel,
        out_shape=[jax.ShapeDtypeStruct((count, width), BF16)] + [inner_shape] * 3,
        in_specs=[ANY] * 4,
        out_specs=[ANY] * 4,
        scratch_shapes=[
            pltpu.VMEM((width, units), BF16),
            pltpu.VMEM((width, units), BF16),
            pltpu.VMEM((count, width), BF16),
            pltpu.VMEM((count, units), BF16),
            pltpu.VMEM((count, units), BF16),
            pltpu.VMEM((count, units), BF16),
            pltpu.SemaphoreType.DMA((3,)),
            pltpu.SemaphoreType.DMA((3,)),
            pltpu.SemaphoreType.DMA((2 * (-(-units // 512)) + 3,)),
            pltpu.SemaphoreType.DMA((16,)),
        ],
        compiler_params=pltpu.CompilerParams(
            collective_id=6, has_side_effects=True, vmem_limit_bytes=VMEM_LIMIT
        ),
        cost_estimate=takes(52),
        name="feed_forward",
    )(own_rows, mate_rows, beyond_rows, gate_up_w)


def ffn_grad_kernel(c0, c1, c2, c3, down_w, active, sloped, cot, grad_gate, grad_up):
    own = c0.shape[0]

    @pl.when(pl.program_id(0) == 0)
    def _():
        for m, piece in enumerate((c0, c1, c2, c3)):
            cot[m * own : (m + 1) * own, :] = piece[...]

    grad = dot(cot[...], down_w[...])
    grad_gate[...] = (sloped[...].astype(F32) * grad).astype(BF16)
    grad_up[...] = (active[...].astype(F32) * grad).astype(BF16)


def ffn_specs(count, width, units):
    step = 512
    whole = pl.BlockSpec((count, width), lambda i: (0, 0))
    weight = pl.BlockSpec((width, step), lambda i: (0, i))
    column = pl.BlockSpec((count, step), lambda i: (0, i))
    return -(-units // step), whole, weight, column


def feed_forward_grad(cots, down_w, active, sloped):
    own, width = cots[0].shape
    count, units = active.shape
    steps, whole, weight, column = ffn_specs(count, width, units)
    piece = pl.BlockSpec((own, width), lambda i: (0, 0))
    return pl.pallas_call(
        ffn_grad_kernel,
        grid=(steps,),
        out_shape=[jax.ShapeDtypeStruct((count, width), BF16)]
        + [jax.ShapeDtypeStruct((count, units), BF16)] * 2,
        in_specs=[piece] * 4 + [weight, column, column],
        out_specs=[whole, column, column],
        compiler_params=pltpu.CompilerParams(vmem_limit_bytes=VMEM_LIMIT),
        cost_estimate=takes(15),
        name="feed_forward_grad",
    )(*cots, down_w, active, sloped)


def ffn_back_kernel(
    grad_gate,
    grad_up,
    gate_up_w,
    down_w,
    hidden,
    rows_in,
    middle,
    cot,
    scale,
    grad_w,
    gate_sum_out,
    ffn_near,
    ffn_far,
    grad_middle,
    branch,
    grad_scale,
    gg,
    gu,
    wg,
    wu,
    x,
    parts,
    got,
    stage,
    mine,
    blocks,
    got_diag,
    got_x,
    got_y,
    send_sems,
    recv_sems,
    own_sems,
    stage_sems,
    give_sems,
    take_sems,
    sum_sems,
):
    ctx, z = where_am_i()
    net = Net(send_sems, recv_sems)
    mate, beyond = (ctx, flip(z, 1)), (ctx, flip(z, 3))
    x_dev, y_dev = (flip(ctx, 2), z), (flip(ctx, 4), z)
    inside_sum = lax.axis_size("ctx") == 8
    greet([mate, beyond, (flip(ctx, 1), z)] + ([x_dev, y_dev] if inside_sum else []))
    inner = (z == 1) | (z == 2)
    own, width = middle.shape
    units = gg.shape[1]
    step = 512
    steps = width // step
    order = (3, 2, 1, 0)
    loads = {}
    used = 0

    def load(name, src, dst):
        nonlocal used
        loads[name] = pltpu.make_async_copy(src, dst, own_sems.at[used])
        loads[name].start()
        used += 1

    for k in range(steps):
        if k < 4:
            m = order[k]
            span = pl.ds(m * own, own)
            load(("gg", m), grad_gate.at[span], gg.at[span])
            load(("gu", m), grad_up.at[span], gu.at[span])
        part = pl.ds(k * step, step)
        load(("wg", k), gate_up_w.at[part, pl.ds(0, units)], wg.at[part])
        load(("wu", k), gate_up_w.at[part, pl.ds(units, units)], wu.at[part])
    load("x", rows_in, x)

    far = net.push(parts.at[3], got.at[0], mate)
    near = net.push(parts.at[2], got.at[1], mate)
    two_over = net.push(parts.at[2], got.at[2], beyond)
    three_over = net.push(parts.at[3], got.at[3], beyond)
    one_mate = net.push(parts.at[1], got.at[4], mate)

    def make(m):
        span = pl.ds(m * own, own)
        loads["gg", m].wait()
        loads["gu", m].wait()
        for k in range(steps):
            part = pl.ds(k * step, step)
            if m == 3:
                loads["wg", k].wait()
                loads["wu", k].wait()
            value = dot_t(gg[span, :], wg[part, :]) + dot_t(gu[span, :], wu[part, :])
            parts[m, :, part] = value.astype(BF16)

    def add_to(m, k):
        parts[m] = (parts[m].astype(F32) + got[k].astype(F32)).astype(BF16)

    make(3)
    pl.when(jnp.logical_not(inner))(far.start)
    make(2)
    pl.when(jnp.logical_not(inner))(near.start)
    make(1)
    make(0)
    load("wd", down_w, wg)
    loads["x"].wait()

    block = 2 * width // lax.axis_size("ctx")
    chips = width // block
    chunk, col_step = stage.shape[1], stage.shape[2]
    sib = (flip(ctx, 1), z)
    core = ctx % 2
    side = block // 2
    slices = units // col_step
    inside = chunk // block
    rounds = width // chunk * slices
    keep_at_of, take_at_of = (0, 1, 1), (0, 1, 0)

    def chip_copies(which, i):
        n = i % slices
        cols = pl.ds(pl.multiple_of(n * col_step, 128), col_step)
        keeps, gives = [], []
        for part in range(inside):
            k = i // slices * inside + part
            sem = (which * chips + k) * slices + n
            keep_rows = pl.ds(pl.multiple_of((keep_at_of[which] * chips + k) * side, 16), side)
            take_rows = pl.ds(pl.multiple_of((take_at_of[which] * chips + k) * side, 16), side)
            mine_at = pl.ds(pl.multiple_of(part * block + core * side, 16), side)
            give_at = pl.ds(pl.multiple_of(part * block + (1 - core) * side, 16), side)
            keeps.append(
                pltpu.make_async_copy(
                    stage.at[i % 2, mine_at], wu.at[keep_rows, cols], stage_sems.at[sem]
                )
            )
            gives.append(
                pltpu.make_async_remote_copy(
                    src_ref=stage.at[i % 2, give_at],
                    dst_ref=blocks.at[take_rows, cols],
                    send_sem=give_sems.at[sem],
                    recv_sem=take_sems.at[sem],
                    device_id=sib,
                    device_id_type=MESH,
                )
            )
        return keeps, gives

    def weight_grad(g, which):
        def done(i):
            keeps, gives = chip_copies(which, i)
            for copy in keeps:
                copy.wait()
            for copy in gives:
                copy.wait_send()

        def body(i, carry):
            pl.when(i >= 2)(lambda: done(i - 2))
            rows = pl.ds(pl.multiple_of(i // slices * chunk, 128), chunk)
            cols = pl.ds(pl.multiple_of(i % slices * col_step, 128), col_step)
            stage[i % 2] = t_dot(x[:, rows], g[:, cols]).astype(BF16)
            keeps, gives = chip_copies(which, i)
            for copy in keeps + gives:
                copy.start()
            return carry

        lax.fori_loop(0, rounds, body, 0)
        done(rounds - 2)
        done(rounds - 1)

    def add_cores(which):
        first, second = keep_at_of[which] * chips * side, take_at_of[which] * chips * side

        def arrived(i, carry):
            for copy in chip_copies(which, i)[1]:
                copy.wait_recv()
            return carry

        lax.fori_loop(0, rounds, arrived, 0)
        unit = 16

        def body(i, carry):
            at = pl.ds(pl.multiple_of(first + i * unit, unit), unit)
            other = blocks[pl.ds(pl.multiple_of(second + i * unit, unit), unit), :]
            wu[at, :] = (wu[at, :].astype(F32) + other.astype(F32)).astype(BF16)
            return carry

        lax.fori_loop(0, chips * side // unit, body, 0)
        if inside_sum and which == 0:
            return None
        first_col = (which - 1 if inside_sum else which) * units
        copy = pltpu.make_async_copy(
            wu.at[pl.ds(first, chips * side)],
            grad_w.at[:, pl.ds(first_col, units)],
            sum_sems.at[which],
        )
        copy.start()
        return copy

    chip_copies_of_gate = []

    def gate_block(m, first, count):
        start = flip(ctx // 2, m) * side + first
        return wu.at[pl.ds(pl.multiple_of(start, 16), count)]

    def gate_diag():
        for k, to in enumerate((y_dev, x_dev)):
            copy = net.push(
                gate_block(3, k * side // 2, side // 2),
                got_diag.at[pl.ds(k * side // 2, side // 2)],
                to,
            )
            copy.start()
            chip_copies_of_gate.append(copy)

    def rows_loop(count, one):
        unit = 16

        def body(i, carry):
            one(i * unit, unit)
            return carry

        lax.fori_loop(0, count // unit, body, 0)

    def gate_near():
        for k, (to, got_from) in enumerate(((x_dev, got_x), (y_dev, got_y))):
            chip_copies_of_gate[k].wait_recv()
            start = flip(ctx // 2, 1 + k) * side + k * side // 2

            def one(first, unit):
                at = pl.ds(pl.multiple_of(start + first, unit), unit)
                other = got_diag[pl.ds(pl.multiple_of(k * side // 2 + first, unit), unit), :]
                wu[at, :] = (wu[at, :].astype(F32) + other.astype(F32)).astype(BF16)

            rows_loop(side // 2, one)
            copy = net.push(gate_block(1 + k, 0, side), got_from, to)
            copy.start()
            chip_copies_of_gate.append(copy)

    def gate_total():
        for copy in chip_copies_of_gate[2:]:
            copy.wait_recv()

        def one(first, unit):
            at = pl.ds(pl.multiple_of(first, unit), unit)
            own_at = pl.ds(pl.multiple_of(ctx // 2 * side + first, unit), unit)
            value = wu[own_at, :].astype(F32) + got_x[at, :].astype(F32)
            got_diag[at, :] = (value + got_y[at, :].astype(F32)).astype(BF16)

        rows_loop(side, one)
        copy = pltpu.make_async_copy(got_diag, gate_sum_out, sum_sems.at[0])
        copy.start()
        for other in chip_copies_of_gate:
            other.wait_send()
        copy.wait()

    @pl.when(inner)
    def _():
        far.wait_recv()
        add_to(2, 0)
        two_over.start()

    weight_grad(gg, 0)

    @pl.when(inner)
    def _():
        near.wait_recv()
        add_to(3, 1)
        three_over.start()
        two_over.wait_recv()
        add_to(1, 2)

    one_mate.start()
    gate_sum = add_cores(0)
    if inside_sum:
        gate_diag()
    weight_grad(gu, 1)
    if inside_sum:
        gate_near()
    load("hidden", hidden, gu)
    load("cot", cot, x)
    up_sum = add_cores(1)
    loads["cot"].wait()
    one_mate.wait_recv()
    pl.when(inner)(three_over.wait_recv)

    def norm_rows(i, scale_sum):
        at = pl.ds(pl.multiple_of(i * 16, 16), 16)
        grad = parts[0, at, :].astype(F32) + got[4, at, :].astype(F32)
        grad = grad + jnp.where(inner, got[3, at, :].astype(F32), 0.0)
        value = middle[at, :]
        r = inv_rms(value)
        scaled = grad * scale[1:2, :]
        lean = jnp.mean(scaled * value, -1, keepdims=True)
        total = x[at, :].astype(F32) + (r * scaled - value * (r * r * r * lean))
        grad_middle[at, :] = total
        mine[at, :] = total.astype(BF16)
        return scale_sum + jnp.sum(grad * value * r, 0, keepdims=True)

    grad_scale[...] = lax.fori_loop(0, own // 16, norm_rows, jnp.zeros((1, width), F32))
    dst = branch.at[pl.ds(pl.multiple_of((z % 2) * own, 16), own)]
    last = net.push(mine, dst, mate)
    last.start()
    local = pltpu.make_async_copy(mine, dst, own_sems.at[used])
    local.start()
    loads["hidden"].wait()
    up_sum.wait()
    weight_grad(gu, 2)
    down_sum = add_cores(2)
    one_mate.wait_send()

    @pl.when(inner)
    def _():
        two_over.wait_send()
        three_over.wait_send()

    @pl.when(jnp.logical_not(inner))
    def _():
        far.wait_send()
        near.wait_send()

    loads["wd"].wait()
    out_copies = []
    for m in order:
        span = pl.ds(m * own, own)
        for k in range(steps):
            part = pl.ds(k * step, step)
            parts[m, :, part] = dot_t(gu[span, :], wg[part, :]).astype(BF16)
        dst = ffn_near.at[m] if m < 2 else ffn_far.at[m - 2]
        copy = pltpu.make_async_copy(parts.at[m], dst, own_sems.at[used + 1 + m])
        copy.start()
        out_copies.append(copy)
    local.wait()
    if inside_sum:
        gate_total()
    else:
        gate_sum.wait()
    down_sum.wait()
    last.wait_recv()
    last.wait_send()
    for copy in out_copies:
        copy.wait()


def feed_forward_back(grad_gate, grad_up, gate_up_w, down_w, hidden, rows_in, middle, cot, scale):
    own, width = middle.shape
    count, units = hidden.shape
    block = 2 * width // lax.axis_size("ctx")
    chunk = block if block % 128 == 0 else 640
    inside_sum = lax.axis_size("ctx") == 8
    rounds = width // block * (units // 640)
    return pl.pallas_call(
        ffn_back_kernel,
        out_shape=[
            jax.ShapeDtypeStruct((width // 2, (2 if inside_sum else 3) * units), BF16),
            jax.ShapeDtypeStruct((block // 2, units), BF16),
            jax.ShapeDtypeStruct((2, own, width), BF16),
            jax.ShapeDtypeStruct((2, own, width), BF16),
            jax.ShapeDtypeStruct((own, width), F32),
            jax.ShapeDtypeStruct((2 * own, width), BF16),
            jax.ShapeDtypeStruct((1, width), F32),
        ],
        in_specs=[ANY] * 6 + [VMEM, ANY, VMEM],
        out_specs=[ANY, ANY, ANY, ANY, VMEM, ANY, VMEM],
        scratch_shapes=[
            pltpu.VMEM((count, units), BF16),
            pltpu.VMEM((count, units), BF16),
            pltpu.VMEM((width, units), BF16),
            pltpu.VMEM((width, units), BF16),
            pltpu.VMEM((count, width), BF16),
            pltpu.VMEM((4, own, width), BF16),
            pltpu.VMEM((5, own, width), BF16),
            pltpu.VMEM((2, chunk, 640), BF16),
            pltpu.VMEM((own, width), BF16),
            pltpu.VMEM((width, units), BF16),
            pltpu.VMEM((block // 2, units), BF16),
            pltpu.VMEM((block // 2, units), BF16),
            pltpu.VMEM((block // 2, units), BF16),
            pltpu.SemaphoreType.DMA((10,)),
            pltpu.SemaphoreType.DMA((10,)),
            pltpu.SemaphoreType.DMA((8 + 2 * (width // 512) + 9,)),
            pltpu.SemaphoreType.DMA((3 * rounds,)),
            pltpu.SemaphoreType.DMA((3 * rounds,)),
            pltpu.SemaphoreType.DMA((3 * rounds,)),
            pltpu.SemaphoreType.DMA((3,)),
        ],
        compiler_params=pltpu.CompilerParams(
            collective_id=5, has_side_effects=True, vmem_limit_bytes=62 * 1024 * 1024
        ),
        cost_estimate=takes(100),
        name="feed_forward_back",
    )(grad_gate, grad_up, gate_up_w, down_w, hidden, rows_in, middle, cot, scale)


def fold(ref, other):
    ref[...] = (ref[...].astype(F32) + other[...].astype(F32)).astype(BF16)


class KvSum:
    def __init__(self, net, parts, out, mine, got_sib, got_diag, got_x, got_y, got_z, give, sems):
        ctx, z = where_am_i()
        self.h, self.upper = z % 2, z // 2 == 1
        self.refs = (out, mine, got_sib, got_diag, got_x, got_y, got_z, give)
        x_dev, y_dev, sib = (flip(ctx, 2), z), (flip(ctx, 4), z), (flip(ctx, 1), z)
        self.load, self.over, self.diag, self.near = {}, {}, {}, {}
        for s in range(2):
            for i, m in enumerate((6, 2, 4, 0)):
                self.load[s, i] = pltpu.make_async_copy(
                    parts.at[s, flip(ctx, m)], mine.at[s, i], sems.at[4 * s + i]
                )
                self.over[s, i] = net.push(
                    parts.at[s, flip(flip(ctx, 1), m)], got_sib.at[s, i], sib
                )
            self.diag[s] = [
                net.push(mine.at[s, 0, 0], got_diag.at[s, 0], y_dev),
                net.push(mine.at[s, 0, 1], got_diag.at[s, 1], x_dev),
            ]
            self.near[s] = [
                net.push(mine.at[s, 1], got_x.at[s], x_dev),
                net.push(mine.at[s, 2], got_y.at[s], y_dev),
            ]
        self.to_mate = net.push(give.at[0], got_z.at[0], (ctx, flip(z, 1)))
        self.to_low = net.push(give.at[1], got_z.at[1], (ctx, flip(z, 2)))
        self.to_low_mate = net.push(give.at[2], got_z.at[2], (ctx, flip(z, 3)))

    def both(self, stage):
        stage(0)
        pl.when(self.upper)(lambda: stage(1))

    def start(self, s):
        for i in range(4):
            self.over[s, i].start()
            self.load[s, i].start()

    def chip_sums(self, s):
        mine, got_sib = self.refs[1:3]
        for i in range(4):
            self.load[s, i].wait()
            self.over[s, i].wait_recv()
            fold(mine.at[s, i], got_sib.at[s, i])
            if i == 0:
                for copy in self.diag[s]:
                    copy.start()

    def forward(self, s):
        mine, got_diag = self.refs[1], self.refs[3]
        for k in range(2):
            self.diag[s][k].wait_recv()
            fold(mine.at[s, 1 + k, k], got_diag.at[s, k])
            self.near[s][k].start()

    def total(self, s, kind):
        mine, got_x, got_y = self.refs[1], self.refs[4], self.refs[5]
        value = mine[s, 3, kind].astype(F32) + got_x[s, kind].astype(F32)
        return value + got_y[s, kind].astype(F32)

    def across(self):
        out, give, h = self.refs[0], self.refs[7], self.h
        for copy in self.near[0]:
            copy.wait_recv()

        @pl.when(jnp.logical_not(self.upper))
        def _():
            give[0] = self.total(0, 1 - h).astype(BF16)
            out[...] = self.total(0, h)

        @pl.when(self.upper)
        def _():
            give[1] = self.total(0, h).astype(BF16)
            give[2] = self.total(0, 1 - h).astype(BF16)
            self.to_low.start()
            self.to_low_mate.start()
            for copy in self.near[1]:
                copy.wait_recv()
            give[0] = self.total(1, 1 - h).astype(BF16)
            out[...] = self.total(1, h)

        self.to_mate.start()

    def finish(self):
        out, got_z = self.refs[0], self.refs[6]
        self.to_mate.wait_recv()
        out[...] += got_z[0].astype(F32)

        @pl.when(jnp.logical_not(self.upper))
        def _():
            self.to_low.wait_recv()
            self.to_low_mate.wait_recv()
            out[...] += got_z[1].astype(F32) + got_z[2].astype(F32)

        def sent(s):
            for i in range(4):
                self.over[s, i].wait_send()
            for copy in self.diag[s] + self.near[s]:
                copy.wait_send()

        self.both(sent)
        self.to_mate.wait_send()

        @pl.when(self.upper)
        def _():
            self.to_low.wait_send()
            self.to_low_mate.wait_send()

    @staticmethod
    def scratch(rows):
        block = (2, rows, HD)
        return [
            pltpu.VMEM((2, 4) + block, BF16),
            pltpu.VMEM((2, 4) + block, BF16),
            pltpu.VMEM((2, 2, rows, HD), BF16),
            pltpu.VMEM((2,) + block, BF16),
            pltpu.VMEM((2,) + block, BF16),
            pltpu.VMEM((3, rows, HD), BF16),
            pltpu.VMEM((3, rows, HD), BF16),
            pltpu.SemaphoreType.DMA((8,)),
        ]

    copies = 19


class WeightSum:
    def __init__(self, net, widths, parts, put, mine, got_sib, got_diag, got_x, got_y, got_z, total, sems):
        ctx, z = where_am_i()
        self.net, self.z = net, z
        self.ctx = ctx
        self.parts, self.put, self.sems = parts, put, sems
        self.refs = (mine, got_sib, got_diag, got_x, got_y, got_z, total)
        self.x_dev, self.y_dev, self.sib = (flip(ctx, 2), z), (flip(ctx, 4), z), (flip(ctx, 1), z)
        self.rows = mine.shape[1]
        self.copies = {}
        self.spans, col = [], 0
        for count in widths:
            self.spans.append(pl.ds(col, count))
            col += count

    def add_to(self, ref, other, count):
        step = 32

        def body(i, carry):
            at = pl.ds(pl.multiple_of(i * step, step), step)
            ref[at, :] = (ref[at, :].astype(F32) + other[at, :].astype(F32)).astype(BF16)
            return carry

        lax.fori_loop(0, count // step, body, 0)

    def start(self, g):
        mine, got_sib = self.refs[:2]
        span, rows, ctx = self.spans[g], self.rows, self.ctx

        def block_rows(source):
            return pl.ds(pl.multiple_of(source * rows, 16), rows)

        for i, m in enumerate((6, 2, 4, 0)):
            load = pltpu.make_async_copy(
                self.parts.at[block_rows(flip(ctx, m)), span],
                mine.at[i, :, span],
                self.sems.at[4 * g + i],
            )
            over = self.net.push(
                self.parts.at[block_rows(flip(flip(ctx, 1), m)), span],
                got_sib.at[i, :, span],
                self.sib,
            )
            load.start()
            over.start()
            self.copies[g, i] = (load, over)

    def chip_sums(self, g):
        mine, got_sib, got_diag = self.refs[:3]
        span, rows = self.spans[g], self.rows
        cut = rows // 2
        for i in range(4):
            load, over = self.copies[g, i]
            if load is not None:
                load.wait()
            over.wait_recv()
            self.add_to(mine.at[i, :, span], got_sib.at[i, :, span], rows)
            if i == 0:
                pair = []
                for k, to in enumerate((self.y_dev, self.x_dev)):
                    part = pl.ds(k * cut, cut)
                    pair.append(self.net.push(mine.at[0, part, span], got_diag.at[part, span], to))
                    pair[k].start()
                self.copies[g, "diag"] = pair

    def forward(self, g):
        mine, _, got_diag, got_x, got_y = self.refs[:5]
        span = self.spans[g]
        cut = self.rows // 2
        pair = []
        for k, (got, to) in enumerate(((got_x, self.x_dev), (got_y, self.y_dev))):
            part = pl.ds(k * cut, cut)
            self.copies[g, "diag"][k].wait_recv()
            self.add_to(mine.at[1 + k, part, span], got_diag.at[part, span], cut)
            pair.append(self.net.push(mine.at[1 + k, :, span], got.at[:, span], to))
            pair[k].start()
        self.copies[g, "near"] = pair

    def line(self, g):
        mine, _, _, got_x, got_y, got_z, total = self.refs
        span, rows, z = self.spans[g], self.rows, self.z
        unit = rows // 4
        for copy in self.copies[g, "near"]:
            copy.wait_recv()
        step = 16

        def body(i, carry):
            at = pl.ds(pl.multiple_of(i * step, step), step)
            value = mine[3, at, span].astype(F32) + got_x[at, span].astype(F32)
            total[at, span] = (value + got_y[at, span].astype(F32)).astype(BF16)
            return carry

        lax.fori_loop(0, rows // step, body, 0)
        sends = []
        for k, m in enumerate((1, 2, 3)):
            start_row = pl.multiple_of(flip(z, m) * unit, 16)
            copy = self.net.push(
                total.at[pl.ds(start_row, unit), span],
                got_z.at[k, :, span],
                (self.ctx, flip(z, m)),
            )
            copy.start()
            sends.append(copy)
        self.copies[g, "line"] = sends

    def finish(self, g):
        got_z, total = self.refs[5:]
        span, unit = self.spans[g], self.rows // 4
        for copy in self.copies[g, "line"]:
            copy.wait_recv()
        own_row = pl.multiple_of(self.z * unit, 16)
        h = self.z % 2
        own_cols = total[pl.ds(own_row, unit), span].astype(F32) + got_z[1, :, span].astype(F32)
        self.put(h, span, own_cols)
        self.put(1 - h, span, got_z[0, :, span].astype(F32) + got_z[2, :, span].astype(F32))
        for i in range(4):
            self.copies[g, i][1].wait_send()
        for name in ("diag", "near", "line"):
            for copy in self.copies[g, name]:
                copy.wait_send()

    @staticmethod
    def scratch(rows, shard, columns, groups):
        return [
            pltpu.VMEM((4, rows, columns), BF16),
            pltpu.VMEM((4, rows, columns), BF16),
            pltpu.VMEM((rows, columns), BF16),
            pltpu.VMEM((rows, columns), BF16),
            pltpu.VMEM((rows, columns), BF16),
            pltpu.VMEM((3, shard, columns), BF16),
            pltpu.VMEM((rows, columns), BF16),
            pltpu.SemaphoreType.DMA((4 * groups,)),
        ]


def everyone():
    ctx, z = where_am_i()
    return [(ctx, flip(z, m)) for m in (1, 2, 3)] + [(flip(ctx, m), z) for m in (1, 2, 4)]


def first_sums_kernel(kv_parts, near_parts, far_parts, come, kv_out, one_out, three_out, *scratch):
    ctx, z = where_am_i()
    kv_scratch, scratch = scratch[:8], scratch[8:]
    parts, got, send_sems, recv_sems, own_sems = scratch
    net = Net(send_sems, recv_sems)
    greet(everyone())
    beyond = (ctx, flip(z, 3))
    inner = (z == 1) | (z == 2)
    kv = KvSum(net, kv_parts, kv_out, *kv_scratch)
    two_over = net.push(parts.at[1], got, beyond)
    loads = []
    sources = (near_parts.at[1], far_parts.at[0], far_parts.at[1], come.at[0], come.at[1])
    for m, src in enumerate(sources):
        loads.append(pltpu.make_async_copy(src, parts.at[m], own_sems.at[m]))
        loads[m].start()
    kv.both(kv.start)
    for copy in loads:
        copy.wait()

    @pl.when(inner)
    def _():
        fold(parts.at[1], parts.at[4])
        two_over.start()
        fold(parts.at[2], parts.at[3])

    three = pltpu.make_async_copy(parts.at[2], three_out, own_sems.at[0])
    three.start()
    kv.both(kv.chip_sums)
    kv.both(kv.forward)
    kv.across()

    @pl.when(inner)
    def _():
        two_over.wait_recv()
        fold(parts.at[0], got)
        two_over.wait_send()

    one = pltpu.make_async_copy(parts.at[0], one_out, own_sems.at[1])
    one.start()
    kv.finish()
    three.wait()
    one.wait()


def plain_axes(shard):
    return lax.axis_size("ctx") != 8 or lax.axis_size("fsdp") != 4 or shard % 16


def plain_weight_sum(parts):
    z = lax.axis_index("fsdp")
    empty = jnp.zeros_like(parts)
    both = jnp.where(z % 2 == 0, jnp.stack([parts, empty]), jnp.stack([empty, parts]))
    summed = lax.psum_scatter(both, "ctx", scatter_dimension=1, tiled=True)
    return lax.psum_scatter(summed, "fsdp", scatter_dimension=1, tiled=True).astype(F32)


def first_sums(kv_parts, near_parts, far_parts, middle, shard):
    total, _, rows, _ = kv_parts.shape
    ctx_total = total // 2
    kv_parts = kv_parts.reshape(2, ctx_total, 2, rows, HD)
    own, width = middle.shape
    if plain_axes(shard):
        flat = kv_parts.transpose(0, 2, 1, 3, 4).reshape(4 * ctx_total * rows, HD)
        z_sum = lax.psum_scatter(flat, "fsdp", scatter_dimension=0, tiled=True)
        kv = lax.psum_scatter(z_sum, "ctx", scatter_dimension=0, tiled=True).astype(F32)
        out = middle + near_parts[0].astype(F32)
        for m in (1, 2, 3):
            part = near_parts[m] if m < 2 else far_parts[m - 2]
            out = out + swap(part, "fsdp", m).astype(F32)
        return kv, out.astype(BF16)
    copies = KvSum.copies + 1
    come = lax.ppermute(far_parts, "fsdp", [(0, 1), (3, 2)])
    line = jax.ShapeDtypeStruct((own, width), BF16)
    kv, one, three = pl.pallas_call(
        first_sums_kernel,
        out_shape=[jax.ShapeDtypeStruct((rows, HD), F32), line, line],
        in_specs=[ANY] * 4,
        out_specs=[VMEM, ANY, ANY],
        scratch_shapes=KvSum.scratch(rows)
        + [
            pltpu.VMEM((5, own, width), BF16),
            pltpu.VMEM((own, width), BF16),
            pltpu.SemaphoreType.DMA((copies,)),
            pltpu.SemaphoreType.DMA((copies,)),
            pltpu.SemaphoreType.DMA((5,)),
        ],
        compiler_params=pltpu.CompilerParams(
            collective_id=2, has_side_effects=True, vmem_limit_bytes=60 * 1024 * 1024
        ),
        cost_estimate=takes(45),
        name="first_sums",
    )(kv_parts, near_parts, far_parts, come)
    out = middle + near_parts[0].astype(F32) + swap(one, "fsdp", 1).astype(F32)
    out = out + lax.ppermute(three, "fsdp", [(1, 2), (2, 1)]).astype(F32)
    return kv, out.astype(BF16)


def last_sums_kernel(
    widths, out_widths, out_parts, w_qkv, grad_q, grad_kv, cosine, sine, normed, tokens, scale, grad_middle, ffn_scale_grad, *refs
):
    ctx, z = where_am_i()
    q_out, k_out, v_out, o_out, grad_tokens, scales = refs[:6]
    w_scratch, o_scratch, scratch = refs[6:14], refs[14:22], refs[22:]
    give_w, product, w, grads, grad_own, give, got, scale_got, send_sems, recv_sems, own_sems = scratch
    h, core, chip = z % 2, ctx % 2, ctx // 2
    net = Net(send_sems, recv_sems)
    own, width = tokens.shape
    step = 512
    steps = width // step
    loads = []
    for k in range(steps):
        part = pl.ds(k * step, step)
        loads.append(pltpu.make_async_copy(w_qkv.at[part], w.at[part], own_sems.at[k]))
        loads[k].start()
    greet(everyone() + [(flip(ctx, m), z) for m in (3, 5, 6, 7)])

    def put_out(which, span, value):
        o_out[:, pl.ds(pl.multiple_of(which * QW + span.start, 128), span.size)] = value

    outs = WeightSum(net, out_widths, out_parts, put_out, *o_scratch)
    outs.start(0)
    outs.start(1)
    grads[:, :QW] = grad_q[...]
    front, back = grad_kv[:, : HD // 2], grad_kv[:, HD // 2 :]
    c, s = cosine[...], sine[...]
    grads[:, QW : QW + HD // 2] = (front * c + back * s).astype(BF16)
    grads[:, QW + HD // 2 :] = (back * c - front * s).astype(BF16)

    def put(which, span, value):
        if span.start < QW:
            q_out[:, pl.ds(pl.multiple_of(which * QW + span.start, 128), span.size)] = value
            return

        @pl.when(which == 0)
        def _():
            k_out[...] = value

        @pl.when(which == 1)
        def _():
            v_out[...] = value

    weights = WeightSum(net, widths, None, put, *w_scratch)
    mine, got_sib = w_scratch[:2]
    side = mine.shape[1]

    def produce(g):
        span = weights.spans[g]
        for i, m in enumerate((3, 1, 2, 0)):
            cols = pl.ds(pl.multiple_of(flip(chip, m) * 2 * side, 128), 2 * side)
            product[:, : span.size] = t_dot(normed[:, cols], grads[:, span]).astype(BF16)
            keep_at = pl.ds(pl.multiple_of(core * side, 16), side)
            give_at = pl.ds(pl.multiple_of((1 - core) * side, 16), side)
            mine[i, :, span] = product[keep_at, : span.size]
            give_w[i, :, span] = product[give_at, : span.size]
            over = net.push(give_w.at[i, :, span], got_sib.at[i, :, span], weights.sib)
            over.start()
            weights.copies[g, i] = (None, over)

    outs.chip_sums(0)
    outs.chip_sums(1)
    outs.forward(0)
    other_grads = grads[pl.ds(pl.multiple_of((1 - h) * own, 16), own), :]
    crossing = []
    for k in range(steps):
        loads[k].wait()
        give[k] = dot_t(other_grads, w[pl.ds(k * step, step), :]).astype(BF16)
        crossing.append(net.push(give.at[k], got.at[k], (ctx, flip(z, 1))))
        crossing[k].start()
    line_mates = [(ctx, flip(z, m)) for m in (1, 2, 3)]
    plane_mates = [(flip(ctx, m), z) for m in range(1, 8)]
    trade = []

    def trade_send(mates):
        for to in mates:
            trade.append(net.push(scales, scale_got.at[len(trade)], to))
            trade[-1].start()

    def trade_add(first, count):
        for k in range(first, first + count):
            trade[k].wait()
        for k in range(first, first + count):
            scales[...] += scale_got[k]

    def own_part():
        own_grads = grads[pl.ds(pl.multiple_of(h * own, 16), own), :]
        for k in range(steps):
            part = pl.ds(k * step, step)
            grad_own[:, part] = dot_t(own_grads, w[part, :])

    def norm_part():
        value = tokens[...].astype(F32)
        for k in range(steps):
            crossing[k].wait_recv()
            grad_own[:, pl.ds(k * step, step)] += got[k].astype(F32)
        grad = grad_own[...]
        r = inv_rms(value)
        scaled = grad * scale[0:1, :]
        lean = jnp.mean(scaled * value, -1, keepdims=True)
        grad_tokens[...] = grad_middle[...] + (r * scaled - value * (r * r * r * lean))
        rows = [jnp.sum(grad * value * r, 0, keepdims=True), ffn_scale_grad[...]]
        quarter = width // 4
        for i in range(8):
            scales[i : i + 1, :] = rows[i // 4][:, i % 4 * quarter : (i % 4 + 1) * quarter]
        trade_send(line_mates)

    outs.forward(1)
    produce(0)
    weights.chip_sums(0)
    produce(1)
    weights.chip_sums(1)
    weights.forward(0)
    own_part()
    norm_part()
    produce(2)
    weights.chip_sums(2)
    weights.forward(1)
    outs.line(0)
    outs.line(1)
    trade_add(0, 3)
    trade_send(plane_mates)
    weights.forward(2)
    weights.line(0)
    outs.finish(0)
    outs.finish(1)
    weights.line(1)
    trade_add(3, 7)
    weights.line(2)
    weights.finish(0)
    weights.finish(1)
    weights.finish(2)
    for copy in crossing:
        copy.wait_send()


def last_sums(out_parts, w_qkv, grad_q, grad_kv, cosine, sine, normed, tokens, scale, grad_middle, ffn_scale_grad, shard):
    own, width = tokens.shape
    columns = w_qkv.shape[1]
    if plain_axes(shard):
        h = lax.axis_index("fsdp") % 2
        front, back = grad_kv[:, : HD // 2], grad_kv[:, HD // 2 :]
        c, s = cosine, sine
        grad_kv = jnp.concatenate([front * c + back * s, back * c - front * s], 1).astype(BF16)
        grads = jnp.concatenate([grad_q, grad_kv], 1)
        both = plain_weight_sum(t_dot(normed, grads).astype(BF16))
        grad_rows = dot_t(grads, w_qkv)
        other = swap(half(grad_rows, 1 - h).astype(BF16), "fsdp", 1).astype(F32)
        grad, scale_grad = norm_back(tokens.astype(F32), scale[:1], half(grad_rows, h) + other)
        scales = jnp.concatenate([scale_grad[None], ffn_scale_grad])
        queries = jnp.concatenate([both[0, :, :QW], both[1, :, :QW]], 1)
        scales = lax.psum(scales, ("ctx", "fsdp"))
        outs = plain_weight_sum(out_parts)
        outs = jnp.concatenate([outs[0], outs[1]], 1)
        return queries, both[0, :, QW:], both[1, :, QW:], outs, grad_middle + grad, scales
    block = 4 * shard
    rows = normed.shape[0]
    widths = (QW // 2, QW // 2, HD)
    steps = width // 512
    out_widths = (QW // 2, QW // 2)
    copies = 11 * (len(widths) + len(out_widths)) + steps + 10
    *weights, scales = pl.pallas_call(
        functools.partial(last_sums_kernel, widths, out_widths),
        out_shape=[
            jax.ShapeDtypeStruct((shard, 2 * QW), F32),
            jax.ShapeDtypeStruct((shard, HD), F32),
            jax.ShapeDtypeStruct((shard, HD), F32),
            jax.ShapeDtypeStruct((shard, 2 * QW), F32),
            jax.ShapeDtypeStruct((own, width), F32),
            jax.ShapeDtypeStruct((8, width // 4), F32),
        ],
        in_specs=[ANY] * 2 + [VMEM] * 9,
        out_specs=[VMEM] * 6,
        scratch_shapes=WeightSum.scratch(block, shard, columns, len(widths))
        + WeightSum.scratch(block, shard, QW, len(out_widths))
        + [
            pltpu.VMEM((4, block, columns), BF16),
            pltpu.VMEM((2 * block, QW // 2), BF16),
            pltpu.VMEM((width, columns), BF16),
            pltpu.VMEM((rows, columns), BF16),
            pltpu.VMEM((own, width), F32),
            pltpu.VMEM((steps, own, 512), BF16),
            pltpu.VMEM((steps, own, 512), BF16),
            pltpu.VMEM((10, 8, width // 4), F32),
            pltpu.SemaphoreType.DMA((copies,)),
            pltpu.SemaphoreType.DMA((copies,)),
            pltpu.SemaphoreType.DMA((steps,)),
        ],
        compiler_params=pltpu.CompilerParams(
            collective_id=4, has_side_effects=True, vmem_limit_bytes=60 * 1024 * 1024
        ),
        cost_estimate=takes(60),
        name="last_sums",
    )(out_parts, w_qkv, grad_q, grad_kv, cosine, sine, normed, tokens, scale, grad_middle, ffn_scale_grad)
    return *weights, scales.reshape(2, width)


def local(
    tokens,
    lengths,
    block_place,
    gain_attn,
    w_query,
    w_key,
    w_value,
    w_out,
    gain_ffn,
    w_gate,
    w_up,
    w_down,
    cotangent,
):
    own_rows, width = tokens.shape
    rows = 2 * own_rows
    ctx_total = lax.axis_size("ctx")
    ctx, z = where_am_i()
    h, pair = z % 2, z // 2
    shard = w_query.shape[0]
    reach = -(-WIN // rows)

    def place_of(stored):
        hit = jnp.arange(block_place.shape[0])[None, :] == stored[:, None]
        return jnp.sum(jnp.where(hit, block_place[None, :], 0), 1)

    own_pos = place_of((2 * ctx + pair)[None])[0]
    query_at = own_pos * rows + jnp.arange(rows, dtype=jnp.int32)
    passed = query_at[:, None] >= jnp.cumsum(lengths)[None, :]
    doc_start = jnp.sum(jnp.where(passed, lengths[None, :], 0), 1)
    rel_pos = query_at - doc_start
    window_start = (own_pos - reach) * rows
    lowest = jnp.maximum(doc_start, query_at - WIN + 1) - window_start
    lowest = jnp.broadcast_to(lowest[:, None], (rows, 128)).astype(jnp.int32)
    holders = jnp.arange(ctx_total)
    held = jnp.concatenate([place_of(2 * holders), place_of(2 * holders + 1)])
    held = jnp.where((pair == 1) | (jnp.arange(2 * ctx_total) < ctx_total), held, -1000)
    want = own_pos - reach + jnp.arange(reach + 1)
    hit = held[None, :] == want[:, None]
    numbers = jnp.arange(2 * ctx_total)
    own_index = pair * ctx_total + ctx
    place = jnp.where(jnp.any(hit, 1), jnp.sum(jnp.where(hit, numbers, 0), 1), own_index)
    place = place.astype(jnp.int32)
    goes = held - (own_pos - reach)
    goes = jnp.where((goes >= 0) & (goes <= reach), goes, reach + 1).astype(jnp.int32)
    half_dim = HD // 2
    frequency = jnp.exp(jnp.arange(half_dim, dtype=F32) * (-jnp.log(10000.0) / half_dim))
    angles = rel_pos.astype(F32)[:, None] * frequency
    cosine, sine = jnp.cos(angles), jnp.sin(angles)
    q_scale = HD ** (-0.5)
    kv_cosine, kv_sine = jnp.where(h == 0, cosine, 1.0), jnp.where(h == 0, sine, 0.0)
    cosine = jnp.stack([cosine * q_scale, kv_cosine])
    sine = jnp.stack([sine * q_scale, kv_sine])

    gate_up_shard = jnp.concatenate([w_gate, w_up], 1)
    down_shard = w_down.T
    w_qkv, w_o, gains, rows_in, cot_one, cot_three = gather_weights(
        w_query, w_key, w_value, w_out, gain_attn, gain_ffn, tokens, cotangent
    )
    w_qkv, w_o, gate_up_shard, down_shard = lax.optimization_barrier(
        (w_qkv, w_o, gate_up_shard, down_shard)
    )
    gate_up_w = lax.all_gather(gate_up_shard, "ctx", axis=0, tiled=True)
    down_w = lax.all_gather(down_shard, "ctx", axis=0, tiled=True)
    normed, queries, kv, scales = project(rows_in, gains, shard, cosine, sine, w_qkv)
    inner = (z == 1) | (z == 2)
    across = lax.ppermute(cot_one, "fsdp", [(1, 2), (2, 1)])
    outward = lax.ppermute(cot_three, "fsdp", [(1, 0), (2, 3)])
    store = gather_kv(kv)
    store, across, outward = lax.optimization_barrier((store, across, outward))
    farther = lax.ppermute(across, "fsdp", [(1, 0), (2, 3)])
    prob, attended = attend(place, lowest, queries, store, reach)
    attended, farther = lax.optimization_barrier((attended, farther))
    cots = (
        cotangent,
        cot_one,
        jnp.where(inner, across, outward),
        jnp.where(inner, cot_three, farther),
    )
    middle, own_normed, mate_normed, beyond_normed = out_norm(attended, tokens, scales, w_o)

    ffn_in, hidden, active, sloped = feed_forward(
        own_normed, mate_normed, beyond_normed, gate_up_w
    )
    ffn_cot, grad_gate, grad_up = feed_forward_grad(cots, down_w, active, sloped)

    w_parts, gate_sum, near_parts, far_parts, grad_middle, grad_branch, grad_ffn_scale = feed_forward_back(
        grad_gate, grad_up, gate_up_w, down_w, hidden, ffn_in, middle, ffn_cot, scales
    )
    same_core = [list(range(core, ctx_total, 2)) for core in range(2)]
    ffn_sums = lax.psum_scatter(
        w_parts, "ctx", scatter_dimension=0, axis_index_groups=same_core, tiled=True
    )
    units = w_gate.shape[1]
    if ctx_total != 8:
        gate_sum, ffn_sums = ffn_sums[:, :units], ffn_sums[:, units:]
    grad_gate_w = gate_sum.astype(F32)
    grad_up_w = ffn_sums[:, :units].astype(F32)
    grad_down = ffn_sums[:, units:].astype(F32).T
    grad_out_part = t_dot(grad_branch, attended).astype(BF16)

    grad_q, kv_parts = attend_back(
        place, goes, prob, queries, grad_branch, w_o, cosine, sine, store, reach
    )
    grad_kv, output = first_sums(kv_parts, near_parts, far_parts, middle, shard)
    grad_query_w, grad_key_w, grad_value_w, grad_out_w, grad_tokens, scale_sums = last_sums(
        grad_out_part,
        w_qkv,
        grad_q,
        grad_kv,
        kv_cosine,
        kv_sine,
        normed,
        tokens,
        scales,
        grad_middle,
        grad_ffn_scale,
        shard,
    )
    first_col = (ctx * lax.axis_size("fsdp") + z) * shard
    scale_sums = lax.dynamic_slice_in_dim(scale_sums, first_col, shard, 1)
    return (
        output,
        grad_tokens,
        scale_sums[0],
        grad_query_w,
        grad_key_w,
        grad_value_w,
        grad_out_w.T,
        scale_sums[1],
        grad_gate_w,
        grad_up_w,
        grad_down,
    )


def solution(mesh):
    in_specs = (
        P(("ctx", "fsdp"), None),
        P(),
        P(),
        P(("ctx", "fsdp")),
        P(("ctx", "fsdp"), None),
        P(("ctx", "fsdp"), None),
        P(("ctx", "fsdp"), None),
        P(None, ("ctx", "fsdp")),
        P(("ctx", "fsdp")),
        P("ctx", "fsdp"),
        P("ctx", "fsdp"),
        P("fsdp", "ctx"),
        P(("ctx", "fsdp"), None),
    )
    out_specs = (
        P(("ctx", "fsdp"), None),
        P(("ctx", "fsdp"), None),
        P(("ctx", "fsdp")),
        P(("ctx", "fsdp"), None),
        P(("ctx", "fsdp"), None),
        P(("ctx", "fsdp"), None),
        P(None, ("ctx", "fsdp")),
        P(("ctx", "fsdp")),
        P("ctx", "fsdp"),
        P("ctx", "fsdp"),
        P("fsdp", "ctx"),
    )
    return jax.shard_map(local, mesh=mesh, in_specs=in_specs, out_specs=out_specs, check_vma=False)
```

```python
import functools

import jax
import jax.numpy as jnp
from jax import lax
from jax.experimental import pallas as pl
from jax.experimental.pallas import tpu as pltpu
from jax.sharding import PartitionSpec as P

H = 10
HD = 256
WIN = 2048
EPS = 1e-06
F32 = jnp.float32
BF16 = jnp.bfloat16
MESH = pl.DeviceIdType.MESH
ANY = pl.BlockSpec(memory_space=pl.ANY)
VMEM = pl.BlockSpec(memory_space=pltpu.VMEM)
HEADS = H // 2
QW = HEADS * HD
VMEM_LIMIT = 56 * 1024 * 1024
FAR = -1e30


def swap(x, axis, mask):
    return lax.ppermute(x, axis, [(i, i ^ mask) for i in range(lax.axis_size(axis))])


def join(own, other, bit, axis):
    return jnp.where(
        bit == 0,
        jnp.concatenate([own, other], axis),
        jnp.concatenate([other, own], axis),
    )


def half(x, which, axis=0):
    size = x.shape[axis] // 2
    return lax.dynamic_slice_in_dim(x, which * size, size, axis)


def dot(a, b):
    return jnp.dot(a, b, preferred_element_type=F32)


def dot_t(a, b):
    return lax.dot_general(a, b, (((1,), (1,)), ((), ())), preferred_element_type=F32)


def t_dot(a, b):
    return lax.dot_general(a, b, (((0,), (0,)), ((), ())), preferred_element_type=F32)


def inv_rms(x):
    return lax.rsqrt(jnp.mean(x * x, -1, keepdims=True) + EPS)


def norm_back(x, scale, grad):
    r = inv_rms(x)
    scaled = grad * scale
    lean = jnp.mean(scaled * x, -1, keepdims=True)
    return r * scaled - x * (r * r * r * lean), jnp.sum(grad * x * r, 0)


def takes(us):
    return pl.CostEstimate(flops=int(us * 1e9), bytes_accessed=0, transcendentals=0)


class Net:
    def __init__(self, send_sems, recv_sems):
        self.send_sems, self.recv_sems, self.used = send_sems, recv_sems, 0

    def push(self, src, dst, to):
        copy = pltpu.make_async_remote_copy(
            src_ref=src,
            dst_ref=dst,
            send_sem=self.send_sems.at[self.used],
            recv_sem=self.recv_sems.at[self.used],
            device_id=to,
            device_id_type=MESH,
        )
        self.used += 1
        return copy


def greet(partners):
    barrier = pltpu.get_barrier_semaphore()
    for to in partners:
        pl.semaphore_signal(barrier, inc=1, device_id=to, device_id_type=MESH)
    pl.semaphore_wait(barrier, len(partners))


def flip(x, mask):
    for bit in (1, 2, 4):
        if mask & bit:
            x = x + bit - 2 * bit * ((x // bit) % 2)
    return x


def where_am_i():
    return lax.axis_index("ctx"), lax.axis_index("fsdp")


def gather_kernel(
    qkv, out, gain, tokens, cot, w_qkv, w_out, gains, rows, cot_one, cot_three, send_sems, recv_sems, own_sems
):
    ctx, z = where_am_i()
    net = Net(send_sems, recv_sems)
    greet([(ctx, flip(z, m)) for m in (1, 2, 3)] + [(flip(ctx, m), z) for m in (1, 2, 4)])
    shard = qkv.shape[0]
    qkv_cols, half_cols = QW + HD, QW // 2

    def cols_of(ref, stride, first, count):
        return lambda h: ref.at[:, pl.ds(pl.multiple_of(h * stride + first, 128), count)]

    groups = [
        (cols_of(qkv, qkv_cols, QW, HD), w_qkv, shard, QW, HD),
        (lambda h: gain, gains, 8, 0, 128),
        (cols_of(qkv, qkv_cols, 0, half_cols), w_qkv, shard, 0, half_cols),
        (cols_of(qkv, qkv_cols, half_cols, half_cols), w_qkv, shard, half_cols, half_cols),
        (cols_of(out, QW, 0, half_cols), w_out, shard, 0, half_cols),
        (cols_of(out, QW, half_cols, half_cols), w_out, shard, half_cols, half_cols),
    ]

    def at(group, source, first, count):
        src, ref, unit, col, cols = group
        start = pl.multiple_of(source * 4 * unit + first, 8 if unit == 8 else 16)
        return ref.at[pl.ds(start, count), pl.ds(col, cols)]

    lines, locals_, sent = [], [], []

    def push(src, dst, to):
        copy = net.push(src, dst, to)
        copy.start()
        sent.append(copy)
        return copy

    token_rows = tokens.shape[0]
    token_dst = rows.at[pl.ds(pl.multiple_of((z % 2) * token_rows, 16), token_rows)]
    for i, group in enumerate(groups):
        unit = group[2]
        dst = at(group, ctx, z * unit, unit)
        lines.append([push(group[0](flip(z, m) % 2), dst, (ctx, flip(z, m))) for m in (2, 3, 1)])
        local = pltpu.make_async_copy(group[0](z % 2), dst, own_sems.at[i])
        local.start()
        locals_.append(local)
        if i == len(groups) - 1:
            token_copy = push(tokens, token_dst, (ctx, flip(z, 1)))
            token_local = pltpu.make_async_copy(tokens, token_dst, own_sems.at[len(groups)])
            token_local.start()
    mate, beyond = (ctx, flip(z, 1)), (ctx, flip(z, 3))
    inner = (z == 1) | (z == 2)
    cot_mate = push(cot, cot_one, mate)
    cot_beyond = net.push(cot, cot_three, beyond)

    @pl.when(inner)
    def _():
        cot_beyond.start()

    by_x, by_y, last = {}, {}, []
    diag = {}
    x_dev, y_dev, sib = (flip(ctx, 2), z), (flip(ctx, 4), z), (flip(ctx, 1), z)

    def same(group, source, first, count, to):
        return push(at(group, source, first, count), at(group, source, first, count), to)

    def spread_own(i):
        group = groups[i]
        locals_[i].wait()
        for copy in lines[i]:
            copy.wait_recv()
        count = 4 * group[2]
        by_x[i] = same(group, ctx, 0, count, x_dev)
        by_y[i] = same(group, ctx, 0, count, y_dev)
        last.append(same(group, ctx, 0, count, sib))

    def spread_near(i):
        group = groups[i]
        count = 4 * group[2]
        by_x[i].wait_recv()
        top = same(group, flip(ctx, 2), 0, count // 2, y_dev)
        last.append(same(group, flip(ctx, 2), 0, count, sib))
        by_y[i].wait_recv()
        low = same(group, flip(ctx, 4), count // 2, count // 2, x_dev)
        last.append(same(group, flip(ctx, 4), 0, count, sib))
        diag[i] = (top, low)

    def spread_far(i):
        group = groups[i]
        count = 4 * group[2]
        for k in range(2):
            diag[i][k].wait_recv()
            last.append(same(group, flip(ctx, 6), k * count // 2, count // 2, sib))

    for i in range(len(groups) + 2):
        if i < len(groups):
            spread_own(i)
        if 0 <= i - 1 < len(groups):
            spread_near(i - 1)
        if 0 <= i - 2 < len(groups):
            spread_far(i - 2)
    token_local.wait()
    token_copy.wait_recv()
    cot_mate.wait_recv()

    @pl.when(inner)
    def _():
        cot_beyond.wait_recv()
        cot_beyond.wait_send()

    for copy in last:
        copy.wait_recv()
    for copy in sent:
        copy.wait_send()


def gather_weights(w_query, w_key, w_value, w_out, gain_attn, gain_ffn, tokens, cotangent):
    shard, width = w_query.shape
    z = lax.axis_index("fsdp")
    ctx_total = lax.axis_size("ctx")
    pieces = []
    for h in range(2):
        pieces += [w_query[:, h * QW : (h + 1) * QW], (w_key, w_value)[h]]
    qkv = jnp.concatenate(pieces, 1)
    out = w_out.T
    gain = jnp.stack([gain_attn, gain_ffn]).astype(F32)
    gain = jnp.pad(gain, ((0, 6), (0, 128 - shard)))
    if ctx_total != 8 or lax.axis_size("fsdp") != 4 or shard % 16:
        both = ("ctx", "fsdp")
        full = lax.all_gather(qkv, both, axis=0, tiled=True)
        full_out = lax.all_gather(out, both, axis=0, tiled=True)
        return (
            half(full, z % 2, 1),
            half(full_out, z % 2, 1),
            lax.all_gather(gain, both, axis=0, tiled=True),
            join(tokens, swap(tokens, "fsdp", 1), z % 2, 0),
            swap(cotangent, "fsdp", 1),
            swap(cotangent, "fsdp", 3),
        )
    devices = 4 * ctx_total
    w_qkv, w_o, gains, rows, cot_one, cot_three = pl.pallas_call(
        gather_kernel,
        out_shape=[
            jax.ShapeDtypeStruct((width, QW + HD), BF16),
            jax.ShapeDtypeStruct((width, QW), BF16),
            jax.ShapeDtypeStruct((8 * devices, 128), F32),
            jax.ShapeDtypeStruct((2 * tokens.shape[0], width), BF16),
            jax.ShapeDtypeStruct(tokens.shape, BF16),
            jax.ShapeDtypeStruct(tokens.shape, BF16),
        ],
        in_specs=[ANY] * 5,
        out_specs=[ANY] * 6,
        scratch_shapes=[
            pltpu.SemaphoreType.DMA((75,)),
            pltpu.SemaphoreType.DMA((75,)),
            pltpu.SemaphoreType.DMA((7,)),
        ],
        compiler_params=pltpu.CompilerParams(collective_id=0, has_side_effects=True),
        cost_estimate=takes(80),
        name="gather_weights",
    )(qkv, out, gain, tokens, cotangent)
    return w_qkv, w_o, gains, rows, cot_one, cot_three


def proj_kernel(shard, rows, gains, cosine, sine, w, normed, out, kv, scales):
    @pl.when(pl.program_id(0) == 0)
    def _():
        for i in range(gains.shape[0] // 8):
            scales[:, i * shard : (i + 1) * shard] = gains[8 * i : 8 * i + 8, :shard]
        x = rows[...].astype(F32)
        normed[...] = (x * inv_rms(x) * scales[0:1, :]).astype(BF16)

    value = dot(normed[...], w[...])
    front, back = value[:, : HD // 2], value[:, HD // 2 :]
    c, s = cosine[0], sine[0]

    def put(ref):
        ref[:, : HD // 2] = (front * c - back * s).astype(BF16)
        ref[:, HD // 2 :] = (back * c + front * s).astype(BF16)

    pl.when(pl.program_id(0) < HEADS)(lambda: put(out))
    pl.when(pl.program_id(0) == HEADS)(lambda: put(kv))


def project(rows, gains, shard, cosine, sine, w):
    count, width = rows.shape
    steps = HEADS + 1
    fixed = lambda i: (0, 0)
    table = pl.BlockSpec((1, count, HD // 2), lambda i: (i // HEADS, 0, 0))
    return pl.pallas_call(
        functools.partial(proj_kernel, shard),
        grid=(steps,),
        out_shape=[
            jax.ShapeDtypeStruct((count, width), BF16),
            jax.ShapeDtypeStruct((count, QW), BF16),
            jax.ShapeDtypeStruct((count, HD), BF16),
            jax.ShapeDtypeStruct((8, width), F32),
        ],
        in_specs=[
            pl.BlockSpec((count, width), fixed),
            pl.BlockSpec(gains.shape, fixed),
            table,
            table,
            pl.BlockSpec((width, HD), lambda i: (0, i)),
        ],
        out_specs=[
            pl.BlockSpec((count, width), fixed),
            pl.BlockSpec((count, HD), lambda i: (0, jnp.minimum(i, HEADS - 1))),
            pl.BlockSpec((count, HD), fixed),
            pl.BlockSpec((8, width), fixed),
        ],
        compiler_params=pltpu.CompilerParams(vmem_limit_bytes=VMEM_LIMIT),
        cost_estimate=takes(10),
        name="project",
    )(rows, gains, cosine, sine, w)


def kv_gather_kernel(kv, store, send_sems, recv_sems, own_sem):
    ctx, z = where_am_i()
    net = Net(send_sems, recv_sems)
    h, pair = z % 2, z // 2
    greet([(ctx, flip(z, m)) for m in (1, 2)] + [(flip(ctx, m), z) for m in (1, 2, 4)])
    local = pltpu.make_async_copy(kv, store.at[pair, ctx, h], own_sem)
    local.start()
    mate, across = (ctx, flip(z, 1)), (ctx, flip(z, 2))
    x_dev, y_dev, sib = (flip(ctx, 2), z), (flip(ctx, 4), z), (flip(ctx, 1), z)
    own = net.push(kv, store.at[pair, ctx, h], mate)
    own.start()
    low = net.push(kv, store.at[0, ctx, h], across)
    low_mate = net.push(store.at[0, ctx, h], store.at[0, ctx, h], mate)

    @pl.when(pair == 0)
    def _():
        low.start()

    local.wait()
    own.wait_recv()

    class Set:
        def __init__(self, which):
            def same(source, kind, to):
                if kind is None:
                    ref = store.at[which, source]
                else:
                    ref = store.at[which, source, kind]
                return net.push(ref, ref, to)

            self.near = [same(ctx, None, x_dev), same(ctx, None, y_dev), same(ctx, None, sib)]
            x_ctx, y_ctx, d_ctx = flip(ctx, 2), flip(ctx, 4), flip(ctx, 6)
            self.after_x = [same(x_ctx, 0, y_dev), same(x_ctx, None, sib)]
            self.after_y = [same(y_ctx, 1, x_dev), same(y_ctx, None, sib)]
            self.after_d = [same(d_ctx, 0, sib), same(d_ctx, 1, sib)]

        def first(self):
            for copy in self.near:
                copy.start()

        def second(self):
            self.near[0].wait_recv()
            for copy in self.after_x:
                copy.start()
            self.near[1].wait_recv()
            for copy in self.after_y:
                copy.start()

        def third(self):
            self.after_x[0].wait_recv()
            self.after_d[0].start()
            self.after_y[0].wait_recv()
            self.after_d[1].start()

        def finish(self):
            for copy in [self.near[2], self.after_x[1], self.after_y[1]] + self.after_d:
                copy.wait_recv()
            for copy in self.near + self.after_x + self.after_y + self.after_d:
                copy.wait_send()

    mine = Set(pair)
    lower = Set(0)
    mine.first()

    @pl.when(pair == 1)
    def _():
        low.wait_recv()
        low_mate.start()
        low_mate.wait_recv()
        lower.first()

    mine.second()

    @pl.when(pair == 1)
    def _():
        lower.second()

    mine.third()

    @pl.when(pair == 1)
    def _():
        lower.third()

    mine.finish()
    own.wait_send()

    @pl.when(pair == 1)
    def _():
        lower.finish()
        low_mate.wait_send()

    @pl.when(pair == 0)
    def _():
        low.wait_send()


def gather_kv(kv):
    ctx_total = lax.axis_size("ctx")
    rows = kv.shape[0]
    if ctx_total != 8 or lax.axis_size("fsdp") != 4:
        every = lax.all_gather(kv, ("fsdp", "ctx"), axis=0, tiled=False)
        every = every.reshape(2, 2, ctx_total, rows, HD).transpose(0, 2, 1, 3, 4)
        return every.reshape(2 * ctx_total, 2, rows, HD)
    store = pl.pallas_call(
        kv_gather_kernel,
        out_shape=jax.ShapeDtypeStruct((2, ctx_total, 2, rows, HD), BF16),
        in_specs=[ANY],
        out_specs=ANY,
        scratch_shapes=[
            pltpu.SemaphoreType.DMA((21,)),
            pltpu.SemaphoreType.DMA((21,)),
            pltpu.SemaphoreType.DMA,
        ],
        compiler_params=pltpu.CompilerParams(collective_id=1, has_side_effects=True),
        cost_estimate=takes(30),
        name="gather_kv",
    )(kv)
    return store.reshape(2 * ctx_total, 2, rows, HD)


def chunks(rows, reach):
    skip = (reach * rows - WIN) // 128 * 128
    parts, at = [], 0
    for r in range(reach + 1):
        begin = max(0, skip - r * rows)
        if begin < rows:
            parts.append((r, begin, at, rows - begin))
            at += rows - begin
    return parts, at


def attend_kernel(reach, place, lowest, q, *refs):
    keys, values = refs[: reach + 1], refs[reach + 1 : 2 * reach + 2]
    prob, out, scores = refs[2 * reach + 2 :]
    rows = q.shape[0]
    parts, total = chunks(rows, reach)
    low = lowest[:, :1]
    peak = None
    for r, begin, at, count in parts:
        s = dot_t(q[...], keys[r][0, 0, begin:, :])
        key_at = lax.broadcasted_iota(jnp.int32, (rows, count), 1) + (r * rows + begin)
        visible = key_at >= low
        if r == reach:
            query_at = lax.broadcasted_iota(jnp.int32, (rows, count), 0) + reach * rows
            visible = visible & (key_at <= query_at)
        s = jnp.where(visible, s, FAR)
        scores[:, at : at + count] = s
        top = jnp.max(s, -1, keepdims=True)
        peak = top if peak is None else jnp.maximum(peak, top)
    weight_sum = jnp.zeros_like(peak)
    for r, begin, at, count in parts:
        e = jnp.exp(scores[:, at : at + count] - peak)
        scores[:, at : at + count] = e
        weight_sum = weight_sum + jnp.sum(e, -1, keepdims=True)
    share = 1.0 / weight_sum
    mixed = jnp.zeros((rows, HD), F32)
    for r, begin, at, count in parts:
        p = (scores[:, at : at + count] * share).astype(BF16)
        prob[0, :, at : at + count] = p
        mixed = mixed + dot(p, values[r][0, 0, begin:, :])
    out[...] = mixed.astype(BF16)


def window_specs(rows, reach):
    def spec(r, kind):
        return pl.BlockSpec((1, 1, rows, HD), lambda i, place: (place[r], kind, 0, 0))

    return [spec(r, kind) for kind in range(2) for r in range(reach + 1)]


def attend(place, lowest, qkv, store, reach):
    rows = qkv.shape[0]
    total = chunks(rows, reach)[1]
    column = pl.BlockSpec((rows, HD), lambda i, place: (0, i))
    return pl.pallas_call(
        functools.partial(attend_kernel, reach),
        grid_spec=pltpu.PrefetchScalarGridSpec(
            num_scalar_prefetch=1,
            grid=(HEADS,),
            in_specs=[pl.BlockSpec((rows, 128), lambda i, place: (0, 0)), column]
            + window_specs(rows, reach),
            out_specs=[
                pl.BlockSpec((1, rows, total), lambda i, place: (i, 0, 0)),
                column,
            ],
            scratch_shapes=[pltpu.VMEM((rows, total), F32)],
        ),
        out_shape=[
            jax.ShapeDtypeStruct((HEADS, rows, total), BF16),
            jax.ShapeDtypeStruct((rows, QW), BF16),
        ],
        compiler_params=pltpu.CompilerParams(vmem_limit_bytes=VMEM_LIMIT),
        cost_estimate=takes(21),
        name="attend",
    )(place, lowest, qkv, *([store] * (2 * reach + 2)))


def attend_back_kernel(reach, place, goes, prob, q, branch, w_out, cosine, sine, *refs):
    keys, values = refs[: reach + 1], refs[reach + 1 : 2 * reach + 2]
    grad_q, store, grad_probs, sums, blocks, sems = refs[2 * reach + 2 :]
    rows = q.shape[0]
    parts, total = chunks(rows, reach)
    head = pl.program_id(0)

    @pl.when(head == 0)
    def _():
        sums[...] = jnp.zeros_like(sums)

    grad_rows = dot(branch[...], w_out[...]).astype(BF16)
    query_rows = q[...]
    lean = jnp.zeros((rows, 1), F32)
    for r, begin, at, count in parts:
        dp = dot_t(grad_rows, values[r][0, 0, begin:, :])
        p = prob[0, :, at : at + count]
        grad_probs[:, at : at + count] = dp
        lean = lean + jnp.sum(dp * p.astype(F32), -1, keepdims=True)
        sums[1, at : at + count, :] += t_dot(p, grad_rows)
    turned = jnp.zeros((rows, HD), F32)
    for r, begin, at, count in parts:
        p = prob[0, :, at : at + count].astype(F32)
        ds = (p * (grad_probs[:, at : at + count] - lean)).astype(BF16)
        turned = turned + dot(ds, keys[r][0, 0, begin:, :])
        sums[0, at : at + count, :] += t_dot(ds, query_rows)
    front, back = turned[:, : HD // 2], turned[:, HD // 2 :]
    c, s = cosine[0], sine[0]
    grad_q[:, : HD // 2] = (front * c + back * s).astype(BF16)
    grad_q[:, HD // 2 :] = (back * c - front * s).astype(BF16)

    @pl.when(head == pl.num_programs(0) - 1)
    def _():
        blocks[reach + 1] = jnp.zeros((2, rows, HD), BF16)
        for r, begin, at, count in parts:
            for kind in range(2):
                if begin > 0:
                    blocks[r, kind, :begin, :] = jnp.zeros((begin, HD), BF16)
                blocks[r, kind, begin:, :] = sums[kind, at : at + count, :].astype(BF16)
        for r in range(parts[0][0]):
            blocks[r] = jnp.zeros((2, rows, HD), BF16)
        count = store.shape[0]

        def copy(i):
            return pltpu.make_async_copy(blocks.at[goes[i]], store.at[i], sems.at[i])

        for i in range(count):
            copy(i).start()
        for i in range(count):
            copy(i).wait()


def attend_back(place, goes, prob, qkv, branch, w_out, cosine, sine, store, reach):
    rows = qkv.shape[0]
    total = chunks(rows, reach)[1]
    column = pl.BlockSpec((rows, HD), lambda i, place, goes: (0, i))
    table = pl.BlockSpec((1, rows, HD // 2), lambda i, place, goes: (0, 0, 0))

    def spec(r, kind):
        return pl.BlockSpec((1, 1, rows, HD), lambda i, place, goes: (place[r], kind, 0, 0))

    return pl.pallas_call(
        functools.partial(attend_back_kernel, reach),
        grid_spec=pltpu.PrefetchScalarGridSpec(
            num_scalar_prefetch=2,
            grid=(HEADS,),
            in_specs=[
                pl.BlockSpec((1, rows, total), lambda i, place, goes: (i, 0, 0)),
                column,
                pl.BlockSpec(branch.shape, lambda i, place, goes: (0, 0)),
                pl.BlockSpec((w_out.shape[0], HD), lambda i, place, goes: (0, i)),
                table,
                table,
            ]
            + [spec(r, kind) for kind in range(2) for r in range(reach + 1)],
            out_specs=[column, ANY],
            scratch_shapes=[
                pltpu.VMEM((rows, total), F32),
                pltpu.VMEM((2, total, HD), F32),
                pltpu.VMEM((reach + 2, 2, rows, HD), BF16),
                pltpu.SemaphoreType.DMA((store.shape[0],)),
            ],
        ),
        out_shape=[
            jax.ShapeDtypeStruct((rows, QW), BF16),
            jax.ShapeDtypeStruct(store.shape, BF16),
        ],
        compiler_params=pltpu.CompilerParams(vmem_limit_bytes=VMEM_LIMIT),
        cost_estimate=takes(24),
        name="attend_back",
    )(place, goes, prob, qkv, branch, w_out, cosine, sine, *([store] * (2 * reach + 2)))


def out_norm_kernel(
    attended, tokens, scale, w_out, middle, own_rows, mate_rows, beyond_rows, wo, other, got, mine, send_sems, recv_sems, own_sems
):
    ctx, z = where_am_i()
    h = z % 2
    net = Net(send_sems, recv_sems)
    mate, beyond = (ctx, flip(z, 1)), (ctx, flip(z, 3))
    own, width = tokens.shape
    step = 512
    steps = width // step
    loads = []
    for k in range(steps):
        part = pl.ds(k * step, step)
        loads.append(pltpu.make_async_copy(w_out.at[part], wo.at[part], own_sems.at[k]))
        loads[k].start()
    greet([mate, beyond])
    keep = attended[pl.ds(pl.multiple_of(h * own, 16), own), :]
    give = attended[pl.ds(pl.multiple_of((1 - h) * own, 16), own), :]
    crossing = []
    for k in range(steps):
        part = pl.ds(k * step, step)
        loads[k].wait()
        other[k] = dot_t(give, wo[part, :]).astype(BF16)
        crossing.append(net.push(other.at[k], got.at[k], mate))
        crossing[k].start()
    for k in range(steps):
        part = pl.ds(k * step, step)
        middle[:, part] = tokens[:, part].astype(F32) + dot_t(keep, wo[part, :])
    square = jnp.zeros((own, 1), F32)
    for k in range(steps):
        part = pl.ds(k * step, step)
        crossing[k].wait_recv()
        value = middle[:, part] + got[k].astype(F32)
        middle[:, part] = value
        square = square + jnp.sum(value * value, -1, keepdims=True)
    r = lax.rsqrt(square / width + EPS)
    for k in range(steps):
        part = pl.ds(k * step, step)
        mine[:, part] = (middle[:, part] * r * scale[1:2, part]).astype(BF16)
    to_mate = net.push(mine, mate_rows, mate)
    to_beyond = net.push(mine, beyond_rows, beyond)
    to_mate.start()
    inner = (z == 1) | (z == 2)
    pl.when(inner)(to_beyond.start)
    local = pltpu.make_async_copy(mine, own_rows, own_sems.at[steps])
    local.start()
    for k in range(steps):
        crossing[k].wait_send()
    local.wait()
    to_mate.wait()
    pl.when(inner)(to_beyond.wait)


def out_norm(attended, tokens, scale, w_out):
    own, width = tokens.shape
    line = jax.ShapeDtypeStruct((own, width), BF16)
    return pl.pallas_call(
        out_norm_kernel,
        out_shape=[jax.ShapeDtypeStruct((own, width), F32), line, line, line],
        in_specs=[VMEM] * 3 + [ANY],
        out_specs=[VMEM] + [ANY] * 3,
        scratch_shapes=[
            pltpu.VMEM(w_out.shape, BF16),
            pltpu.VMEM((width // 512, own, 512), BF16),
            pltpu.VMEM((width // 512, own, 512), BF16),
            pltpu.VMEM((own, width), BF16),
            pltpu.SemaphoreType.DMA((width // 512 + 2,)),
            pltpu.SemaphoreType.DMA((width // 512 + 2,)),
            pltpu.SemaphoreType.DMA((width // 512 + 1,)),
        ],
        compiler_params=pltpu.CompilerParams(
            collective_id=3, has_side_effects=True, vmem_limit_bytes=VMEM_LIMIT
        ),
        cost_estimate=takes(55),
        name="out_norm",
    )(attended, tokens, scale, w_out)


def ffn_kernel(
    own_rows,
    mate_rows,
    beyond_rows,
    gate_up_w,
    rows_out,
    hidden_out,
    active_out,
    sloped_out,
    wg,
    wu,
    x,
    hidden,
    active,
    sloped,
    send_sems,
    recv_sems,
    own_sems,
    out_sems,
):
    ctx, z = where_am_i()
    net = Net(send_sems, recv_sems)
    mate, beyond = (ctx, flip(z, 1)), (ctx, flip(z, 3))
    own, width = own_rows.shape
    units = wg.shape[1]
    spans = [pl.ds(c, min(512, units - c)) for c in range(0, units, 512)]
    count = len(spans)
    inner = (z == 1) | (z == 2)
    pulls = []
    for m, src in ((0, own_rows), (1, mate_rows)):
        pulls.append(
            pltpu.make_async_copy(src, x.at[pl.ds(m * own, own)], own_sems.at[2 * count + m])
        )
        pulls[m].start()
    loads = []
    for c in range(count):
        span = spans[c]
        pair = []
        for k, dst in enumerate((wg, wu)):
            src = gate_up_w.at[:, pl.ds(k * units + span.start, span.size)]
            pair.append(pltpu.make_async_copy(src, dst.at[:, span], own_sems.at[2 * c + k]))
            pair[k].start()
        loads.append(pair)
    greet([mate, beyond])
    one_beyond = net.push(mate_rows, x.at[pl.ds(2 * own, own)], beyond)
    three_mate = net.push(beyond_rows, x.at[pl.ds(2 * own, own)], mate)
    two_mate = net.push(x.at[pl.ds(2 * own, own)], x.at[pl.ds(3 * own, own)], mate)
    three_local = pltpu.make_async_copy(
        beyond_rows, x.at[pl.ds(3 * own, own)], own_sems.at[2 * count + 2]
    )

    @pl.when(inner)
    def _():
        one_beyond.start()
        three_mate.start()
        three_local.start()

    def work(first, rows, c, ready):
        if ready is not None:
            for copy in ready:
                copy.wait()
        span = spans[c]
        at = pl.ds(first, rows)
        gate = dot(x[at, :], wg[:, span])
        up = dot(x[at, :], wu[:, span])
        root, cubic = 0.7978845608028654, 0.044715
        square = gate * gate
        bent = jnp.tanh(root * (gate + cubic * square * gate))
        value = 0.5 * gate * (1.0 + bent)
        slope = 0.5 * (1.0 + bent) + 0.5 * gate * (1.0 - bent * bent) * root * (
            1.0 + 3.0 * cubic * square
        )
        hidden[at, span] = (value * up).astype(BF16)
        active[at, span] = value.astype(BF16)
        sloped[at, span] = (slope * up).astype(BF16)

    outs = []

    def flush(m):
        at = pl.ds(m * own, own)
        pairs = ((hidden, hidden_out), (active, active_out), (sloped, sloped_out), (x, rows_out))
        for k, (src, dst) in enumerate(pairs):
            copy = pltpu.make_async_copy(src.at[at], dst.at[at], out_sems.at[4 * m + k])
            copy.start()
            outs.append(copy)

    for copy in pulls:
        copy.wait()
    for c in range(count):
        work(0, 2 * own, c, loads[c])
    flush(0)
    flush(1)

    @pl.when(inner)
    def _():
        one_beyond.wait_recv()
        two_mate.start()

    @pl.when(jnp.logical_not(inner))
    def _():
        three_mate.wait_recv()

    for c in range(count):
        work(2 * own, own, c, None)
    flush(2)

    @pl.when(inner)
    def _():
        three_local.wait()

    @pl.when(jnp.logical_not(inner))
    def _():
        two_mate.wait_recv()

    for c in range(count):
        work(3 * own, own, c, None)
    flush(3)

    @pl.when(inner)
    def _():
        for copy in (one_beyond, three_mate, two_mate):
            copy.wait_send()

    for copy in outs:
        copy.wait()


def feed_forward(own_rows, mate_rows, beyond_rows, gate_up_w):
    own, width = own_rows.shape
    units = gate_up_w.shape[1] // 2
    count = 4 * own
    inner_shape = jax.ShapeDtypeStruct((count, units), BF16)
    return pl.pallas_call(
        ffn_kernel,
        out_shape=[jax.ShapeDtypeStruct((count, width), BF16)] + [inner_shape] * 3,
        in_specs=[ANY] * 4,
        out_specs=[ANY] * 4,
        scratch_shapes=[
            pltpu.VMEM((width, units), BF16),
            pltpu.VMEM((width, units), BF16),
            pltpu.VMEM((count, width), BF16),
            pltpu.VMEM((count, units), BF16),
            pltpu.VMEM((count, units), BF16),
            pltpu.VMEM((count, units), BF16),
            pltpu.SemaphoreType.DMA((3,)),
            pltpu.SemaphoreType.DMA((3,)),
            pltpu.SemaphoreType.DMA((2 * (-(-units // 512)) + 3,)),
            pltpu.SemaphoreType.DMA((16,)),
        ],
        compiler_params=pltpu.CompilerParams(
            collective_id=6, has_side_effects=True, vmem_limit_bytes=VMEM_LIMIT
        ),
        cost_estimate=takes(52),
        name="feed_forward",
    )(own_rows, mate_rows, beyond_rows, gate_up_w)


def ffn_grad_kernel(c0, c1, c2, c3, down_w, active, sloped, cot, grad_gate, grad_up):
    own = c0.shape[0]

    @pl.when(pl.program_id(0) == 0)
    def _():
        for m, piece in enumerate((c0, c1, c2, c3)):
            cot[m * own : (m + 1) * own, :] = piece[...]

    grad = dot(cot[...], down_w[...])
    grad_gate[...] = (sloped[...].astype(F32) * grad).astype(BF16)
    grad_up[...] = (active[...].astype(F32) * grad).astype(BF16)


def ffn_specs(count, width, units):
    step = 512
    whole = pl.BlockSpec((count, width), lambda i: (0, 0))
    weight = pl.BlockSpec((width, step), lambda i: (0, i))
    column = pl.BlockSpec((count, step), lambda i: (0, i))
    return -(-units // step), whole, weight, column


def feed_forward_grad(cots, down_w, active, sloped):
    own, width = cots[0].shape
    count, units = active.shape
    steps, whole, weight, column = ffn_specs(count, width, units)
    piece = pl.BlockSpec((own, width), lambda i: (0, 0))
    return pl.pallas_call(
        ffn_grad_kernel,
        grid=(steps,),
        out_shape=[jax.ShapeDtypeStruct((count, width), BF16)]
        + [jax.ShapeDtypeStruct((count, units), BF16)] * 2,
        in_specs=[piece] * 4 + [weight, column, column],
        out_specs=[whole, column, column],
        compiler_params=pltpu.CompilerParams(vmem_limit_bytes=VMEM_LIMIT),
        cost_estimate=takes(15),
        name="feed_forward_grad",
    )(*cots, down_w, active, sloped)


def ffn_back_kernel(
    grad_gate,
    grad_up,
    gate_up_w,
    down_w,
    hidden,
    rows_in,
    middle,
    cot,
    scale,
    grad_w,
    gate_sum_out,
    ffn_near,
    ffn_far,
    grad_middle,
    branch,
    grad_scale,
    gg,
    gu,
    wg,
    wu,
    x,
    parts,
    got,
    stage,
    mine,
    blocks,
    got_diag,
    got_x,
    got_y,
    send_sems,
    recv_sems,
    own_sems,
    stage_sems,
    give_sems,
    take_sems,
    sum_sems,
):
    ctx, z = where_am_i()
    net = Net(send_sems, recv_sems)
    mate, beyond = (ctx, flip(z, 1)), (ctx, flip(z, 3))
    x_dev, y_dev = (flip(ctx, 2), z), (flip(ctx, 4), z)
    inside_sum = lax.axis_size("ctx") == 8
    greet([mate, beyond, (flip(ctx, 1), z)] + ([x_dev, y_dev] if inside_sum else []))
    inner = (z == 1) | (z == 2)
    own, width = middle.shape
    units = gg.shape[1]
    step = 512
    steps = width // step
    order = (3, 2, 1, 0)
    loads = {}
    used = 0

    def load(name, src, dst):
        nonlocal used
        loads[name] = pltpu.make_async_copy(src, dst, own_sems.at[used])
        loads[name].start()
        used += 1

    for k in range(steps):
        if k < 4:
            m = order[k]
            span = pl.ds(m * own, own)
            load(("gg", m), grad_gate.at[span], gg.at[span])
            load(("gu", m), grad_up.at[span], gu.at[span])
        part = pl.ds(k * step, step)
        load(("wg", k), gate_up_w.at[part, pl.ds(0, units)], wg.at[part])
        load(("wu", k), gate_up_w.at[part, pl.ds(units, units)], wu.at[part])
    load("x", rows_in, x)

    far = net.push(parts.at[3], got.at[0], mate)
    near = net.push(parts.at[2], got.at[1], mate)
    two_over = net.push(parts.at[2], got.at[2], beyond)
    three_over = net.push(parts.at[3], got.at[3], beyond)
    one_mate = net.push(parts.at[1], got.at[4], mate)

    def make(m):
        span = pl.ds(m * own, own)
        loads["gg", m].wait()
        loads["gu", m].wait()
        for k in range(steps):
            part = pl.ds(k * step, step)
            if m == 3:
                loads["wg", k].wait()
                loads["wu", k].wait()
            value = dot_t(gg[span, :], wg[part, :]) + dot_t(gu[span, :], wu[part, :])
            parts[m, :, part] = value.astype(BF16)

    def add_to(m, k):
        parts[m] = (parts[m].astype(F32) + got[k].astype(F32)).astype(BF16)

    make(3)
    pl.when(jnp.logical_not(inner))(far.start)
    make(2)
    pl.when(jnp.logical_not(inner))(near.start)
    make(1)
    make(0)
    load("wd", down_w, wg)
    loads["x"].wait()

    block = 2 * width // lax.axis_size("ctx")
    chips = width // block
    chunk = stage.shape[1]
    sib = (flip(ctx, 1), z)
    core = ctx % 2
    side = block // 2
    first_cols = stage.shape[2]
    slices = ((0, first_cols), (first_cols, units - first_cols))
    inside = chunk // block
    rounds = width // chunk
    keep_at_of, take_at_of = (0, 1, 1), (0, 1, 0)

    def chip_copies(which, i, n):
        cols = pl.ds(*slices[n])
        used_cols = pl.ds(0, slices[n][1])
        keeps, gives = [], []
        for part in range(inside):
            k = i * inside + part
            sem = (which * chips + k) * 2 + n
            keep_rows = pl.ds(pl.multiple_of((keep_at_of[which] * chips + k) * side, 16), side)
            take_rows = pl.ds(pl.multiple_of((take_at_of[which] * chips + k) * side, 16), side)
            mine_at = pl.ds(pl.multiple_of(part * block + core * side, 16), side)
            give_at = pl.ds(pl.multiple_of(part * block + (1 - core) * side, 16), side)
            keeps.append(
                pltpu.make_async_copy(
                    stage.at[n, mine_at, used_cols], wu.at[keep_rows, cols], stage_sems.at[sem]
                )
            )
            gives.append(
                pltpu.make_async_remote_copy(
                    src_ref=stage.at[n, give_at, used_cols],
                    dst_ref=blocks.at[take_rows, cols],
                    send_sem=give_sems.at[sem],
                    recv_sem=take_sems.at[sem],
                    device_id=sib,
                    device_id_type=MESH,
                )
            )
        return keeps, gives

    def weight_grad(g, which):
        def done(i, n):
            keeps, gives = chip_copies(which, i, n)
            for copy in keeps:
                copy.wait()
            for copy in gives:
                copy.wait_send()

        def body(i, carry):
            rows = pl.ds(pl.multiple_of(i * chunk, 128), chunk)
            for n in range(2):
                pl.when(i >= 1)(lambda: done(i - 1, n))
                cols = pl.ds(*slices[n])
                stage[n, :, : slices[n][1]] = t_dot(x[:, rows], g[:, cols]).astype(BF16)
                keeps, gives = chip_copies(which, i, n)
                for copy in keeps + gives:
                    copy.start()
            return carry

        lax.fori_loop(0, rounds, body, 0)
        done(rounds - 1, 0)
        done(rounds - 1, 1)

    def add_cores(which):
        first, second = keep_at_of[which] * chips * side, take_at_of[which] * chips * side

        def arrived(i, carry):
            for n in range(2):
                for copy in chip_copies(which, i, n)[1]:
                    copy.wait_recv()
            return carry

        lax.fori_loop(0, rounds, arrived, 0)
        unit = 16

        def body(i, carry):
            at = pl.ds(pl.multiple_of(first + i * unit, unit), unit)
            other = blocks[pl.ds(pl.multiple_of(second + i * unit, unit), unit), :]
            wu[at, :] = (wu[at, :].astype(F32) + other.astype(F32)).astype(BF16)
            return carry

        lax.fori_loop(0, chips * side // unit, body, 0)
        if inside_sum and which == 0:
            return None
        first_col = (which - 1 if inside_sum else which) * units
        copy = pltpu.make_async_copy(
            wu.at[pl.ds(first, chips * side)],
            grad_w.at[:, pl.ds(first_col, units)],
            sum_sems.at[which],
        )
        copy.start()
        return copy

    chip_copies_of_gate = []

    def gate_block(m, first, count):
        start = flip(ctx // 2, m) * side + first
        return wu.at[pl.ds(pl.multiple_of(start, 16), count)]

    def gate_diag():
        for k, to in enumerate((y_dev, x_dev)):
            copy = net.push(
                gate_block(3, k * side // 2, side // 2),
                got_diag.at[pl.ds(k * side // 2, side // 2)],
                to,
            )
            copy.start()
            chip_copies_of_gate.append(copy)

    def rows_loop(count, one):
        unit = 16

        def body(i, carry):
            one(i * unit, unit)
            return carry

        lax.fori_loop(0, count // unit, body, 0)

    def gate_near():
        for k, (to, got_from) in enumerate(((x_dev, got_x), (y_dev, got_y))):
            chip_copies_of_gate[k].wait_recv()
            start = flip(ctx // 2, 1 + k) * side + k * side // 2

            def one(first, unit):
                at = pl.ds(pl.multiple_of(start + first, unit), unit)
                other = got_diag[pl.ds(pl.multiple_of(k * side // 2 + first, unit), unit), :]
                wu[at, :] = (wu[at, :].astype(F32) + other.astype(F32)).astype(BF16)

            rows_loop(side // 2, one)
            copy = net.push(gate_block(1 + k, 0, side), got_from, to)
            copy.start()
            chip_copies_of_gate.append(copy)

    def gate_total():
        for copy in chip_copies_of_gate[2:]:
            copy.wait_recv()

        def one(first, unit):
            at = pl.ds(pl.multiple_of(first, unit), unit)
            own_at = pl.ds(pl.multiple_of(ctx // 2 * side + first, unit), unit)
            value = wu[own_at, :].astype(F32) + got_x[at, :].astype(F32)
            got_diag[at, :] = (value + got_y[at, :].astype(F32)).astype(BF16)

        rows_loop(side, one)
        copy = pltpu.make_async_copy(got_diag, gate_sum_out, sum_sems.at[0])
        copy.start()
        for other in chip_copies_of_gate:
            other.wait_send()
        copy.wait()

    @pl.when(inner)
    def _():
        far.wait_recv()
        add_to(2, 0)
        two_over.start()

    weight_grad(gg, 0)
    gate_sum = add_cores(0)
    if inside_sum:
        gate_diag()

    @pl.when(inner)
    def _():
        near.wait_recv()
        add_to(3, 1)
        three_over.start()
        two_over.wait_recv()
        add_to(1, 2)

    one_mate.start()
    weight_grad(gu, 1)
    if inside_sum:
        gate_near()
    load("hidden", hidden, gu)
    load("cot", cot, x)
    up_sum = add_cores(1)
    loads["cot"].wait()
    one_mate.wait_recv()
    pl.when(inner)(three_over.wait_recv)

    def norm_rows(i, scale_sum):
        at = pl.ds(pl.multiple_of(i * 16, 16), 16)
        grad = parts[0, at, :].astype(F32) + got[4, at, :].astype(F32)
        grad = grad + jnp.where(inner, got[3, at, :].astype(F32), 0.0)
        value = middle[at, :]
        r = inv_rms(value)
        scaled = grad * scale[1:2, :]
        lean = jnp.mean(scaled * value, -1, keepdims=True)
        total = x[at, :].astype(F32) + (r * scaled - value * (r * r * r * lean))
        grad_middle[at, :] = total
        mine[at, :] = total.astype(BF16)
        return scale_sum + jnp.sum(grad * value * r, 0, keepdims=True)

    grad_scale[...] = lax.fori_loop(0, own // 16, norm_rows, jnp.zeros((1, width), F32))
    dst = branch.at[pl.ds(pl.multiple_of((z % 2) * own, 16), own)]
    last = net.push(mine, dst, mate)
    last.start()
    local = pltpu.make_async_copy(mine, dst, own_sems.at[used])
    local.start()
    loads["hidden"].wait()
    up_sum.wait()
    weight_grad(gu, 2)
    down_sum = add_cores(2)
    one_mate.wait_send()

    @pl.when(inner)
    def _():
        two_over.wait_send()
        three_over.wait_send()

    @pl.when(jnp.logical_not(inner))
    def _():
        far.wait_send()
        near.wait_send()

    loads["wd"].wait()
    out_copies = []
    for m in order:
        span = pl.ds(m * own, own)
        for k in range(steps):
            part = pl.ds(k * step, step)
            parts[m, :, part] = dot_t(gu[span, :], wg[part, :]).astype(BF16)
        dst = ffn_near.at[m] if m < 2 else ffn_far.at[m - 2]
        copy = pltpu.make_async_copy(parts.at[m], dst, own_sems.at[used + 1 + m])
        copy.start()
        out_copies.append(copy)
    local.wait()
    if inside_sum:
        gate_total()
    else:
        gate_sum.wait()
    down_sum.wait()
    last.wait_recv()
    last.wait_send()
    for copy in out_copies:
        copy.wait()


def feed_forward_back(grad_gate, grad_up, gate_up_w, down_w, hidden, rows_in, middle, cot, scale):
    own, width = middle.shape
    count, units = hidden.shape
    block = 2 * width // lax.axis_size("ctx")
    chunk = block if block % 128 == 0 else 640
    inside_sum = lax.axis_size("ctx") == 8
    rounds = width // block * 2
    return pl.pallas_call(
        ffn_back_kernel,
        out_shape=[
            jax.ShapeDtypeStruct((width // 2, (2 if inside_sum else 3) * units), BF16),
            jax.ShapeDtypeStruct((block // 2, units), BF16),
            jax.ShapeDtypeStruct((2, own, width), BF16),
            jax.ShapeDtypeStruct((2, own, width), BF16),
            jax.ShapeDtypeStruct((own, width), F32),
            jax.ShapeDtypeStruct((2 * own, width), BF16),
            jax.ShapeDtypeStruct((1, width), F32),
        ],
        in_specs=[ANY] * 6 + [VMEM, ANY, VMEM],
        out_specs=[ANY, ANY, ANY, ANY, VMEM, ANY, VMEM],
        scratch_shapes=[
            pltpu.VMEM((count, units), BF16),
            pltpu.VMEM((count, units), BF16),
            pltpu.VMEM((width, units), BF16),
            pltpu.VMEM((width, units), BF16),
            pltpu.VMEM((count, width), BF16),
            pltpu.VMEM((4, own, width), BF16),
            pltpu.VMEM((5, own, width), BF16),
            pltpu.VMEM((2, chunk, -(-units // 256) * 128), BF16),
            pltpu.VMEM((own, width), BF16),
            pltpu.VMEM((width, units), BF16),
            pltpu.VMEM((block // 2, units), BF16),
            pltpu.VMEM((block // 2, units), BF16),
            pltpu.VMEM((block // 2, units), BF16),
            pltpu.SemaphoreType.DMA((10,)),
            pltpu.SemaphoreType.DMA((10,)),
            pltpu.SemaphoreType.DMA((8 + 2 * (width // 512) + 9,)),
            pltpu.SemaphoreType.DMA((3 * rounds,)),
            pltpu.SemaphoreType.DMA((3 * rounds,)),
            pltpu.SemaphoreType.DMA((3 * rounds,)),
            pltpu.SemaphoreType.DMA((3,)),
        ],
        compiler_params=pltpu.CompilerParams(
            collective_id=5, has_side_effects=True, vmem_limit_bytes=62 * 1024 * 1024
        ),
        cost_estimate=takes(100),
        name="feed_forward_back",
    )(grad_gate, grad_up, gate_up_w, down_w, hidden, rows_in, middle, cot, scale)


def fold(ref, other):
    ref[...] = (ref[...].astype(F32) + other[...].astype(F32)).astype(BF16)


class KvSum:
    def __init__(self, net, parts, out, mine, got_sib, got_diag, got_x, got_y, got_z, give, sems):
        ctx, z = where_am_i()
        self.h, self.upper = z % 2, z // 2 == 1
        self.refs = (out, mine, got_sib, got_diag, got_x, got_y, got_z, give)
        x_dev, y_dev, sib = (flip(ctx, 2), z), (flip(ctx, 4), z), (flip(ctx, 1), z)
        self.load, self.over, self.diag, self.near = {}, {}, {}, {}
        for s in range(2):
            for i, m in enumerate((6, 2, 4, 0)):
                self.load[s, i] = pltpu.make_async_copy(
                    parts.at[s, flip(ctx, m)], mine.at[s, i], sems.at[4 * s + i]
                )
                self.over[s, i] = net.push(
                    parts.at[s, flip(flip(ctx, 1), m)], got_sib.at[s, i], sib
                )
            self.diag[s] = [
                net.push(mine.at[s, 0, 0], got_diag.at[s, 0], y_dev),
                net.push(mine.at[s, 0, 1], got_diag.at[s, 1], x_dev),
            ]
            self.near[s] = [
                net.push(mine.at[s, 1], got_x.at[s], x_dev),
                net.push(mine.at[s, 2], got_y.at[s], y_dev),
            ]
        self.to_mate = net.push(give.at[0], got_z.at[0], (ctx, flip(z, 1)))
        self.to_low = net.push(give.at[1], got_z.at[1], (ctx, flip(z, 2)))
        self.to_low_mate = net.push(give.at[2], got_z.at[2], (ctx, flip(z, 3)))

    def both(self, stage):
        stage(0)
        pl.when(self.upper)(lambda: stage(1))

    def start(self, s):
        for i in range(4):
            self.over[s, i].start()
            self.load[s, i].start()

    def chip_sums(self, s):
        mine, got_sib = self.refs[1:3]
        for i in range(4):
            self.load[s, i].wait()
            self.over[s, i].wait_recv()
            fold(mine.at[s, i], got_sib.at[s, i])
            if i == 0:
                for copy in self.diag[s]:
                    copy.start()

    def forward(self, s):
        mine, got_diag = self.refs[1], self.refs[3]
        for k in range(2):
            self.diag[s][k].wait_recv()
            fold(mine.at[s, 1 + k, k], got_diag.at[s, k])
            self.near[s][k].start()

    def total(self, s, kind):
        mine, got_x, got_y = self.refs[1], self.refs[4], self.refs[5]
        value = mine[s, 3, kind].astype(F32) + got_x[s, kind].astype(F32)
        return value + got_y[s, kind].astype(F32)

    def across(self):
        out, give, h = self.refs[0], self.refs[7], self.h
        for copy in self.near[0]:
            copy.wait_recv()

        @pl.when(jnp.logical_not(self.upper))
        def _():
            give[0] = self.total(0, 1 - h).astype(BF16)
            out[...] = self.total(0, h)

        @pl.when(self.upper)
        def _():
            give[1] = self.total(0, h).astype(BF16)
            give[2] = self.total(0, 1 - h).astype(BF16)
            self.to_low.start()
            self.to_low_mate.start()
            for copy in self.near[1]:
                copy.wait_recv()
            give[0] = self.total(1, 1 - h).astype(BF16)
            out[...] = self.total(1, h)

        self.to_mate.start()

    def finish(self):
        out, got_z = self.refs[0], self.refs[6]
        self.to_mate.wait_recv()
        out[...] += got_z[0].astype(F32)

        @pl.when(jnp.logical_not(self.upper))
        def _():
            self.to_low.wait_recv()
            self.to_low_mate.wait_recv()
            out[...] += got_z[1].astype(F32) + got_z[2].astype(F32)

        def sent(s):
            for i in range(4):
                self.over[s, i].wait_send()
            for copy in self.diag[s] + self.near[s]:
                copy.wait_send()

        self.both(sent)
        self.to_mate.wait_send()

        @pl.when(self.upper)
        def _():
            self.to_low.wait_send()
            self.to_low_mate.wait_send()

    @staticmethod
    def scratch(rows):
        block = (2, rows, HD)
        return [
            pltpu.VMEM((2, 4) + block, BF16),
            pltpu.VMEM((2, 4) + block, BF16),
            pltpu.VMEM((2, 2, rows, HD), BF16),
            pltpu.VMEM((2,) + block, BF16),
            pltpu.VMEM((2,) + block, BF16),
            pltpu.VMEM((3, rows, HD), BF16),
            pltpu.VMEM((3, rows, HD), BF16),
            pltpu.SemaphoreType.DMA((8,)),
        ]

    copies = 19


class WeightSum:
    def __init__(self, net, widths, parts, put, mine, got_sib, got_diag, got_x, got_y, got_z, total, sems):
        ctx, z = where_am_i()
        self.net, self.z = net, z
        self.ctx = ctx
        self.parts, self.put, self.sems = parts, put, sems
        self.refs = (mine, got_sib, got_diag, got_x, got_y, got_z, total)
        self.x_dev, self.y_dev, self.sib = (flip(ctx, 2), z), (flip(ctx, 4), z), (flip(ctx, 1), z)
        self.rows = mine.shape[1]
        self.copies = {}
        self.spans, col = [], 0
        for count in widths:
            self.spans.append(pl.ds(col, count))
            col += count

    def add_to(self, ref, other, count):
        step = 32

        def body(i, carry):
            at = pl.ds(pl.multiple_of(i * step, step), step)
            ref[at, :] = (ref[at, :].astype(F32) + other[at, :].astype(F32)).astype(BF16)
            return carry

        lax.fori_loop(0, count // step, body, 0)

    def start(self, g):
        mine, got_sib = self.refs[:2]
        span, rows, ctx = self.spans[g], self.rows, self.ctx

        def block_rows(source):
            return pl.ds(pl.multiple_of(source * rows, 16), rows)

        for i, m in enumerate((6, 2, 4, 0)):
            load = pltpu.make_async_copy(
                self.parts.at[block_rows(flip(ctx, m)), span],
                mine.at[i, :, span],
                self.sems.at[4 * g + i],
            )
            over = self.net.push(
                self.parts.at[block_rows(flip(flip(ctx, 1), m)), span],
                got_sib.at[i, :, span],
                self.sib,
            )
            load.start()
            over.start()
            self.copies[g, i] = (load, over)

    def chip_sums(self, g):
        mine, got_sib, got_diag = self.refs[:3]
        span, rows = self.spans[g], self.rows
        cut = rows // 2
        for i in range(4):
            load, over = self.copies[g, i]
            if load is not None:
                load.wait()
            over.wait_recv()
            self.add_to(mine.at[i, :, span], got_sib.at[i, :, span], rows)
            if i == 0:
                pair = []
                for k, to in enumerate((self.y_dev, self.x_dev)):
                    part = pl.ds(k * cut, cut)
                    pair.append(self.net.push(mine.at[0, part, span], got_diag.at[part, span], to))
                    pair[k].start()
                self.copies[g, "diag"] = pair

    def forward(self, g):
        mine, _, got_diag, got_x, got_y = self.refs[:5]
        span = self.spans[g]
        cut = self.rows // 2
        pair = []
        for k, (got, to) in enumerate(((got_x, self.x_dev), (got_y, self.y_dev))):
            part = pl.ds(k * cut, cut)
            self.copies[g, "diag"][k].wait_recv()
            self.add_to(mine.at[1 + k, part, span], got_diag.at[part, span], cut)
            pair.append(self.net.push(mine.at[1 + k, :, span], got.at[:, span], to))
            pair[k].start()
        self.copies[g, "near"] = pair

    def line(self, g):
        mine, _, _, got_x, got_y, got_z, total = self.refs
        span, rows, z = self.spans[g], self.rows, self.z
        unit = rows // 4
        for copy in self.copies[g, "near"]:
            copy.wait_recv()
        step = 16

        def body(i, carry):
            at = pl.ds(pl.multiple_of(i * step, step), step)
            value = mine[3, at, span].astype(F32) + got_x[at, span].astype(F32)
            total[at, span] = (value + got_y[at, span].astype(F32)).astype(BF16)
            return carry

        lax.fori_loop(0, rows // step, body, 0)
        sends = []
        for k, m in enumerate((1, 2, 3)):
            start_row = pl.multiple_of(flip(z, m) * unit, 16)
            copy = self.net.push(
                total.at[pl.ds(start_row, unit), span],
                got_z.at[k, :, span],
                (self.ctx, flip(z, m)),
            )
            copy.start()
            sends.append(copy)
        self.copies[g, "line"] = sends

    def finish(self, g):
        got_z, total = self.refs[5:]
        span, unit = self.spans[g], self.rows // 4
        for copy in self.copies[g, "line"]:
            copy.wait_recv()
        own_row = pl.multiple_of(self.z * unit, 16)
        h = self.z % 2
        own_cols = total[pl.ds(own_row, unit), span].astype(F32) + got_z[1, :, span].astype(F32)
        self.put(h, span, own_cols)
        self.put(1 - h, span, got_z[0, :, span].astype(F32) + got_z[2, :, span].astype(F32))
        for i in range(4):
            self.copies[g, i][1].wait_send()
        for name in ("diag", "near", "line"):
            for copy in self.copies[g, name]:
                copy.wait_send()

    @staticmethod
    def scratch(rows, shard, columns, groups):
        return [
            pltpu.VMEM((4, rows, columns), BF16),
            pltpu.VMEM((4, rows, columns), BF16),
            pltpu.VMEM((rows, columns), BF16),
            pltpu.VMEM((rows, columns), BF16),
            pltpu.VMEM((rows, columns), BF16),
            pltpu.VMEM((3, shard, columns), BF16),
            pltpu.VMEM((rows, columns), BF16),
            pltpu.SemaphoreType.DMA((4 * groups,)),
        ]


def everyone():
    ctx, z = where_am_i()
    return [(ctx, flip(z, m)) for m in (1, 2, 3)] + [(flip(ctx, m), z) for m in (1, 2, 4)]


def first_sums_kernel(kv_parts, near_parts, far_parts, come, kv_out, one_out, three_out, *scratch):
    ctx, z = where_am_i()
    kv_scratch, scratch = scratch[:8], scratch[8:]
    parts, got, send_sems, recv_sems, own_sems = scratch
    net = Net(send_sems, recv_sems)
    greet(everyone())
    beyond = (ctx, flip(z, 3))
    inner = (z == 1) | (z == 2)
    kv = KvSum(net, kv_parts, kv_out, *kv_scratch)
    two_over = net.push(parts.at[1], got, beyond)
    loads = []
    sources = (near_parts.at[1], far_parts.at[0], far_parts.at[1], come.at[0], come.at[1])
    for m, src in enumerate(sources):
        loads.append(pltpu.make_async_copy(src, parts.at[m], own_sems.at[m]))
        loads[m].start()
    kv.both(kv.start)
    for copy in loads:
        copy.wait()

    @pl.when(inner)
    def _():
        fold(parts.at[1], parts.at[4])
        two_over.start()
        fold(parts.at[2], parts.at[3])

    three = pltpu.make_async_copy(parts.at[2], three_out, own_sems.at[0])
    three.start()
    kv.both(kv.chip_sums)
    kv.both(kv.forward)
    kv.across()

    @pl.when(inner)
    def _():
        two_over.wait_recv()
        fold(parts.at[0], got)
        two_over.wait_send()

    one = pltpu.make_async_copy(parts.at[0], one_out, own_sems.at[1])
    one.start()
    kv.finish()
    three.wait()
    one.wait()


def plain_axes(shard):
    return lax.axis_size("ctx") != 8 or lax.axis_size("fsdp") != 4 or shard % 16


def plain_weight_sum(parts):
    z = lax.axis_index("fsdp")
    empty = jnp.zeros_like(parts)
    both = jnp.where(z % 2 == 0, jnp.stack([parts, empty]), jnp.stack([empty, parts]))
    summed = lax.psum_scatter(both, "ctx", scatter_dimension=1, tiled=True)
    return lax.psum_scatter(summed, "fsdp", scatter_dimension=1, tiled=True).astype(F32)


def first_sums(kv_parts, near_parts, far_parts, middle, shard):
    total, _, rows, _ = kv_parts.shape
    ctx_total = total // 2
    kv_parts = kv_parts.reshape(2, ctx_total, 2, rows, HD)
    own, width = middle.shape
    if plain_axes(shard):
        flat = kv_parts.transpose(0, 2, 1, 3, 4).reshape(4 * ctx_total * rows, HD)
        z_sum = lax.psum_scatter(flat, "fsdp", scatter_dimension=0, tiled=True)
        kv = lax.psum_scatter(z_sum, "ctx", scatter_dimension=0, tiled=True).astype(F32)
        out = middle + near_parts[0].astype(F32)
        for m in (1, 2, 3):
            part = near_parts[m] if m < 2 else far_parts[m - 2]
            out = out + swap(part, "fsdp", m).astype(F32)
        return kv, out.astype(BF16)
    copies = KvSum.copies + 1
    come = lax.ppermute(far_parts, "fsdp", [(0, 1), (3, 2)])
    line = jax.ShapeDtypeStruct((own, width), BF16)
    kv, one, three = pl.pallas_call(
        first_sums_kernel,
        out_shape=[jax.ShapeDtypeStruct((rows, HD), F32), line, line],
        in_specs=[ANY] * 4,
        out_specs=[VMEM, ANY, ANY],
        scratch_shapes=KvSum.scratch(rows)
        + [
            pltpu.VMEM((5, own, width), BF16),
            pltpu.VMEM((own, width), BF16),
            pltpu.SemaphoreType.DMA((copies,)),
            pltpu.SemaphoreType.DMA((copies,)),
            pltpu.SemaphoreType.DMA((5,)),
        ],
        compiler_params=pltpu.CompilerParams(
            collective_id=2, has_side_effects=True, vmem_limit_bytes=60 * 1024 * 1024
        ),
        cost_estimate=takes(45),
        name="first_sums",
    )(kv_parts, near_parts, far_parts, come)
    out = middle + near_parts[0].astype(F32) + swap(one, "fsdp", 1).astype(F32)
    out = out + lax.ppermute(three, "fsdp", [(1, 2), (2, 1)]).astype(F32)
    return kv, out.astype(BF16)


def last_sums_kernel(
    widths, out_widths, out_parts, w_qkv, grad_q, grad_kv, cosine, sine, normed, tokens, scale, grad_middle, ffn_scale_grad, *refs
):
    ctx, z = where_am_i()
    q_out, k_out, v_out, o_out, grad_tokens, scales = refs[:6]
    w_scratch, o_scratch, scratch = refs[6:14], refs[14:22], refs[22:]
    give_w, product, w, grads, grad_own, give, got, scale_got, send_sems, recv_sems, own_sems = scratch
    h, core, chip = z % 2, ctx % 2, ctx // 2
    net = Net(send_sems, recv_sems)
    own, width = tokens.shape
    step = 512
    steps = width // step
    loads = []
    for k in range(steps):
        part = pl.ds(k * step, step)
        loads.append(pltpu.make_async_copy(w_qkv.at[part], w.at[part], own_sems.at[k]))
        loads[k].start()
    greet(everyone() + [(flip(ctx, m), z) for m in (3, 5, 6, 7)])

    def put_out(which, span, value):
        o_out[:, pl.ds(pl.multiple_of(which * QW + span.start, 128), span.size)] = value

    outs = WeightSum(net, out_widths, out_parts, put_out, *o_scratch)
    outs.start(0)
    outs.start(1)
    grads[:, :QW] = grad_q[...]
    front, back = grad_kv[:, : HD // 2], grad_kv[:, HD // 2 :]
    c, s = cosine[...], sine[...]
    grads[:, QW : QW + HD // 2] = (front * c + back * s).astype(BF16)
    grads[:, QW + HD // 2 :] = (back * c - front * s).astype(BF16)

    def put(which, span, value):
        if span.start < QW:
            q_out[:, pl.ds(pl.multiple_of(which * QW + span.start, 128), span.size)] = value
            return

        @pl.when(which == 0)
        def _():
            k_out[...] = value

        @pl.when(which == 1)
        def _():
            v_out[...] = value

    weights = WeightSum(net, widths, None, put, *w_scratch)
    mine, got_sib = w_scratch[:2]
    side = mine.shape[1]

    def produce(g):
        span = weights.spans[g]
        for i, m in enumerate((3, 1, 2, 0)):
            cols = pl.ds(pl.multiple_of(flip(chip, m) * 2 * side, 128), 2 * side)
            product[:, : span.size] = t_dot(normed[:, cols], grads[:, span]).astype(BF16)
            keep_at = pl.ds(pl.multiple_of(core * side, 16), side)
            give_at = pl.ds(pl.multiple_of((1 - core) * side, 16), side)
            mine[i, :, span] = product[keep_at, : span.size]
            give_w[i, :, span] = product[give_at, : span.size]
            over = net.push(give_w.at[i, :, span], got_sib.at[i, :, span], weights.sib)
            over.start()
            weights.copies[g, i] = (None, over)

    outs.chip_sums(0)
    outs.chip_sums(1)
    outs.forward(0)
    other_grads = grads[pl.ds(pl.multiple_of((1 - h) * own, 16), own), :]
    crossing = []
    for k in range(steps):
        loads[k].wait()
        give[k] = dot_t(other_grads, w[pl.ds(k * step, step), :]).astype(BF16)
        crossing.append(net.push(give.at[k], got.at[k], (ctx, flip(z, 1))))
        crossing[k].start()
    line_mates = [(ctx, flip(z, m)) for m in (1, 2, 3)]
    plane_mates = [(flip(ctx, m), z) for m in range(1, 8)]
    trade = []

    def trade_send(mates):
        for to in mates:
            trade.append(net.push(scales, scale_got.at[len(trade)], to))
            trade[-1].start()

    def trade_add(first, count):
        for k in range(first, first + count):
            trade[k].wait()
        for k in range(first, first + count):
            scales[...] += scale_got[k]

    def own_part():
        own_grads = grads[pl.ds(pl.multiple_of(h * own, 16), own), :]
        for k in range(steps):
            part = pl.ds(k * step, step)
            grad_own[:, part] = dot_t(own_grads, w[part, :])

    def norm_part():
        value = tokens[...].astype(F32)
        for k in range(steps):
            crossing[k].wait_recv()
            grad_own[:, pl.ds(k * step, step)] += got[k].astype(F32)
        grad = grad_own[...]
        r = inv_rms(value)
        scaled = grad * scale[0:1, :]
        lean = jnp.mean(scaled * value, -1, keepdims=True)
        grad_tokens[...] = grad_middle[...] + (r * scaled - value * (r * r * r * lean))
        rows = [jnp.sum(grad * value * r, 0, keepdims=True), ffn_scale_grad[...]]
        quarter = width // 4
        for i in range(8):
            scales[i : i + 1, :] = rows[i // 4][:, i % 4 * quarter : (i % 4 + 1) * quarter]
        trade_send(line_mates)

    outs.forward(1)
    produce(0)
    weights.chip_sums(0)
    produce(1)
    weights.chip_sums(1)
    outs.line(0)
    weights.forward(0)
    outs.line(1)
    produce(2)
    weights.chip_sums(2)
    weights.forward(1)
    own_part()
    norm_part()
    weights.line(0)
    weights.forward(2)
    trade_add(0, 3)
    trade_send(plane_mates)
    weights.line(1)
    outs.finish(0)
    outs.finish(1)
    weights.line(2)
    trade_add(3, 7)
    weights.finish(0)
    weights.finish(1)
    weights.finish(2)
    for copy in crossing:
        copy.wait_send()


def last_sums(out_parts, w_qkv, grad_q, grad_kv, cosine, sine, normed, tokens, scale, grad_middle, ffn_scale_grad, shard):
    own, width = tokens.shape
    columns = w_qkv.shape[1]
    if plain_axes(shard):
        h = lax.axis_index("fsdp") % 2
        front, back = grad_kv[:, : HD // 2], grad_kv[:, HD // 2 :]
        c, s = cosine, sine
        grad_kv = jnp.concatenate([front * c + back * s, back * c - front * s], 1).astype(BF16)
        grads = jnp.concatenate([grad_q, grad_kv], 1)
        both = plain_weight_sum(t_dot(normed, grads).astype(BF16))
        grad_rows = dot_t(grads, w_qkv)
        other = swap(half(grad_rows, 1 - h).astype(BF16), "fsdp", 1).astype(F32)
        grad, scale_grad = norm_back(tokens.astype(F32), scale[:1], half(grad_rows, h) + other)
        scales = jnp.concatenate([scale_grad[None], ffn_scale_grad])
        queries = jnp.concatenate([both[0, :, :QW], both[1, :, :QW]], 1)
        scales = lax.psum(scales, ("ctx", "fsdp"))
        outs = plain_weight_sum(out_parts)
        outs = jnp.concatenate([outs[0], outs[1]], 1)
        return queries, both[0, :, QW:], both[1, :, QW:], outs, grad_middle + grad, scales
    block = 4 * shard
    rows = normed.shape[0]
    widths = (QW // 2, QW // 2, HD)
    steps = width // 512
    out_widths = (QW // 2, QW // 2)
    copies = 11 * (len(widths) + len(out_widths)) + steps + 10
    *weights, scales = pl.pallas_call(
        functools.partial(last_sums_kernel, widths, out_widths),
        out_shape=[
            jax.ShapeDtypeStruct((shard, 2 * QW), F32),
            jax.ShapeDtypeStruct((shard, HD), F32),
            jax.ShapeDtypeStruct((shard, HD), F32),
            jax.ShapeDtypeStruct((shard, 2 * QW), F32),
            jax.ShapeDtypeStruct((own, width), F32),
            jax.ShapeDtypeStruct((8, width // 4), F32),
        ],
        in_specs=[ANY] * 2 + [VMEM] * 9,
        out_specs=[VMEM] * 6,
        scratch_shapes=WeightSum.scratch(block, shard, columns, len(widths))
        + WeightSum.scratch(block, shard, QW, len(out_widths))
        + [
            pltpu.VMEM((4, block, columns), BF16),
            pltpu.VMEM((2 * block, QW // 2), BF16),
            pltpu.VMEM((width, columns), BF16),
            pltpu.VMEM((rows, columns), BF16),
            pltpu.VMEM((own, width), F32),
            pltpu.VMEM((steps, own, 512), BF16),
            pltpu.VMEM((steps, own, 512), BF16),
            pltpu.VMEM((10, 8, width // 4), F32),
            pltpu.SemaphoreType.DMA((copies,)),
            pltpu.SemaphoreType.DMA((copies,)),
            pltpu.SemaphoreType.DMA((steps,)),
        ],
        compiler_params=pltpu.CompilerParams(
            collective_id=4, has_side_effects=True, vmem_limit_bytes=60 * 1024 * 1024
        ),
        cost_estimate=takes(60),
        name="last_sums",
    )(out_parts, w_qkv, grad_q, grad_kv, cosine, sine, normed, tokens, scale, grad_middle, ffn_scale_grad)
    return *weights, scales.reshape(2, width)


def local(
    tokens,
    lengths,
    block_place,
    gain_attn,
    w_query,
    w_key,
    w_value,
    w_out,
    gain_ffn,
    w_gate,
    w_up,
    w_down,
    cotangent,
):
    own_rows, width = tokens.shape
    rows = 2 * own_rows
    ctx_total = lax.axis_size("ctx")
    ctx, z = where_am_i()
    h, pair = z % 2, z // 2
    shard = w_query.shape[0]
    reach = -(-WIN // rows)

    def place_of(stored):
        hit = jnp.arange(block_place.shape[0])[None, :] == stored[:, None]
        return jnp.sum(jnp.where(hit, block_place[None, :], 0), 1)

    own_pos = place_of((2 * ctx + pair)[None])[0]
    query_at = own_pos * rows + jnp.arange(rows, dtype=jnp.int32)
    passed = query_at[:, None] >= jnp.cumsum(lengths)[None, :]
    doc_start = jnp.sum(jnp.where(passed, lengths[None, :], 0), 1)
    rel_pos = query_at - doc_start
    window_start = (own_pos - reach) * rows
    lowest = jnp.maximum(doc_start, query_at - WIN + 1) - window_start
    lowest = jnp.broadcast_to(lowest[:, None], (rows, 128)).astype(jnp.int32)
    holders = jnp.arange(ctx_total)
    held = jnp.concatenate([place_of(2 * holders), place_of(2 * holders + 1)])
    held = jnp.where((pair == 1) | (jnp.arange(2 * ctx_total) < ctx_total), held, -1000)
    want = own_pos - reach + jnp.arange(reach + 1)
    hit = held[None, :] == want[:, None]
    numbers = jnp.arange(2 * ctx_total)
    own_index = pair * ctx_total + ctx
    place = jnp.where(jnp.any(hit, 1), jnp.sum(jnp.where(hit, numbers, 0), 1), own_index)
    place = place.astype(jnp.int32)
    goes = held - (own_pos - reach)
    goes = jnp.where((goes >= 0) & (goes <= reach), goes, reach + 1).astype(jnp.int32)
    half_dim = HD // 2
    frequency = jnp.exp(jnp.arange(half_dim, dtype=F32) * (-jnp.log(10000.0) / half_dim))
    angles = rel_pos.astype(F32)[:, None] * frequency
    cosine, sine = jnp.cos(angles), jnp.sin(angles)
    q_scale = HD ** (-0.5)
    kv_cosine, kv_sine = jnp.where(h == 0, cosine, 1.0), jnp.where(h == 0, sine, 0.0)
    cosine = jnp.stack([cosine * q_scale, kv_cosine])
    sine = jnp.stack([sine * q_scale, kv_sine])

    gate_up_shard = jnp.concatenate([w_gate, w_up], 1)
    down_shard = w_down.T
    w_qkv, w_o, gains, rows_in, cot_one, cot_three = gather_weights(
        w_query, w_key, w_value, w_out, gain_attn, gain_ffn, tokens, cotangent
    )
    w_qkv, w_o, gate_up_shard, down_shard = lax.optimization_barrier(
        (w_qkv, w_o, gate_up_shard, down_shard)
    )
    gate_up_w = lax.all_gather(gate_up_shard, "ctx", axis=0, tiled=True)
    down_w = lax.all_gather(down_shard, "ctx", axis=0, tiled=True)
    normed, queries, kv, scales = project(rows_in, gains, shard, cosine, sine, w_qkv)
    inner = (z == 1) | (z == 2)
    across = lax.ppermute(cot_one, "fsdp", [(1, 2), (2, 1)])
    outward = lax.ppermute(cot_three, "fsdp", [(1, 0), (2, 3)])
    store = gather_kv(kv)
    store, across, outward = lax.optimization_barrier((store, across, outward))
    farther = lax.ppermute(across, "fsdp", [(1, 0), (2, 3)])
    prob, attended = attend(place, lowest, queries, store, reach)
    attended, farther = lax.optimization_barrier((attended, farther))
    cots = (
        cotangent,
        cot_one,
        jnp.where(inner, across, outward),
        jnp.where(inner, cot_three, farther),
    )
    middle, own_normed, mate_normed, beyond_normed = out_norm(attended, tokens, scales, w_o)

    ffn_in, hidden, active, sloped = feed_forward(
        own_normed, mate_normed, beyond_normed, gate_up_w
    )
    ffn_cot, grad_gate, grad_up = feed_forward_grad(cots, down_w, active, sloped)

    w_parts, gate_sum, near_parts, far_parts, grad_middle, grad_branch, grad_ffn_scale = feed_forward_back(
        grad_gate, grad_up, gate_up_w, down_w, hidden, ffn_in, middle, ffn_cot, scales
    )
    same_core = [list(range(core, ctx_total, 2)) for core in range(2)]
    ffn_sums = lax.psum_scatter(
        w_parts, "ctx", scatter_dimension=0, axis_index_groups=same_core, tiled=True
    )
    units = w_gate.shape[1]
    if ctx_total != 8:
        gate_sum, ffn_sums = ffn_sums[:, :units], ffn_sums[:, units:]
    grad_gate_w = gate_sum.astype(F32)
    grad_up_w = ffn_sums[:, :units].astype(F32)
    grad_down = ffn_sums[:, units:].astype(F32).T
    grad_out_part = t_dot(grad_branch, attended).astype(BF16)

    grad_q, kv_parts = attend_back(
        place, goes, prob, queries, grad_branch, w_o, cosine, sine, store, reach
    )
    grad_kv, output = first_sums(kv_parts, near_parts, far_parts, middle, shard)
    grad_query_w, grad_key_w, grad_value_w, grad_out_w, grad_tokens, scale_sums = last_sums(
        grad_out_part,
        w_qkv,
        grad_q,
        grad_kv,
        kv_cosine,
        kv_sine,
        normed,
        tokens,
        scales,
        grad_middle,
        grad_ffn_scale,
        shard,
    )
    first_col = (ctx * lax.axis_size("fsdp") + z) * shard
    scale_sums = lax.dynamic_slice_in_dim(scale_sums, first_col, shard, 1)
    return (
        output,
        grad_tokens,
        scale_sums[0],
        grad_query_w,
        grad_key_w,
        grad_value_w,
        grad_out_w.T,
        scale_sums[1],
        grad_gate_w,
        grad_up_w,
        grad_down,
    )


def solution(mesh):
    in_specs = (
        P(("ctx", "fsdp"), None),
        P(),
        P(),
        P(("ctx", "fsdp")),
        P(("ctx", "fsdp"), None),
        P(("ctx", "fsdp"), None),
        P(("ctx", "fsdp"), None),
        P(None, ("ctx", "fsdp")),
        P(("ctx", "fsdp")),
        P("ctx", "fsdp"),
        P("ctx", "fsdp"),
        P("fsdp", "ctx"),
        P(("ctx", "fsdp"), None),
    )
    out_specs = (
        P(("ctx", "fsdp"), None),
        P(("ctx", "fsdp"), None),
        P(("ctx", "fsdp")),
        P(("ctx", "fsdp"), None),
        P(("ctx", "fsdp"), None),
        P(("ctx", "fsdp"), None),
        P(None, ("ctx", "fsdp")),
        P(("ctx", "fsdp")),
        P("ctx", "fsdp"),
        P("ctx", "fsdp"),
        P("fsdp", "ctx"),
    )
    return jax.shard_map(local, mesh=mesh, in_specs=in_specs, out_specs=out_specs, check_vma=False)
```

```python
import functools

import jax
import jax.numpy as jnp
from jax import lax
from jax.experimental import pallas as pl
from jax.experimental.pallas import tpu as pltpu
from jax.sharding import PartitionSpec as P

H = 10
HD = 256
WIN = 2048
EPS = 1e-06
F32 = jnp.float32
BF16 = jnp.bfloat16
MESH = pl.DeviceIdType.MESH
ANY = pl.BlockSpec(memory_space=pl.ANY)
VMEM = pl.BlockSpec(memory_space=pltpu.VMEM)
HEADS = H // 2
QW = HEADS * HD
VMEM_LIMIT = 56 * 1024 * 1024
FAR = -1e30


def swap(x, axis, mask):
    return lax.ppermute(x, axis, [(i, i ^ mask) for i in range(lax.axis_size(axis))])


def join(own, other, bit, axis):
    return jnp.where(
        bit == 0,
        jnp.concatenate([own, other], axis),
        jnp.concatenate([other, own], axis),
    )


def half(x, which, axis=0):
    size = x.shape[axis] // 2
    return lax.dynamic_slice_in_dim(x, which * size, size, axis)


def dot(a, b):
    return jnp.dot(a, b, preferred_element_type=F32)


def dot_t(a, b):
    return lax.dot_general(a, b, (((1,), (1,)), ((), ())), preferred_element_type=F32)


def t_dot(a, b):
    return lax.dot_general(a, b, (((0,), (0,)), ((), ())), preferred_element_type=F32)


def inv_rms(x):
    return lax.rsqrt(jnp.mean(x * x, -1, keepdims=True) + EPS)


def norm_back(x, scale, grad):
    r = inv_rms(x)
    scaled = grad * scale
    lean = jnp.mean(scaled * x, -1, keepdims=True)
    return r * scaled - x * (r * r * r * lean), jnp.sum(grad * x * r, 0)


def takes(us):
    return pl.CostEstimate(flops=int(us * 1e9), bytes_accessed=0, transcendentals=0)


class Net:
    def __init__(self, send_sems, recv_sems):
        self.send_sems, self.recv_sems, self.used = send_sems, recv_sems, 0

    def push(self, src, dst, to):
        copy = pltpu.make_async_remote_copy(
            src_ref=src,
            dst_ref=dst,
            send_sem=self.send_sems.at[self.used],
            recv_sem=self.recv_sems.at[self.used],
            device_id=to,
            device_id_type=MESH,
        )
        self.used += 1
        return copy


def greet(partners):
    barrier = pltpu.get_barrier_semaphore()
    for to in partners:
        pl.semaphore_signal(barrier, inc=1, device_id=to, device_id_type=MESH)
    pl.semaphore_wait(barrier, len(partners))


def flip(x, mask):
    for bit in (1, 2, 4):
        if mask & bit:
            x = x + bit - 2 * bit * ((x // bit) % 2)
    return x


def where_am_i():
    return lax.axis_index("ctx"), lax.axis_index("fsdp")


def gather_kernel(
    qkv, out, gain, tokens, cot, w_qkv, w_out, gains, rows, cot_one, cot_three, send_sems, recv_sems, own_sems
):
    ctx, z = where_am_i()
    net = Net(send_sems, recv_sems)
    greet([(ctx, flip(z, m)) for m in (1, 2, 3)] + [(flip(ctx, m), z) for m in (1, 2, 4)])
    shard = qkv.shape[0]
    qkv_cols, half_cols = QW + HD, QW // 2

    def cols_of(ref, stride, first, count):
        return lambda h: ref.at[:, pl.ds(pl.multiple_of(h * stride + first, 128), count)]

    groups = [
        (cols_of(qkv, qkv_cols, QW, HD), w_qkv, shard, QW, HD),
        (lambda h: gain, gains, 8, 0, 128),
        (cols_of(qkv, qkv_cols, 0, half_cols), w_qkv, shard, 0, half_cols),
        (cols_of(qkv, qkv_cols, half_cols, half_cols), w_qkv, shard, half_cols, half_cols),
        (cols_of(out, QW, 0, half_cols), w_out, shard, 0, half_cols),
        (cols_of(out, QW, half_cols, half_cols), w_out, shard, half_cols, half_cols),
    ]

    def at(group, source, first, count):
        src, ref, unit, col, cols = group
        start = pl.multiple_of(source * 4 * unit + first, 8 if unit == 8 else 16)
        return ref.at[pl.ds(start, count), pl.ds(col, cols)]

    lines, locals_, sent = [], [], []

    def push(src, dst, to):
        copy = net.push(src, dst, to)
        copy.start()
        sent.append(copy)
        return copy

    token_rows = tokens.shape[0]
    token_dst = rows.at[pl.ds(pl.multiple_of((z % 2) * token_rows, 16), token_rows)]
    for i, group in enumerate(groups):
        unit = group[2]
        dst = at(group, ctx, z * unit, unit)
        lines.append([push(group[0](flip(z, m) % 2), dst, (ctx, flip(z, m))) for m in (2, 3, 1)])
        local = pltpu.make_async_copy(group[0](z % 2), dst, own_sems.at[i])
        local.start()
        locals_.append(local)
        if i == len(groups) - 1:
            token_copy = push(tokens, token_dst, (ctx, flip(z, 1)))
            token_local = pltpu.make_async_copy(tokens, token_dst, own_sems.at[len(groups)])
            token_local.start()
    mate, beyond = (ctx, flip(z, 1)), (ctx, flip(z, 3))
    inner = (z == 1) | (z == 2)
    cot_mate = push(cot, cot_one, mate)
    cot_beyond = net.push(cot, cot_three, beyond)

    @pl.when(inner)
    def _():
        cot_beyond.start()

    by_x, by_y, last = {}, {}, []
    diag = {}
    x_dev, y_dev, sib = (flip(ctx, 2), z), (flip(ctx, 4), z), (flip(ctx, 1), z)

    def same(group, source, first, count, to):
        return push(at(group, source, first, count), at(group, source, first, count), to)

    def spread_own(i):
        group = groups[i]
        locals_[i].wait()
        for copy in lines[i]:
            copy.wait_recv()
        count = 4 * group[2]
        by_x[i] = same(group, ctx, 0, count, x_dev)
        by_y[i] = same(group, ctx, 0, count, y_dev)
        last.append(same(group, ctx, 0, count, sib))

    def spread_near(i):
        group = groups[i]
        count = 4 * group[2]
        by_x[i].wait_recv()
        top = same(group, flip(ctx, 2), 0, count // 2, y_dev)
        last.append(same(group, flip(ctx, 2), 0, count, sib))
        by_y[i].wait_recv()
        low = same(group, flip(ctx, 4), count // 2, count // 2, x_dev)
        last.append(same(group, flip(ctx, 4), 0, count, sib))
        diag[i] = (top, low)

    def spread_far(i):
        group = groups[i]
        count = 4 * group[2]
        for k in range(2):
            diag[i][k].wait_recv()
            last.append(same(group, flip(ctx, 6), k * count // 2, count // 2, sib))

    for i in range(len(groups) + 2):
        if i < len(groups):
            spread_own(i)
        if 0 <= i - 1 < len(groups):
            spread_near(i - 1)
        if 0 <= i - 2 < len(groups):
            spread_far(i - 2)
    token_local.wait()
    token_copy.wait_recv()
    cot_mate.wait_recv()

    @pl.when(inner)
    def _():
        cot_beyond.wait_recv()
        cot_beyond.wait_send()

    for copy in last:
        copy.wait_recv()
    for copy in sent:
        copy.wait_send()


def gather_weights(w_query, w_key, w_value, w_out, gain_attn, gain_ffn, tokens, cotangent):
    shard, width = w_query.shape
    z = lax.axis_index("fsdp")
    ctx_total = lax.axis_size("ctx")
    pieces = []
    for h in range(2):
        pieces += [w_query[:, h * QW : (h + 1) * QW], (w_key, w_value)[h]]
    qkv = jnp.concatenate(pieces, 1)
    out = w_out.T
    gain = jnp.stack([gain_attn, gain_ffn]).astype(F32)
    gain = jnp.pad(gain, ((0, 6), (0, 128 - shard)))
    if ctx_total != 8 or lax.axis_size("fsdp") != 4 or shard % 16:
        both = ("ctx", "fsdp")
        full = lax.all_gather(qkv, both, axis=0, tiled=True)
        full_out = lax.all_gather(out, both, axis=0, tiled=True)
        return (
            half(full, z % 2, 1),
            half(full_out, z % 2, 1),
            lax.all_gather(gain, both, axis=0, tiled=True),
            join(tokens, swap(tokens, "fsdp", 1), z % 2, 0),
            swap(cotangent, "fsdp", 1),
            swap(cotangent, "fsdp", 3),
        )
    devices = 4 * ctx_total
    w_qkv, w_o, gains, rows, cot_one, cot_three = pl.pallas_call(
        gather_kernel,
        out_shape=[
            jax.ShapeDtypeStruct((width, QW + HD), BF16),
            jax.ShapeDtypeStruct((width, QW), BF16),
            jax.ShapeDtypeStruct((8 * devices, 128), F32),
            jax.ShapeDtypeStruct((2 * tokens.shape[0], width), BF16),
            jax.ShapeDtypeStruct(tokens.shape, BF16),
            jax.ShapeDtypeStruct(tokens.shape, BF16),
        ],
        in_specs=[ANY] * 5,
        out_specs=[ANY] * 6,
        scratch_shapes=[
            pltpu.SemaphoreType.DMA((75,)),
            pltpu.SemaphoreType.DMA((75,)),
            pltpu.SemaphoreType.DMA((7,)),
        ],
        compiler_params=pltpu.CompilerParams(collective_id=0, has_side_effects=True),
        cost_estimate=takes(80),
        name="gather_weights",
    )(qkv, out, gain, tokens, cotangent)
    return w_qkv, w_o, gains, rows, cot_one, cot_three


def proj_kernel(shard, rows, gains, cosine, sine, w, normed, out, kv, scales):
    @pl.when(pl.program_id(0) == 0)
    def _():
        for i in range(gains.shape[0] // 8):
            scales[:, i * shard : (i + 1) * shard] = gains[8 * i : 8 * i + 8, :shard]
        x = rows[...].astype(F32)
        normed[...] = (x * inv_rms(x) * scales[0:1, :]).astype(BF16)

    value = dot(normed[...], w[...])
    front, back = value[:, : HD // 2], value[:, HD // 2 :]
    c, s = cosine[0], sine[0]

    def put(ref):
        ref[:, : HD // 2] = (front * c - back * s).astype(BF16)
        ref[:, HD // 2 :] = (back * c + front * s).astype(BF16)

    pl.when(pl.program_id(0) < HEADS)(lambda: put(out))
    pl.when(pl.program_id(0) == HEADS)(lambda: put(kv))


def project(rows, gains, shard, cosine, sine, w):
    count, width = rows.shape
    steps = HEADS + 1
    fixed = lambda i: (0, 0)
    table = pl.BlockSpec((1, count, HD // 2), lambda i: (i // HEADS, 0, 0))
    return pl.pallas_call(
        functools.partial(proj_kernel, shard),
        grid=(steps,),
        out_shape=[
            jax.ShapeDtypeStruct((count, width), BF16),
            jax.ShapeDtypeStruct((count, QW), BF16),
            jax.ShapeDtypeStruct((count, HD), BF16),
            jax.ShapeDtypeStruct((8, width), F32),
        ],
        in_specs=[
            pl.BlockSpec((count, width), fixed),
            pl.BlockSpec(gains.shape, fixed),
            table,
            table,
            pl.BlockSpec((width, HD), lambda i: (0, i)),
        ],
        out_specs=[
            pl.BlockSpec((count, width), fixed),
            pl.BlockSpec((count, HD), lambda i: (0, jnp.minimum(i, HEADS - 1))),
            pl.BlockSpec((count, HD), fixed),
            pl.BlockSpec((8, width), fixed),
        ],
        compiler_params=pltpu.CompilerParams(vmem_limit_bytes=VMEM_LIMIT),
        cost_estimate=takes(10),
        name="project",
    )(rows, gains, cosine, sine, w)


def kv_gather_kernel(kv, store, send_sems, recv_sems, own_sem):
    ctx, z = where_am_i()
    net = Net(send_sems, recv_sems)
    h, pair = z % 2, z // 2
    greet([(ctx, flip(z, m)) for m in (1, 2)] + [(flip(ctx, m), z) for m in (1, 2, 4)])
    local = pltpu.make_async_copy(kv, store.at[pair, ctx, h], own_sem)
    local.start()
    mate, across = (ctx, flip(z, 1)), (ctx, flip(z, 2))
    x_dev, y_dev, sib = (flip(ctx, 2), z), (flip(ctx, 4), z), (flip(ctx, 1), z)
    own = net.push(kv, store.at[pair, ctx, h], mate)
    own.start()
    low = net.push(kv, store.at[0, ctx, h], across)
    low_mate = net.push(store.at[0, ctx, h], store.at[0, ctx, h], mate)

    @pl.when(pair == 0)
    def _():
        low.start()

    local.wait()
    own.wait_recv()

    class Set:
        def __init__(self, which):
            def same(source, kind, to):
                if kind is None:
                    ref = store.at[which, source]
                else:
                    ref = store.at[which, source, kind]
                return net.push(ref, ref, to)

            self.near = [same(ctx, None, x_dev), same(ctx, None, y_dev), same(ctx, None, sib)]
            x_ctx, y_ctx, d_ctx = flip(ctx, 2), flip(ctx, 4), flip(ctx, 6)
            self.after_x = [same(x_ctx, 0, y_dev), same(x_ctx, None, sib)]
            self.after_y = [same(y_ctx, 1, x_dev), same(y_ctx, None, sib)]
            self.after_d = [same(d_ctx, 0, sib), same(d_ctx, 1, sib)]

        def first(self):
            for copy in self.near:
                copy.start()

        def second(self):
            self.near[0].wait_recv()
            for copy in self.after_x:
                copy.start()
            self.near[1].wait_recv()
            for copy in self.after_y:
                copy.start()

        def third(self):
            self.after_x[0].wait_recv()
            self.after_d[0].start()
            self.after_y[0].wait_recv()
            self.after_d[1].start()

        def finish(self):
            for copy in [self.near[2], self.after_x[1], self.after_y[1]] + self.after_d:
                copy.wait_recv()
            for copy in self.near + self.after_x + self.after_y + self.after_d:
                copy.wait_send()

    mine = Set(pair)
    lower = Set(0)
    mine.first()

    @pl.when(pair == 1)
    def _():
        low.wait_recv()
        low_mate.start()
        low_mate.wait_recv()
        lower.first()

    mine.second()

    @pl.when(pair == 1)
    def _():
        lower.second()

    mine.third()

    @pl.when(pair == 1)
    def _():
        lower.third()

    mine.finish()
    own.wait_send()

    @pl.when(pair == 1)
    def _():
        lower.finish()
        low_mate.wait_send()

    @pl.when(pair == 0)
    def _():
        low.wait_send()


def gather_kv(kv):
    ctx_total = lax.axis_size("ctx")
    rows = kv.shape[0]
    if ctx_total != 8 or lax.axis_size("fsdp") != 4:
        every = lax.all_gather(kv, ("fsdp", "ctx"), axis=0, tiled=False)
        every = every.reshape(2, 2, ctx_total, rows, HD).transpose(0, 2, 1, 3, 4)
        return every.reshape(2 * ctx_total, 2, rows, HD)
    store = pl.pallas_call(
        kv_gather_kernel,
        out_shape=jax.ShapeDtypeStruct((2, ctx_total, 2, rows, HD), BF16),
        in_specs=[ANY],
        out_specs=ANY,
        scratch_shapes=[
            pltpu.SemaphoreType.DMA((21,)),
            pltpu.SemaphoreType.DMA((21,)),
            pltpu.SemaphoreType.DMA,
        ],
        compiler_params=pltpu.CompilerParams(collective_id=1, has_side_effects=True),
        cost_estimate=takes(30),
        name="gather_kv",
    )(kv)
    return store.reshape(2 * ctx_total, 2, rows, HD)


def chunks(rows, reach):
    skip = (reach * rows - WIN) // 128 * 128
    parts, at = [], 0
    for r in range(reach + 1):
        begin = max(0, skip - r * rows)
        if begin < rows:
            parts.append((r, begin, at, rows - begin))
            at += rows - begin
    return parts, at


def attend_kernel(reach, place, lowest, q, *refs):
    keys, values = refs[: reach + 1], refs[reach + 1 : 2 * reach + 2]
    prob, out, scores = refs[2 * reach + 2 :]
    rows = q.shape[0]
    parts, total = chunks(rows, reach)
    low = lowest[:, :1]
    peak = None
    for r, begin, at, count in parts:
        s = dot_t(q[...], keys[r][0, 0, begin:, :])
        key_at = lax.broadcasted_iota(jnp.int32, (rows, count), 1) + (r * rows + begin)
        visible = key_at >= low
        if r == reach:
            query_at = lax.broadcasted_iota(jnp.int32, (rows, count), 0) + reach * rows
            visible = visible & (key_at <= query_at)
        s = jnp.where(visible, s, FAR)
        scores[:, at : at + count] = s
        top = jnp.max(s, -1, keepdims=True)
        peak = top if peak is None else jnp.maximum(peak, top)
    weight_sum = jnp.zeros_like(peak)
    for r, begin, at, count in parts:
        e = jnp.exp(scores[:, at : at + count] - peak)
        scores[:, at : at + count] = e
        weight_sum = weight_sum + jnp.sum(e, -1, keepdims=True)
    share = 1.0 / weight_sum
    mixed = jnp.zeros((rows, HD), F32)
    for r, begin, at, count in parts:
        p = (scores[:, at : at + count] * share).astype(BF16)
        prob[0, :, at : at + count] = p
        mixed = mixed + dot(p, values[r][0, 0, begin:, :])
    out[...] = mixed.astype(BF16)


def window_specs(rows, reach):
    def spec(r, kind):
        return pl.BlockSpec((1, 1, rows, HD), lambda i, place: (place[r], kind, 0, 0))

    return [spec(r, kind) for kind in range(2) for r in range(reach + 1)]


def attend(place, lowest, qkv, store, reach):
    rows = qkv.shape[0]
    total = chunks(rows, reach)[1]
    column = pl.BlockSpec((rows, HD), lambda i, place: (0, i))
    return pl.pallas_call(
        functools.partial(attend_kernel, reach),
        grid_spec=pltpu.PrefetchScalarGridSpec(
            num_scalar_prefetch=1,
            grid=(HEADS,),
            in_specs=[pl.BlockSpec((rows, 128), lambda i, place: (0, 0)), column]
            + window_specs(rows, reach),
            out_specs=[
                pl.BlockSpec((1, rows, total), lambda i, place: (i, 0, 0)),
                column,
            ],
            scratch_shapes=[pltpu.VMEM((rows, total), F32)],
        ),
        out_shape=[
            jax.ShapeDtypeStruct((HEADS, rows, total), BF16),
            jax.ShapeDtypeStruct((rows, QW), BF16),
        ],
        compiler_params=pltpu.CompilerParams(vmem_limit_bytes=VMEM_LIMIT),
        cost_estimate=takes(21),
        name="attend",
    )(place, lowest, qkv, *([store] * (2 * reach + 2)))


def attend_back_kernel(reach, place, goes, prob, q, branch, w_out, cosine, sine, *refs):
    keys, values = refs[: reach + 1], refs[reach + 1 : 2 * reach + 2]
    grad_q, store, grad_probs, sums, blocks, sems = refs[2 * reach + 2 :]
    rows = q.shape[0]
    parts, total = chunks(rows, reach)
    head = pl.program_id(0)

    @pl.when(head == 0)
    def _():
        sums[...] = jnp.zeros_like(sums)

    grad_rows = dot(branch[...], w_out[...]).astype(BF16)
    query_rows = q[...]
    lean = jnp.zeros((rows, 1), F32)
    for r, begin, at, count in parts:
        dp = dot_t(grad_rows, values[r][0, 0, begin:, :])
        p = prob[0, :, at : at + count]
        grad_probs[:, at : at + count] = dp
        lean = lean + jnp.sum(dp * p.astype(F32), -1, keepdims=True)
        sums[1, at : at + count, :] += t_dot(p, grad_rows)
    turned = jnp.zeros((rows, HD), F32)
    for r, begin, at, count in parts:
        p = prob[0, :, at : at + count].astype(F32)
        ds = (p * (grad_probs[:, at : at + count] - lean)).astype(BF16)
        turned = turned + dot(ds, keys[r][0, 0, begin:, :])
        sums[0, at : at + count, :] += t_dot(ds, query_rows)
    front, back = turned[:, : HD // 2], turned[:, HD // 2 :]
    c, s = cosine[0], sine[0]
    grad_q[:, : HD // 2] = (front * c + back * s).astype(BF16)
    grad_q[:, HD // 2 :] = (back * c - front * s).astype(BF16)

    @pl.when(head == pl.num_programs(0) - 1)
    def _():
        blocks[reach + 1] = jnp.zeros((2, rows, HD), BF16)
        for r, begin, at, count in parts:
            for kind in range(2):
                if begin > 0:
                    blocks[r, kind, :begin, :] = jnp.zeros((begin, HD), BF16)
                blocks[r, kind, begin:, :] = sums[kind, at : at + count, :].astype(BF16)
        for r in range(parts[0][0]):
            blocks[r] = jnp.zeros((2, rows, HD), BF16)
        count = store.shape[0]

        def copy(i):
            return pltpu.make_async_copy(blocks.at[goes[i]], store.at[i], sems.at[i])

        for i in range(count):
            copy(i).start()
        for i in range(count):
            copy(i).wait()


def attend_back(place, goes, prob, qkv, branch, w_out, cosine, sine, store, reach):
    rows = qkv.shape[0]
    total = chunks(rows, reach)[1]
    column = pl.BlockSpec((rows, HD), lambda i, place, goes: (0, i))
    table = pl.BlockSpec((1, rows, HD // 2), lambda i, place, goes: (0, 0, 0))

    def spec(r, kind):
        return pl.BlockSpec((1, 1, rows, HD), lambda i, place, goes: (place[r], kind, 0, 0))

    return pl.pallas_call(
        functools.partial(attend_back_kernel, reach),
        grid_spec=pltpu.PrefetchScalarGridSpec(
            num_scalar_prefetch=2,
            grid=(HEADS,),
            in_specs=[
                pl.BlockSpec((1, rows, total), lambda i, place, goes: (i, 0, 0)),
                column,
                pl.BlockSpec(branch.shape, lambda i, place, goes: (0, 0)),
                pl.BlockSpec((w_out.shape[0], HD), lambda i, place, goes: (0, i)),
                table,
                table,
            ]
            + [spec(r, kind) for kind in range(2) for r in range(reach + 1)],
            out_specs=[column, ANY],
            scratch_shapes=[
                pltpu.VMEM((rows, total), F32),
                pltpu.VMEM((2, total, HD), F32),
                pltpu.VMEM((reach + 2, 2, rows, HD), BF16),
                pltpu.SemaphoreType.DMA((store.shape[0],)),
            ],
        ),
        out_shape=[
            jax.ShapeDtypeStruct((rows, QW), BF16),
            jax.ShapeDtypeStruct(store.shape, BF16),
        ],
        compiler_params=pltpu.CompilerParams(vmem_limit_bytes=VMEM_LIMIT),
        cost_estimate=takes(24),
        name="attend_back",
    )(place, goes, prob, qkv, branch, w_out, cosine, sine, *([store] * (2 * reach + 2)))


def out_norm_kernel(
    attended, tokens, scale, w_out, middle, own_rows, mate_rows, beyond_rows, wo, other, got, mine, send_sems, recv_sems, own_sems
):
    ctx, z = where_am_i()
    h = z % 2
    net = Net(send_sems, recv_sems)
    mate, beyond = (ctx, flip(z, 1)), (ctx, flip(z, 3))
    own, width = tokens.shape
    step = 512
    steps = width // step
    loads = []
    for k in range(steps):
        part = pl.ds(k * step, step)
        loads.append(pltpu.make_async_copy(w_out.at[part], wo.at[part], own_sems.at[k]))
        loads[k].start()
    greet([mate, beyond])
    keep = attended[pl.ds(pl.multiple_of(h * own, 16), own), :]
    give = attended[pl.ds(pl.multiple_of((1 - h) * own, 16), own), :]
    crossing = []
    for k in range(steps):
        part = pl.ds(k * step, step)
        loads[k].wait()
        other[k] = dot_t(give, wo[part, :]).astype(BF16)
        crossing.append(net.push(other.at[k], got.at[k], mate))
        crossing[k].start()
    for k in range(steps):
        part = pl.ds(k * step, step)
        middle[:, part] = tokens[:, part].astype(F32) + dot_t(keep, wo[part, :])
    square = jnp.zeros((own, 1), F32)
    for k in range(steps):
        part = pl.ds(k * step, step)
        crossing[k].wait_recv()
        value = middle[:, part] + got[k].astype(F32)
        middle[:, part] = value
        square = square + jnp.sum(value * value, -1, keepdims=True)
    r = lax.rsqrt(square / width + EPS)
    for k in range(steps):
        part = pl.ds(k * step, step)
        mine[:, part] = (middle[:, part] * r * scale[1:2, part]).astype(BF16)
    to_mate = net.push(mine, mate_rows, mate)
    to_beyond = net.push(mine, beyond_rows, beyond)
    to_mate.start()
    inner = (z == 1) | (z == 2)
    pl.when(inner)(to_beyond.start)
    local = pltpu.make_async_copy(mine, own_rows, own_sems.at[steps])
    local.start()
    for k in range(steps):
        crossing[k].wait_send()
    local.wait()
    to_mate.wait()
    pl.when(inner)(to_beyond.wait)


def out_norm(attended, tokens, scale, w_out):
    own, width = tokens.shape
    line = jax.ShapeDtypeStruct((own, width), BF16)
    return pl.pallas_call(
        out_norm_kernel,
        out_shape=[jax.ShapeDtypeStruct((own, width), F32), line, line, line],
        in_specs=[VMEM] * 3 + [ANY],
        out_specs=[VMEM] + [ANY] * 3,
        scratch_shapes=[
            pltpu.VMEM(w_out.shape, BF16),
            pltpu.VMEM((width // 512, own, 512), BF16),
            pltpu.VMEM((width // 512, own, 512), BF16),
            pltpu.VMEM((own, width), BF16),
            pltpu.SemaphoreType.DMA((width // 512 + 2,)),
            pltpu.SemaphoreType.DMA((width // 512 + 2,)),
            pltpu.SemaphoreType.DMA((width // 512 + 1,)),
        ],
        compiler_params=pltpu.CompilerParams(
            collective_id=3, has_side_effects=True, vmem_limit_bytes=VMEM_LIMIT
        ),
        cost_estimate=takes(55),
        name="out_norm",
    )(attended, tokens, scale, w_out)


def ffn_kernel(
    own_rows,
    mate_rows,
    beyond_rows,
    gate_up_w,
    rows_out,
    hidden_out,
    active_out,
    sloped_out,
    wg,
    wu,
    x,
    hidden,
    active,
    sloped,
    send_sems,
    recv_sems,
    own_sems,
    out_sems,
):
    ctx, z = where_am_i()
    net = Net(send_sems, recv_sems)
    mate, beyond = (ctx, flip(z, 1)), (ctx, flip(z, 3))
    own, width = own_rows.shape
    units = wg.shape[1]
    spans = [pl.ds(c, min(512, units - c)) for c in range(0, units, 512)]
    count = len(spans)
    inner = (z == 1) | (z == 2)
    pulls = []
    for m, src in ((0, own_rows), (1, mate_rows)):
        pulls.append(
            pltpu.make_async_copy(src, x.at[pl.ds(m * own, own)], own_sems.at[2 * count + m])
        )
        pulls[m].start()
    loads = []
    for c in range(count):
        span = spans[c]
        pair = []
        for k, dst in enumerate((wg, wu)):
            src = gate_up_w.at[:, pl.ds(k * units + span.start, span.size)]
            pair.append(pltpu.make_async_copy(src, dst.at[:, span], own_sems.at[2 * c + k]))
            pair[k].start()
        loads.append(pair)
    greet([mate, beyond])
    one_beyond = net.push(mate_rows, x.at[pl.ds(2 * own, own)], beyond)
    three_mate = net.push(beyond_rows, x.at[pl.ds(2 * own, own)], mate)
    two_mate = net.push(x.at[pl.ds(2 * own, own)], x.at[pl.ds(3 * own, own)], mate)
    three_local = pltpu.make_async_copy(
        beyond_rows, x.at[pl.ds(3 * own, own)], own_sems.at[2 * count + 2]
    )

    @pl.when(inner)
    def _():
        one_beyond.start()
        three_mate.start()
        three_local.start()

    def work(first, rows, c, ready):
        if ready is not None:
            for copy in ready:
                copy.wait()
        span = spans[c]
        at = pl.ds(first, rows)
        gate = dot(x[at, :], wg[:, span])
        up = dot(x[at, :], wu[:, span])
        root, cubic = 0.7978845608028654, 0.044715
        square = gate * gate
        bent = jnp.tanh(root * (gate + cubic * square * gate))
        value = 0.5 * gate * (1.0 + bent)
        slope = 0.5 * (1.0 + bent) + 0.5 * gate * (1.0 - bent * bent) * root * (
            1.0 + 3.0 * cubic * square
        )
        hidden[at, span] = (value * up).astype(BF16)
        active[at, span] = value.astype(BF16)
        sloped[at, span] = (slope * up).astype(BF16)

    outs = []

    def flush(m):
        at = pl.ds(m * own, own)
        pairs = ((hidden, hidden_out), (active, active_out), (sloped, sloped_out), (x, rows_out))
        for k, (src, dst) in enumerate(pairs):
            copy = pltpu.make_async_copy(src.at[at], dst.at[at], out_sems.at[4 * m + k])
            copy.start()
            outs.append(copy)

    for copy in pulls:
        copy.wait()
    for c in range(count):
        work(0, 2 * own, c, loads[c])
    flush(0)
    flush(1)

    @pl.when(inner)
    def _():
        one_beyond.wait_recv()
        two_mate.start()

    @pl.when(jnp.logical_not(inner))
    def _():
        three_mate.wait_recv()

    for c in range(count):
        work(2 * own, own, c, None)
    flush(2)

    @pl.when(inner)
    def _():
        three_local.wait()

    @pl.when(jnp.logical_not(inner))
    def _():
        two_mate.wait_recv()

    for c in range(count):
        work(3 * own, own, c, None)
    flush(3)

    @pl.when(inner)
    def _():
        for copy in (one_beyond, three_mate, two_mate):
            copy.wait_send()

    for copy in outs:
        copy.wait()


def feed_forward(own_rows, mate_rows, beyond_rows, gate_up_w):
    own, width = own_rows.shape
    units = gate_up_w.shape[1] // 2
    count = 4 * own
    inner_shape = jax.ShapeDtypeStruct((count, units), BF16)
    return pl.pallas_call(
        ffn_kernel,
        out_shape=[jax.ShapeDtypeStruct((count, width), BF16)] + [inner_shape] * 3,
        in_specs=[ANY] * 4,
        out_specs=[ANY] * 4,
        scratch_shapes=[
            pltpu.VMEM((width, units), BF16),
            pltpu.VMEM((width, units), BF16),
            pltpu.VMEM((count, width), BF16),
            pltpu.VMEM((count, units), BF16),
            pltpu.VMEM((count, units), BF16),
            pltpu.VMEM((count, units), BF16),
            pltpu.SemaphoreType.DMA((3,)),
            pltpu.SemaphoreType.DMA((3,)),
            pltpu.SemaphoreType.DMA((2 * (-(-units // 512)) + 3,)),
            pltpu.SemaphoreType.DMA((16,)),
        ],
        compiler_params=pltpu.CompilerParams(
            collective_id=6, has_side_effects=True, vmem_limit_bytes=VMEM_LIMIT
        ),
        cost_estimate=takes(52),
        name="feed_forward",
    )(own_rows, mate_rows, beyond_rows, gate_up_w)


def ffn_grad_kernel(c0, c1, c2, c3, down_w, active, sloped, cot, grad_gate, grad_up):
    own = c0.shape[0]

    @pl.when(pl.program_id(0) == 0)
    def _():
        for m, piece in enumerate((c0, c1, c2, c3)):
            cot[m * own : (m + 1) * own, :] = piece[...]

    grad = dot(cot[...], down_w[...])
    grad_gate[...] = (sloped[...].astype(F32) * grad).astype(BF16)
    grad_up[...] = (active[...].astype(F32) * grad).astype(BF16)


def ffn_specs(count, width, units):
    step = 640 if units % 640 == 0 else 128
    whole = pl.BlockSpec((count, width), lambda i: (0, 0))
    weight = pl.BlockSpec((width, step), lambda i: (0, i))
    column = pl.BlockSpec((count, step), lambda i: (0, i))
    return units // step, whole, weight, column


def feed_forward_grad(cots, down_w, active, sloped):
    own, width = cots[0].shape
    count, units = active.shape
    steps, whole, weight, column = ffn_specs(count, width, units)
    piece = pl.BlockSpec((own, width), lambda i: (0, 0))
    return pl.pallas_call(
        ffn_grad_kernel,
        grid=(steps,),
        out_shape=[jax.ShapeDtypeStruct((count, width), BF16)]
        + [jax.ShapeDtypeStruct((count, units), BF16)] * 2,
        in_specs=[piece] * 4 + [weight, column, column],
        out_specs=[whole, column, column],
        compiler_params=pltpu.CompilerParams(vmem_limit_bytes=VMEM_LIMIT),
        cost_estimate=takes(15),
        name="feed_forward_grad",
    )(*cots, down_w, active, sloped)


def ffn_back_kernel(
    grad_gate,
    grad_up,
    gate_up_w,
    down_w,
    hidden,
    rows_in,
    middle,
    cot,
    scale,
    grad_w,
    gate_sum_out,
    ffn_near,
    ffn_far,
    grad_middle,
    branch,
    grad_scale,
    gg,
    gu,
    wg,
    wu,
    x,
    parts,
    got,
    stage,
    mine,
    blocks,
    got_diag,
    got_x,
    got_y,
    send_sems,
    recv_sems,
    own_sems,
    stage_sems,
    give_sems,
    take_sems,
    sum_sems,
):
    ctx, z = where_am_i()
    net = Net(send_sems, recv_sems)
    mate, beyond = (ctx, flip(z, 1)), (ctx, flip(z, 3))
    x_dev, y_dev = (flip(ctx, 2), z), (flip(ctx, 4), z)
    inside_sum = lax.axis_size("ctx") == 8
    greet([mate, beyond, (flip(ctx, 1), z)] + ([x_dev, y_dev] if inside_sum else []))
    inner = (z == 1) | (z == 2)
    own, width = middle.shape
    units = gg.shape[1]
    step = 512
    steps = width // step
    order = (3, 2, 1, 0)
    loads = {}
    used = 0

    def load(name, src, dst):
        nonlocal used
        loads[name] = pltpu.make_async_copy(src, dst, own_sems.at[used])
        loads[name].start()
        used += 1

    for k in range(steps):
        if k < 4:
            m = order[k]
            span = pl.ds(m * own, own)
            load(("gg", m), grad_gate.at[span], gg.at[span])
            load(("gu", m), grad_up.at[span], gu.at[span])
        part = pl.ds(k * step, step)
        load(("wg", k), gate_up_w.at[part, pl.ds(0, units)], wg.at[part])
        load(("wu", k), gate_up_w.at[part, pl.ds(units, units)], wu.at[part])
    load("x", rows_in, x)

    far = net.push(parts.at[3], got.at[0], mate)
    near = net.push(parts.at[2], got.at[1], mate)
    two_over = net.push(parts.at[2], got.at[2], beyond)
    three_over = net.push(parts.at[3], got.at[3], beyond)
    one_mate = net.push(parts.at[1], got.at[4], mate)

    def make(m):
        span = pl.ds(m * own, own)
        loads["gg", m].wait()
        loads["gu", m].wait()
        for k in range(steps):
            part = pl.ds(k * step, step)
            if m == 3:
                loads["wg", k].wait()
                loads["wu", k].wait()
            value = dot_t(gg[span, :], wg[part, :]) + dot_t(gu[span, :], wu[part, :])
            parts[m, :, part] = value.astype(BF16)

    def add_to(m, k):
        parts[m] = (parts[m].astype(F32) + got[k].astype(F32)).astype(BF16)

    make(3)
    pl.when(jnp.logical_not(inner))(far.start)
    make(2)
    pl.when(jnp.logical_not(inner))(near.start)
    make(1)
    make(0)
    load("wd", down_w, wg)
    loads["x"].wait()

    block = 2 * width // lax.axis_size("ctx")
    chips = width // block
    chunk = stage.shape[1]
    sib = (flip(ctx, 1), z)
    core = ctx % 2
    side = block // 2
    first_cols = stage.shape[2]
    slices = ((0, first_cols), (first_cols, units - first_cols))
    inside = chunk // block
    rounds = width // chunk
    keep_at_of, take_at_of = (0, 1, 1), (0, 1, 0)

    def chip_copies(which, i, n):
        cols = pl.ds(*slices[n])
        used_cols = pl.ds(0, slices[n][1])
        keeps, gives = [], []
        for part in range(inside):
            k = i * inside + part
            sem = (which * chips + k) * 2 + n
            keep_rows = pl.ds(pl.multiple_of((keep_at_of[which] * chips + k) * side, 16), side)
            take_rows = pl.ds(pl.multiple_of((take_at_of[which] * chips + k) * side, 16), side)
            mine_at = pl.ds(pl.multiple_of(part * block + core * side, 16), side)
            give_at = pl.ds(pl.multiple_of(part * block + (1 - core) * side, 16), side)
            keeps.append(
                pltpu.make_async_copy(
                    stage.at[n, mine_at, used_cols], wu.at[keep_rows, cols], stage_sems.at[sem]
                )
            )
            gives.append(
                pltpu.make_async_remote_copy(
                    src_ref=stage.at[n, give_at, used_cols],
                    dst_ref=blocks.at[take_rows, cols],
                    send_sem=give_sems.at[sem],
                    recv_sem=take_sems.at[sem],
                    device_id=sib,
                    device_id_type=MESH,
                )
            )
        return keeps, gives

    def weight_grad(g, which):
        def done(i, n):
            keeps, gives = chip_copies(which, i, n)
            for copy in keeps:
                copy.wait()
            for copy in gives:
                copy.wait_send()

        def body(i, carry):
            rows = pl.ds(pl.multiple_of(i * chunk, 128), chunk)
            for n in range(2):
                pl.when(i >= 1)(lambda: done(i - 1, n))
                cols = pl.ds(*slices[n])
                stage[n, :, : slices[n][1]] = t_dot(x[:, rows], g[:, cols]).astype(BF16)
                keeps, gives = chip_copies(which, i, n)
                for copy in keeps + gives:
                    copy.start()
            return carry

        lax.fori_loop(0, rounds, body, 0)
        done(rounds - 1, 0)
        done(rounds - 1, 1)

    def add_cores(which):
        first, second = keep_at_of[which] * chips * side, take_at_of[which] * chips * side

        def arrived(i, carry):
            for n in range(2):
                for copy in chip_copies(which, i, n)[1]:
                    copy.wait_recv()
            return carry

        lax.fori_loop(0, rounds, arrived, 0)
        unit = 16

        def body(i, carry):
            at = pl.ds(pl.multiple_of(first + i * unit, unit), unit)
            other = blocks[pl.ds(pl.multiple_of(second + i * unit, unit), unit), :]
            wu[at, :] = (wu[at, :].astype(F32) + other.astype(F32)).astype(BF16)
            return carry

        lax.fori_loop(0, chips * side // unit, body, 0)
        if inside_sum and which == 0:
            return None
        first_col = (which - 1 if inside_sum else which) * units
        copy = pltpu.make_async_copy(
            wu.at[pl.ds(first, chips * side)],
            grad_w.at[:, pl.ds(first_col, units)],
            sum_sems.at[which],
        )
        copy.start()
        return copy

    chip_copies_of_gate = []

    def gate_block(m, first, count):
        start = flip(ctx // 2, m) * side + first
        return wu.at[pl.ds(pl.multiple_of(start, 16), count)]

    def gate_diag():
        for k, to in enumerate((y_dev, x_dev)):
            copy = net.push(
                gate_block(3, k * side // 2, side // 2),
                got_diag.at[pl.ds(k * side // 2, side // 2)],
                to,
            )
            copy.start()
            chip_copies_of_gate.append(copy)

    def rows_loop(count, one):
        unit = 16

        def body(i, carry):
            one(i * unit, unit)
            return carry

        lax.fori_loop(0, count // unit, body, 0)

    def gate_near():
        for k, (to, got_from) in enumerate(((x_dev, got_x), (y_dev, got_y))):
            chip_copies_of_gate[k].wait_recv()
            start = flip(ctx // 2, 1 + k) * side + k * side // 2

            def one(first, unit):
                at = pl.ds(pl.multiple_of(start + first, unit), unit)
                other = got_diag[pl.ds(pl.multiple_of(k * side // 2 + first, unit), unit), :]
                wu[at, :] = (wu[at, :].astype(F32) + other.astype(F32)).astype(BF16)

            rows_loop(side // 2, one)
            copy = net.push(gate_block(1 + k, 0, side), got_from, to)
            copy.start()
            chip_copies_of_gate.append(copy)

    def gate_total():
        for copy in chip_copies_of_gate[2:]:
            copy.wait_recv()

        def one(first, unit):
            at = pl.ds(pl.multiple_of(first, unit), unit)
            own_at = pl.ds(pl.multiple_of(ctx // 2 * side + first, unit), unit)
            value = wu[own_at, :].astype(F32) + got_x[at, :].astype(F32)
            got_diag[at, :] = (value + got_y[at, :].astype(F32)).astype(BF16)

        rows_loop(side, one)
        copy = pltpu.make_async_copy(got_diag, gate_sum_out, sum_sems.at[0])
        copy.start()
        for other in chip_copies_of_gate:
            other.wait_send()
        copy.wait()

    @pl.when(inner)
    def _():
        far.wait_recv()
        add_to(2, 0)
        two_over.start()

    weight_grad(gg, 0)
    gate_sum = add_cores(0)
    if inside_sum:
        gate_diag()

    @pl.when(inner)
    def _():
        near.wait_recv()
        add_to(3, 1)
        three_over.start()
        two_over.wait_recv()
        add_to(1, 2)

    one_mate.start()
    weight_grad(gu, 1)
    if inside_sum:
        gate_near()
    load("hidden", hidden, gu)
    load("cot", cot, x)
    up_sum = add_cores(1)
    loads["cot"].wait()
    one_mate.wait_recv()
    pl.when(inner)(three_over.wait_recv)

    def norm_rows(i, scale_sum):
        at = pl.ds(pl.multiple_of(i * 16, 16), 16)
        grad = parts[0, at, :].astype(F32) + got[4, at, :].astype(F32)
        grad = grad + jnp.where(inner, got[3, at, :].astype(F32), 0.0)
        value = middle[at, :]
        r = inv_rms(value)
        scaled = grad * scale[1:2, :]
        lean = jnp.mean(scaled * value, -1, keepdims=True)
        total = x[at, :].astype(F32) + (r * scaled - value * (r * r * r * lean))
        grad_middle[at, :] = total
        mine[at, :] = total.astype(BF16)
        return scale_sum + jnp.sum(grad * value * r, 0, keepdims=True)

    grad_scale[...] = lax.fori_loop(0, own // 16, norm_rows, jnp.zeros((1, width), F32))
    dst = branch.at[pl.ds(pl.multiple_of((z % 2) * own, 16), own)]
    last = net.push(mine, dst, mate)
    last.start()
    local = pltpu.make_async_copy(mine, dst, own_sems.at[used])
    local.start()
    loads["hidden"].wait()
    up_sum.wait()
    weight_grad(gu, 2)
    down_sum = add_cores(2)
    one_mate.wait_send()

    @pl.when(inner)
    def _():
        two_over.wait_send()
        three_over.wait_send()

    @pl.when(jnp.logical_not(inner))
    def _():
        far.wait_send()
        near.wait_send()

    loads["wd"].wait()
    out_copies = []
    for m in order:
        span = pl.ds(m * own, own)
        for k in range(steps):
            part = pl.ds(k * step, step)
            parts[m, :, part] = dot_t(gu[span, :], wg[part, :]).astype(BF16)
        dst = ffn_near.at[m] if m < 2 else ffn_far.at[m - 2]
        copy = pltpu.make_async_copy(parts.at[m], dst, own_sems.at[used + 1 + m])
        copy.start()
        out_copies.append(copy)
    local.wait()
    if inside_sum:
        gate_total()
    else:
        gate_sum.wait()
    down_sum.wait()
    last.wait_recv()
    last.wait_send()
    for copy in out_copies:
        copy.wait()


def feed_forward_back(grad_gate, grad_up, gate_up_w, down_w, hidden, rows_in, middle, cot, scale):
    own, width = middle.shape
    count, units = hidden.shape
    block = 2 * width // lax.axis_size("ctx")
    chunk = block if block % 128 == 0 else 640
    inside_sum = lax.axis_size("ctx") == 8
    rounds = width // block * 2
    return pl.pallas_call(
        ffn_back_kernel,
        out_shape=[
            jax.ShapeDtypeStruct((width // 2, (2 if inside_sum else 3) * units), BF16),
            jax.ShapeDtypeStruct((block // 2, units), BF16),
            jax.ShapeDtypeStruct((2, own, width), BF16),
            jax.ShapeDtypeStruct((2, own, width), BF16),
            jax.ShapeDtypeStruct((own, width), F32),
            jax.ShapeDtypeStruct((2 * own, width), BF16),
            jax.ShapeDtypeStruct((1, width), F32),
        ],
        in_specs=[ANY] * 6 + [VMEM, ANY, VMEM],
        out_specs=[ANY, ANY, ANY, ANY, VMEM, ANY, VMEM],
        scratch_shapes=[
            pltpu.VMEM((count, units), BF16),
            pltpu.VMEM((count, units), BF16),
            pltpu.VMEM((width, units), BF16),
            pltpu.VMEM((width, units), BF16),
            pltpu.VMEM((count, width), BF16),
            pltpu.VMEM((4, own, width), BF16),
            pltpu.VMEM((5, own, width), BF16),
            pltpu.VMEM((2, chunk, -(-units // 256) * 128), BF16),
            pltpu.VMEM((own, width), BF16),
            pltpu.VMEM((width, units), BF16),
            pltpu.VMEM((block // 2, units), BF16),
            pltpu.VMEM((block // 2, units), BF16),
            pltpu.VMEM((block // 2, units), BF16),
            pltpu.SemaphoreType.DMA((10,)),
            pltpu.SemaphoreType.DMA((10,)),
            pltpu.SemaphoreType.DMA((8 + 2 * (width // 512) + 9,)),
            pltpu.SemaphoreType.DMA((3 * rounds,)),
            pltpu.SemaphoreType.DMA((3 * rounds,)),
            pltpu.SemaphoreType.DMA((3 * rounds,)),
            pltpu.SemaphoreType.DMA((3,)),
        ],
        compiler_params=pltpu.CompilerParams(
            collective_id=5, has_side_effects=True, vmem_limit_bytes=62 * 1024 * 1024
        ),
        cost_estimate=takes(100),
        name="feed_forward_back",
    )(grad_gate, grad_up, gate_up_w, down_w, hidden, rows_in, middle, cot, scale)


def fold(ref, other):
    ref[...] = (ref[...].astype(F32) + other[...].astype(F32)).astype(BF16)


class KvSum:
    def __init__(self, net, parts, out, mine, got_sib, got_diag, got_x, got_y, got_z, give, sems):
        ctx, z = where_am_i()
        self.h, self.upper = z % 2, z // 2 == 1
        self.refs = (out, mine, got_sib, got_diag, got_x, got_y, got_z, give)
        x_dev, y_dev, sib = (flip(ctx, 2), z), (flip(ctx, 4), z), (flip(ctx, 1), z)
        self.load, self.over, self.diag, self.near = {}, {}, {}, {}
        for s in range(2):
            for i, m in enumerate((6, 2, 4, 0)):
                self.load[s, i] = pltpu.make_async_copy(
                    parts.at[s, flip(ctx, m)], mine.at[s, i], sems.at[4 * s + i]
                )
                self.over[s, i] = net.push(
                    parts.at[s, flip(flip(ctx, 1), m)], got_sib.at[s, i], sib
                )
            self.diag[s] = [
                net.push(mine.at[s, 0, 0], got_diag.at[s, 0], y_dev),
                net.push(mine.at[s, 0, 1], got_diag.at[s, 1], x_dev),
            ]
            self.near[s] = [
                net.push(mine.at[s, 1], got_x.at[s], x_dev),
                net.push(mine.at[s, 2], got_y.at[s], y_dev),
            ]
        self.to_mate = net.push(give.at[0], got_z.at[0], (ctx, flip(z, 1)))
        self.to_low = net.push(give.at[1], got_z.at[1], (ctx, flip(z, 2)))
        self.to_low_mate = net.push(give.at[2], got_z.at[2], (ctx, flip(z, 3)))

    def both(self, stage):
        stage(0)
        pl.when(self.upper)(lambda: stage(1))

    def start(self, s):
        for i in range(4):
            self.over[s, i].start()
            self.load[s, i].start()

    def chip_sums(self, s):
        mine, got_sib = self.refs[1:3]
        for i in range(4):
            self.load[s, i].wait()
            self.over[s, i].wait_recv()
            fold(mine.at[s, i], got_sib.at[s, i])
            if i == 0:
                for copy in self.diag[s]:
                    copy.start()

    def forward(self, s):
        mine, got_diag = self.refs[1], self.refs[3]
        for k in range(2):
            self.diag[s][k].wait_recv()
            fold(mine.at[s, 1 + k, k], got_diag.at[s, k])
            self.near[s][k].start()

    def total(self, s, kind):
        mine, got_x, got_y = self.refs[1], self.refs[4], self.refs[5]
        value = mine[s, 3, kind].astype(F32) + got_x[s, kind].astype(F32)
        return value + got_y[s, kind].astype(F32)

    def across(self):
        out, give, h = self.refs[0], self.refs[7], self.h
        for copy in self.near[0]:
            copy.wait_recv()

        @pl.when(jnp.logical_not(self.upper))
        def _():
            give[0] = self.total(0, 1 - h).astype(BF16)
            out[...] = self.total(0, h)

        @pl.when(self.upper)
        def _():
            give[1] = self.total(0, h).astype(BF16)
            give[2] = self.total(0, 1 - h).astype(BF16)
            self.to_low.start()
            self.to_low_mate.start()
            for copy in self.near[1]:
                copy.wait_recv()
            give[0] = self.total(1, 1 - h).astype(BF16)
            out[...] = self.total(1, h)

        self.to_mate.start()

    def finish(self):
        out, got_z = self.refs[0], self.refs[6]
        self.to_mate.wait_recv()
        out[...] += got_z[0].astype(F32)

        @pl.when(jnp.logical_not(self.upper))
        def _():
            self.to_low.wait_recv()
            self.to_low_mate.wait_recv()
            out[...] += got_z[1].astype(F32) + got_z[2].astype(F32)

        def sent(s):
            for i in range(4):
                self.over[s, i].wait_send()
            for copy in self.diag[s] + self.near[s]:
                copy.wait_send()

        self.both(sent)
        self.to_mate.wait_send()

        @pl.when(self.upper)
        def _():
            self.to_low.wait_send()
            self.to_low_mate.wait_send()

    @staticmethod
    def scratch(rows):
        block = (2, rows, HD)
        return [
            pltpu.VMEM((2, 4) + block, BF16),
            pltpu.VMEM((2, 4) + block, BF16),
            pltpu.VMEM((2, 2, rows, HD), BF16),
            pltpu.VMEM((2,) + block, BF16),
            pltpu.VMEM((2,) + block, BF16),
            pltpu.VMEM((3, rows, HD), BF16),
            pltpu.VMEM((3, rows, HD), BF16),
            pltpu.SemaphoreType.DMA((8,)),
        ]

    copies = 19


class WeightSum:
    def __init__(self, net, widths, parts, put, mine, got_sib, got_diag, got_x, got_y, got_z, total, sems):
        ctx, z = where_am_i()
        self.net, self.z = net, z
        self.ctx = ctx
        self.parts, self.put, self.sems = parts, put, sems
        self.refs = (mine, got_sib, got_diag, got_x, got_y, got_z, total)
        self.x_dev, self.y_dev, self.sib = (flip(ctx, 2), z), (flip(ctx, 4), z), (flip(ctx, 1), z)
        self.rows = mine.shape[1]
        self.copies = {}
        self.spans, col = [], 0
        for count in widths:
            self.spans.append(pl.ds(col, count))
            col += count

    def add_to(self, ref, other, count):
        step = 32

        def body(i, carry):
            at = pl.ds(pl.multiple_of(i * step, step), step)
            ref[at, :] = (ref[at, :].astype(F32) + other[at, :].astype(F32)).astype(BF16)
            return carry

        lax.fori_loop(0, count // step, body, 0)

    def start(self, g):
        mine, got_sib = self.refs[:2]
        span, rows, ctx = self.spans[g], self.rows, self.ctx

        def block_rows(source):
            return pl.ds(pl.multiple_of(source * rows, 16), rows)

        for i, m in enumerate((6, 2, 4, 0)):
            load = pltpu.make_async_copy(
                self.parts.at[block_rows(flip(ctx, m)), span],
                mine.at[i, :, span],
                self.sems.at[4 * g + i],
            )
            over = self.net.push(
                self.parts.at[block_rows(flip(flip(ctx, 1), m)), span],
                got_sib.at[i, :, span],
                self.sib,
            )
            load.start()
            over.start()
            self.copies[g, i] = (load, over)

    def chip_sums(self, g):
        mine, got_sib, got_diag = self.refs[:3]
        span, rows = self.spans[g], self.rows
        cut = rows // 2
        for i in range(4):
            load, over = self.copies[g, i]
            if load is not None:
                load.wait()
            over.wait_recv()
            self.add_to(mine.at[i, :, span], got_sib.at[i, :, span], rows)
            if i == 0:
                pair = []
                for k, to in enumerate((self.y_dev, self.x_dev)):
                    part = pl.ds(k * cut, cut)
                    pair.append(self.net.push(mine.at[0, part, span], got_diag.at[part, span], to))
                    pair[k].start()
                self.copies[g, "diag"] = pair

    def forward(self, g):
        mine, _, got_diag, got_x, got_y = self.refs[:5]
        span = self.spans[g]
        cut = self.rows // 2
        pair = []
        for k, (got, to) in enumerate(((got_x, self.x_dev), (got_y, self.y_dev))):
            part = pl.ds(k * cut, cut)
            self.copies[g, "diag"][k].wait_recv()
            self.add_to(mine.at[1 + k, part, span], got_diag.at[part, span], cut)
            pair.append(self.net.push(mine.at[1 + k, :, span], got.at[:, span], to))
            pair[k].start()
        self.copies[g, "near"] = pair

    def line(self, g):
        mine, _, _, got_x, got_y, got_z, total = self.refs
        span, rows, z = self.spans[g], self.rows, self.z
        unit = rows // 4
        for copy in self.copies[g, "near"]:
            copy.wait_recv()
        step = 16

        def body(i, carry):
            at = pl.ds(pl.multiple_of(i * step, step), step)
            value = mine[3, at, span].astype(F32) + got_x[at, span].astype(F32)
            total[at, span] = (value + got_y[at, span].astype(F32)).astype(BF16)
            return carry

        lax.fori_loop(0, rows // step, body, 0)
        sends = []
        for k, m in enumerate((1, 2, 3)):
            start_row = pl.multiple_of(flip(z, m) * unit, 16)
            copy = self.net.push(
                total.at[pl.ds(start_row, unit), span],
                got_z.at[k, :, span],
                (self.ctx, flip(z, m)),
            )
            copy.start()
            sends.append(copy)
        self.copies[g, "line"] = sends

    def finish(self, g):
        got_z, total = self.refs[5:]
        span, unit = self.spans[g], self.rows // 4
        for copy in self.copies[g, "line"]:
            copy.wait_recv()
        own_row = pl.multiple_of(self.z * unit, 16)
        h = self.z % 2
        own_cols = total[pl.ds(own_row, unit), span].astype(F32) + got_z[1, :, span].astype(F32)
        self.put(h, span, own_cols)
        self.put(1 - h, span, got_z[0, :, span].astype(F32) + got_z[2, :, span].astype(F32))
        for i in range(4):
            self.copies[g, i][1].wait_send()
        for name in ("diag", "near", "line"):
            for copy in self.copies[g, name]:
                copy.wait_send()

    @staticmethod
    def scratch(rows, shard, columns, groups):
        return [
            pltpu.VMEM((4, rows, columns), BF16),
            pltpu.VMEM((4, rows, columns), BF16),
            pltpu.VMEM((rows, columns), BF16),
            pltpu.VMEM((rows, columns), BF16),
            pltpu.VMEM((rows, columns), BF16),
            pltpu.VMEM((3, shard, columns), BF16),
            pltpu.VMEM((rows, columns), BF16),
            pltpu.SemaphoreType.DMA((4 * groups,)),
        ]


def everyone():
    ctx, z = where_am_i()
    return [(ctx, flip(z, m)) for m in (1, 2, 3)] + [(flip(ctx, m), z) for m in (1, 2, 4)]


def first_sums_kernel(kv_parts, near_parts, far_parts, come, kv_out, one_out, three_out, *scratch):
    ctx, z = where_am_i()
    kv_scratch, scratch = scratch[:8], scratch[8:]
    parts, got, send_sems, recv_sems, own_sems = scratch
    net = Net(send_sems, recv_sems)
    greet(everyone())
    beyond = (ctx, flip(z, 3))
    inner = (z == 1) | (z == 2)
    kv = KvSum(net, kv_parts, kv_out, *kv_scratch)
    two_over = net.push(parts.at[1], got, beyond)
    loads = []
    sources = (near_parts.at[1], far_parts.at[0], far_parts.at[1], come.at[0], come.at[1])
    for m, src in enumerate(sources):
        loads.append(pltpu.make_async_copy(src, parts.at[m], own_sems.at[m]))
        loads[m].start()
    kv.both(kv.start)
    for copy in loads:
        copy.wait()

    @pl.when(inner)
    def _():
        fold(parts.at[1], parts.at[4])
        two_over.start()
        fold(parts.at[2], parts.at[3])

    three = pltpu.make_async_copy(parts.at[2], three_out, own_sems.at[0])
    three.start()
    kv.both(kv.chip_sums)
    kv.both(kv.forward)
    kv.across()

    @pl.when(inner)
    def _():
        two_over.wait_recv()
        fold(parts.at[0], got)
        two_over.wait_send()

    one = pltpu.make_async_copy(parts.at[0], one_out, own_sems.at[1])
    one.start()
    kv.finish()
    three.wait()
    one.wait()


def plain_axes(shard):
    return lax.axis_size("ctx") != 8 or lax.axis_size("fsdp") != 4 or shard % 16


def plain_weight_sum(parts):
    z = lax.axis_index("fsdp")
    empty = jnp.zeros_like(parts)
    both = jnp.where(z % 2 == 0, jnp.stack([parts, empty]), jnp.stack([empty, parts]))
    summed = lax.psum_scatter(both, "ctx", scatter_dimension=1, tiled=True)
    return lax.psum_scatter(summed, "fsdp", scatter_dimension=1, tiled=True).astype(F32)


def first_sums(kv_parts, near_parts, far_parts, middle, shard):
    total, _, rows, _ = kv_parts.shape
    ctx_total = total // 2
    kv_parts = kv_parts.reshape(2, ctx_total, 2, rows, HD)
    own, width = middle.shape
    if plain_axes(shard):
        flat = kv_parts.transpose(0, 2, 1, 3, 4).reshape(4 * ctx_total * rows, HD)
        z_sum = lax.psum_scatter(flat, "fsdp", scatter_dimension=0, tiled=True)
        kv = lax.psum_scatter(z_sum, "ctx", scatter_dimension=0, tiled=True).astype(F32)
        out = middle + near_parts[0].astype(F32)
        for m in (1, 2, 3):
            part = near_parts[m] if m < 2 else far_parts[m - 2]
            out = out + swap(part, "fsdp", m).astype(F32)
        return kv, out.astype(BF16)
    copies = KvSum.copies + 1
    come = lax.ppermute(far_parts, "fsdp", [(0, 1), (3, 2)])
    line = jax.ShapeDtypeStruct((own, width), BF16)
    kv, one, three = pl.pallas_call(
        first_sums_kernel,
        out_shape=[jax.ShapeDtypeStruct((rows, HD), F32), line, line],
        in_specs=[ANY] * 4,
        out_specs=[VMEM, ANY, ANY],
        scratch_shapes=KvSum.scratch(rows)
        + [
            pltpu.VMEM((5, own, width), BF16),
            pltpu.VMEM((own, width), BF16),
            pltpu.SemaphoreType.DMA((copies,)),
            pltpu.SemaphoreType.DMA((copies,)),
            pltpu.SemaphoreType.DMA((5,)),
        ],
        compiler_params=pltpu.CompilerParams(
            collective_id=2, has_side_effects=True, vmem_limit_bytes=60 * 1024 * 1024
        ),
        cost_estimate=takes(45),
        name="first_sums",
    )(kv_parts, near_parts, far_parts, come)
    out = middle + near_parts[0].astype(F32) + swap(one, "fsdp", 1).astype(F32)
    out = out + lax.ppermute(three, "fsdp", [(1, 2), (2, 1)]).astype(F32)
    return kv, out.astype(BF16)


def last_sums_kernel(
    widths, out_widths, out_parts, w_qkv, grad_q, grad_kv, cosine, sine, normed, tokens, scale, grad_middle, ffn_scale_grad, *refs
):
    ctx, z = where_am_i()
    q_out, k_out, v_out, o_out, grad_tokens, scales = refs[:6]
    w_scratch, o_scratch, scratch = refs[6:14], refs[14:22], refs[22:]
    give_w, product, w, grads, grad_own, give, got, scale_got, send_sems, recv_sems, own_sems = scratch
    h, core, chip = z % 2, ctx % 2, ctx // 2
    net = Net(send_sems, recv_sems)
    own, width = tokens.shape
    step = 512
    steps = width // step
    loads = []
    for k in range(steps):
        part = pl.ds(k * step, step)
        loads.append(pltpu.make_async_copy(w_qkv.at[part], w.at[part], own_sems.at[k]))
        loads[k].start()
    greet(everyone() + [(flip(ctx, m), z) for m in (3, 5, 6, 7)])

    def put_out(which, span, value):
        o_out[:, pl.ds(pl.multiple_of(which * QW + span.start, 128), span.size)] = value

    outs = WeightSum(net, out_widths, out_parts, put_out, *o_scratch)
    outs.start(0)
    outs.start(1)
    grads[:, :QW] = grad_q[...]
    front, back = grad_kv[:, : HD // 2], grad_kv[:, HD // 2 :]
    c, s = cosine[...], sine[...]
    grads[:, QW : QW + HD // 2] = (front * c + back * s).astype(BF16)
    grads[:, QW + HD // 2 :] = (back * c - front * s).astype(BF16)

    def put(which, span, value):
        if span.start < QW:
            q_out[:, pl.ds(pl.multiple_of(which * QW + span.start, 128), span.size)] = value
            return

        @pl.when(which == 0)
        def _():
            k_out[...] = value

        @pl.when(which == 1)
        def _():
            v_out[...] = value

    weights = WeightSum(net, widths, None, put, *w_scratch)
    mine, got_sib = w_scratch[:2]
    side = mine.shape[1]

    def produce(g):
        span = weights.spans[g]
        for i, m in enumerate((3, 1, 2, 0)):
            cols = pl.ds(pl.multiple_of(flip(chip, m) * 2 * side, 128), 2 * side)
            product[:, : span.size] = t_dot(normed[:, cols], grads[:, span]).astype(BF16)
            keep_at = pl.ds(pl.multiple_of(core * side, 16), side)
            give_at = pl.ds(pl.multiple_of((1 - core) * side, 16), side)
            mine[i, :, span] = product[keep_at, : span.size]
            give_w[i, :, span] = product[give_at, : span.size]
            over = net.push(give_w.at[i, :, span], got_sib.at[i, :, span], weights.sib)
            over.start()
            weights.copies[g, i] = (None, over)

    outs.chip_sums(0)
    outs.chip_sums(1)
    outs.forward(0)
    other_grads = grads[pl.ds(pl.multiple_of((1 - h) * own, 16), own), :]
    crossing = []
    for k in range(steps):
        loads[k].wait()
        give[k] = dot_t(other_grads, w[pl.ds(k * step, step), :]).astype(BF16)
        crossing.append(net.push(give.at[k], got.at[k], (ctx, flip(z, 1))))
        crossing[k].start()
    line_mates = [(ctx, flip(z, m)) for m in (1, 2, 3)]
    plane_mates = [(flip(ctx, m), z) for m in range(1, 8)]
    trade = []

    def trade_send(mates):
        for to in mates:
            trade.append(net.push(scales, scale_got.at[len(trade)], to))
            trade[-1].start()

    def trade_add(first, count):
        for k in range(first, first + count):
            trade[k].wait()
        for k in range(first, first + count):
            scales[...] += scale_got[k]

    def own_part():
        own_grads = grads[pl.ds(pl.multiple_of(h * own, 16), own), :]
        for k in range(steps):
            part = pl.ds(k * step, step)
            grad_own[:, part] = dot_t(own_grads, w[part, :])

    def norm_part():
        value = tokens[...].astype(F32)
        for k in range(steps):
            crossing[k].wait_recv()
            grad_own[:, pl.ds(k * step, step)] += got[k].astype(F32)
        grad = grad_own[...]
        r = inv_rms(value)
        scaled = grad * scale[0:1, :]
        lean = jnp.mean(scaled * value, -1, keepdims=True)
        grad_tokens[...] = grad_middle[...] + (r * scaled - value * (r * r * r * lean))
        rows = [jnp.sum(grad * value * r, 0, keepdims=True), ffn_scale_grad[...]]
        quarter = width // 4
        for i in range(8):
            scales[i : i + 1, :] = rows[i // 4][:, i % 4 * quarter : (i % 4 + 1) * quarter]
        trade_send(line_mates)

    outs.forward(1)
    produce(0)
    weights.chip_sums(0)
    produce(1)
    weights.chip_sums(1)
    outs.line(0)
    weights.forward(0)
    outs.line(1)
    produce(2)
    weights.chip_sums(2)
    weights.forward(1)
    own_part()
    norm_part()
    weights.line(0)
    weights.forward(2)
    trade_add(0, 3)
    trade_send(plane_mates)
    weights.line(1)
    outs.finish(0)
    outs.finish(1)
    weights.line(2)
    trade_add(3, 7)
    weights.finish(0)
    weights.finish(1)
    weights.finish(2)
    for copy in crossing:
        copy.wait_send()


def last_sums(out_parts, w_qkv, grad_q, grad_kv, cosine, sine, normed, tokens, scale, grad_middle, ffn_scale_grad, shard):
    own, width = tokens.shape
    columns = w_qkv.shape[1]
    if plain_axes(shard):
        h = lax.axis_index("fsdp") % 2
        front, back = grad_kv[:, : HD // 2], grad_kv[:, HD // 2 :]
        c, s = cosine, sine
        grad_kv = jnp.concatenate([front * c + back * s, back * c - front * s], 1).astype(BF16)
        grads = jnp.concatenate([grad_q, grad_kv], 1)
        both = plain_weight_sum(t_dot(normed, grads).astype(BF16))
        grad_rows = dot_t(grads, w_qkv)
        other = swap(half(grad_rows, 1 - h).astype(BF16), "fsdp", 1).astype(F32)
        grad, scale_grad = norm_back(tokens.astype(F32), scale[:1], half(grad_rows, h) + other)
        scales = jnp.concatenate([scale_grad[None], ffn_scale_grad])
        queries = jnp.concatenate([both[0, :, :QW], both[1, :, :QW]], 1)
        scales = lax.psum(scales, ("ctx", "fsdp"))
        outs = plain_weight_sum(out_parts)
        outs = jnp.concatenate([outs[0], outs[1]], 1)
        return queries, both[0, :, QW:], both[1, :, QW:], outs, grad_middle + grad, scales
    block = 4 * shard
    rows = normed.shape[0]
    widths = (QW // 2, QW // 2, HD)
    steps = width // 512
    out_widths = (QW // 2, QW // 2)
    copies = 11 * (len(widths) + len(out_widths)) + steps + 10
    *weights, scales = pl.pallas_call(
        functools.partial(last_sums_kernel, widths, out_widths),
        out_shape=[
            jax.ShapeDtypeStruct((shard, 2 * QW), F32),
            jax.ShapeDtypeStruct((shard, HD), F32),
            jax.ShapeDtypeStruct((shard, HD), F32),
            jax.ShapeDtypeStruct((shard, 2 * QW), F32),
            jax.ShapeDtypeStruct((own, width), F32),
            jax.ShapeDtypeStruct((8, width // 4), F32),
        ],
        in_specs=[ANY] * 2 + [VMEM] * 9,
        out_specs=[VMEM] * 6,
        scratch_shapes=WeightSum.scratch(block, shard, columns, len(widths))
        + WeightSum.scratch(block, shard, QW, len(out_widths))
        + [
            pltpu.VMEM((4, block, columns), BF16),
            pltpu.VMEM((2 * block, QW // 2), BF16),
            pltpu.VMEM((width, columns), BF16),
            pltpu.VMEM((rows, columns), BF16),
            pltpu.VMEM((own, width), F32),
            pltpu.VMEM((steps, own, 512), BF16),
            pltpu.VMEM((steps, own, 512), BF16),
            pltpu.VMEM((10, 8, width // 4), F32),
            pltpu.SemaphoreType.DMA((copies,)),
            pltpu.SemaphoreType.DMA((copies,)),
            pltpu.SemaphoreType.DMA((steps,)),
        ],
        compiler_params=pltpu.CompilerParams(
            collective_id=4, has_side_effects=True, vmem_limit_bytes=60 * 1024 * 1024
        ),
        cost_estimate=takes(60),
        name="last_sums",
    )(out_parts, w_qkv, grad_q, grad_kv, cosine, sine, normed, tokens, scale, grad_middle, ffn_scale_grad)
    return *weights, scales.reshape(2, width)


def local(
    tokens,
    lengths,
    block_place,
    gain_attn,
    w_query,
    w_key,
    w_value,
    w_out,
    gain_ffn,
    w_gate,
    w_up,
    w_down,
    cotangent,
):
    own_rows, width = tokens.shape
    rows = 2 * own_rows
    ctx_total = lax.axis_size("ctx")
    ctx, z = where_am_i()
    h, pair = z % 2, z // 2
    shard = w_query.shape[0]
    reach = -(-WIN // rows)

    def place_of(stored):
        hit = jnp.arange(block_place.shape[0])[None, :] == stored[:, None]
        return jnp.sum(jnp.where(hit, block_place[None, :], 0), 1)

    own_pos = place_of((2 * ctx + pair)[None])[0]
    query_at = own_pos * rows + jnp.arange(rows, dtype=jnp.int32)
    passed = query_at[:, None] >= jnp.cumsum(lengths)[None, :]
    doc_start = jnp.sum(jnp.where(passed, lengths[None, :], 0), 1)
    rel_pos = query_at - doc_start
    window_start = (own_pos - reach) * rows
    lowest = jnp.maximum(doc_start, query_at - WIN + 1) - window_start
    lowest = jnp.broadcast_to(lowest[:, None], (rows, 128)).astype(jnp.int32)
    holders = jnp.arange(ctx_total)
    held = jnp.concatenate([place_of(2 * holders), place_of(2 * holders + 1)])
    held = jnp.where((pair == 1) | (jnp.arange(2 * ctx_total) < ctx_total), held, -1000)
    want = own_pos - reach + jnp.arange(reach + 1)
    hit = held[None, :] == want[:, None]
    numbers = jnp.arange(2 * ctx_total)
    own_index = pair * ctx_total + ctx
    place = jnp.where(jnp.any(hit, 1), jnp.sum(jnp.where(hit, numbers, 0), 1), own_index)
    place = place.astype(jnp.int32)
    goes = held - (own_pos - reach)
    goes = jnp.where((goes >= 0) & (goes <= reach), goes, reach + 1).astype(jnp.int32)
    half_dim = HD // 2
    frequency = jnp.exp(jnp.arange(half_dim, dtype=F32) * (-jnp.log(10000.0) / half_dim))
    angles = rel_pos.astype(F32)[:, None] * frequency
    cosine, sine = jnp.cos(angles), jnp.sin(angles)
    q_scale = HD ** (-0.5)
    kv_cosine, kv_sine = jnp.where(h == 0, cosine, 1.0), jnp.where(h == 0, sine, 0.0)
    cosine = jnp.stack([cosine * q_scale, kv_cosine])
    sine = jnp.stack([sine * q_scale, kv_sine])

    gate_up_shard = jnp.concatenate([w_gate, w_up], 1)
    down_shard = w_down.T
    w_qkv, w_o, gains, rows_in, cot_one, cot_three = gather_weights(
        w_query, w_key, w_value, w_out, gain_attn, gain_ffn, tokens, cotangent
    )
    w_qkv, w_o, gate_up_shard, down_shard = lax.optimization_barrier(
        (w_qkv, w_o, gate_up_shard, down_shard)
    )
    gate_up_w = lax.all_gather(gate_up_shard, "ctx", axis=0, tiled=True)
    down_w = lax.all_gather(down_shard, "ctx", axis=0, tiled=True)
    normed, queries, kv, scales = project(rows_in, gains, shard, cosine, sine, w_qkv)
    inner = (z == 1) | (z == 2)
    across = lax.ppermute(cot_one, "fsdp", [(1, 2), (2, 1)])
    outward = lax.ppermute(cot_three, "fsdp", [(1, 0), (2, 3)])
    store = gather_kv(kv)
    store, across, outward = lax.optimization_barrier((store, across, outward))
    farther = lax.ppermute(across, "fsdp", [(1, 0), (2, 3)])
    prob, attended = attend(place, lowest, queries, store, reach)
    attended, farther = lax.optimization_barrier((attended, farther))
    cots = (
        cotangent,
        cot_one,
        jnp.where(inner, across, outward),
        jnp.where(inner, cot_three, farther),
    )
    middle, own_normed, mate_normed, beyond_normed = out_norm(attended, tokens, scales, w_o)

    ffn_in, hidden, active, sloped = feed_forward(
        own_normed, mate_normed, beyond_normed, gate_up_w
    )
    ffn_cot, grad_gate, grad_up = feed_forward_grad(cots, down_w, active, sloped)

    w_parts, gate_sum, near_parts, far_parts, grad_middle, grad_branch, grad_ffn_scale = feed_forward_back(
        grad_gate, grad_up, gate_up_w, down_w, hidden, ffn_in, middle, ffn_cot, scales
    )
    same_core = [list(range(core, ctx_total, 2)) for core in range(2)]
    ffn_sums = lax.psum_scatter(
        w_parts, "ctx", scatter_dimension=0, axis_index_groups=same_core, tiled=True
    )
    units = w_gate.shape[1]
    if ctx_total != 8:
        gate_sum, ffn_sums = ffn_sums[:, :units], ffn_sums[:, units:]
    grad_gate_w = gate_sum.astype(F32)
    grad_up_w = ffn_sums[:, :units].astype(F32)
    grad_down = ffn_sums[:, units:].astype(F32).T
    grad_out_part = t_dot(grad_branch, attended).astype(BF16)

    grad_q, kv_parts = attend_back(
        place, goes, prob, queries, grad_branch, w_o, cosine, sine, store, reach
    )
    grad_kv, output = first_sums(kv_parts, near_parts, far_parts, middle, shard)
    grad_query_w, grad_key_w, grad_value_w, grad_out_w, grad_tokens, scale_sums = last_sums(
        grad_out_part,
        w_qkv,
        grad_q,
        grad_kv,
        kv_cosine,
        kv_sine,
        normed,
        tokens,
        scales,
        grad_middle,
        grad_ffn_scale,
        shard,
    )
    first_col = (ctx * lax.axis_size("fsdp") + z) * shard
    scale_sums = lax.dynamic_slice_in_dim(scale_sums, first_col, shard, 1)
    return (
        output,
        grad_tokens,
        scale_sums[0],
        grad_query_w,
        grad_key_w,
        grad_value_w,
        grad_out_w.T,
        scale_sums[1],
        grad_gate_w,
        grad_up_w,
        grad_down,
    )


def solution(mesh):
    in_specs = (
        P(("ctx", "fsdp"), None),
        P(),
        P(),
        P(("ctx", "fsdp")),
        P(("ctx", "fsdp"), None),
        P(("ctx", "fsdp"), None),
        P(("ctx", "fsdp"), None),
        P(None, ("ctx", "fsdp")),
        P(("ctx", "fsdp")),
        P("ctx", "fsdp"),
        P("ctx", "fsdp"),
        P("fsdp", "ctx"),
        P(("ctx", "fsdp"), None),
    )
    out_specs = (
        P(("ctx", "fsdp"), None),
        P(("ctx", "fsdp"), None),
        P(("ctx", "fsdp")),
        P(("ctx", "fsdp"), None),
        P(("ctx", "fsdp"), None),
        P(("ctx", "fsdp"), None),
        P(None, ("ctx", "fsdp")),
        P(("ctx", "fsdp")),
        P("ctx", "fsdp"),
        P("ctx", "fsdp"),
        P("fsdp", "ctx"),
    )
    return jax.shard_map(local, mesh=mesh, in_specs=in_specs, out_specs=out_specs, check_vma=False)
```
